32 devices in a mesh: section: 2 (over x), dp: 16 (over z, y, core).
Axes of the slice: x: 2, y: 2, z: 4, core: 2. Of those that a mesh axis runs over, the one named last changes fastest.
Arguments:
- spectra: bfloat16 [2, 16, 4096, 80], P(None, 'dp'), may hold values from -6 to 6
- lengths: int32 [2, 16], P(None, 'dp'), may hold values from 128 to 512, as said below
- languages: int32 [2, 16], P(None, 'dp'), may hold values from 0 to 7
- token_masks: int32 [8, 1024], replicated, may hold values from 0 to 1, as said below
- cotangent: bfloat16 [2, 2, 16, 512, 1024], P('section', None, 'dp'), may hold values from -6 to 6
- feed_in: float32 [2, 2, 512, 2048], P('section', None, 'dp'), may hold values from -0.25 to 0.25
- feed_out: float32 [2, 2, 2048, 512], P('section', None, 'dp'), may hold values from -0.25 to 0.25
- attend_in: float32 [2, 512, 1536], P('section', 'dp'), may hold values from -0.25 to 0.25
- attend_out: float32 [2, 512, 512], P('section', 'dp'), may hold values from -0.75 to 0.75
- conv_in: float32 [2, 512, 1024], P('section', 'dp'), may hold values from -0.25 to 0.25
- conv_depth: float32 [2, 9, 512], P('section', None, 'dp'), may hold values from -2 to 2
- conv_out: float32 [2, 512, 512], P('section', 'dp'), may hold values from -0.375 to 0.375
- norm_gains: float32 [2, 6, 512], P('section', None, 'dp'), may hold values from 0.1 to 1.9
- stem_in: float32 [640, 256], P(None, ('section', 'dp')), may hold values from -0.25 to 0.25
- stem_out: float32 [256, 512], P(('section', 'dp')), may hold values from -0.5 to 0.5
- head_weight: float32 [512, 1024], P(None, ('section', 'dp')), may hold values from -0.5 to 0.5
Outputs:
- activations: float32 [2, 2, 16, 512, 512], P('section', None, 'dp')
- log_probs: float32 [2, 2, 16, 512, 1024], P('section', None, 'dp')
- input_grads: float32 [2, 2, 16, 512, 512], P('section', None, 'dp')
- grad_feed_in: float32 [2, 2, 512, 2048], P('section', None, 'dp')
- grad_feed_out: float32 [2, 2, 2048, 512], P('section', None, 'dp')
- grad_attend_in: float32 [2, 512, 1536], P('section', 'dp')
- grad_attend_out: float32 [2, 512, 512], P('section', 'dp')
- grad_conv_in: float32 [2, 512, 1024], P('section', 'dp')
- grad_conv_depth: float32 [2, 9, 512], P('section', None, 'dp')
- grad_conv_out: float32 [2, 512, 512], P('section', 'dp')
- grad_gains: float32 [2, 6, 512], P('section', None, 'dp')
- grad_stem_in: float32 [640, 256], P(None, ('section', 'dp'))
- grad_stem_out: float32 [256, 512], P(('section', 'dp'))
- grad_head: float32 [512, 1024], P(None, ('section', 'dp'))
The draws below stay inside these ranges and needn't reach their ends.
Inputs may be any that keep to these rules, and one draw needn't show every extreme that they name: `lengths`: every micro-batch holds an utterance of exactly 512 tokens. `token_masks`: token 0 is allowed for every language group.
All inputs are finite; a program needn't handle non-finite values.
Results may differ from the reference program's by a relative error of at most 0.02.
Values may be sent and summed in bfloat16 or wider, within the bound.
No kernel may reach another device: no remote copies, remote signals or barrier semaphores. Data moves between devices by JAX's collectives and lax.ppermute only.
A program may use at most 256 MiB of HBM per device.

```python
import jax
import jax.numpy as jnp
from jax import lax

D = 512
HEADS = 8
HDIM = 64
FF = 2048
KERNEL = 9
VOCAB = 1024
MELS = 80
STEMC = 256
STACK = 8
LANGS = 8
MB = 2
LEN = 512
UTTS = 16
N_SECTION = 2


def draw_lengths(key, part):
    key = jax.random.fold_in(key, 11)
    first_key, second_key = jax.random.split(key)
    drawn = jax.random.randint(first_key, (MB, UTTS), LEN // 4, LEN + 1)
    longest = jax.random.randint(second_key, (MB, 1), 0, UTTS)
    chosen = jnp.arange(UTTS)[None, :] == longest
    return jnp.where(chosen, LEN, drawn).astype(jnp.int32)


def draw_token_masks(key, part):
    key = jax.random.fold_in(key, 23)
    drawn = jax.random.randint(key, (LANGS, VOCAB), 0, 2)
    blank = jnp.arange(VOCAB)[None, :] == 0
    return jnp.where(blank, 1, drawn).astype(jnp.int32)


def plant(array, own_key, least, high):
    longest = array.shape.index(max(array.shape))
    spots = []
    for shift in (0, 1):
        where = [jax.random.randint(jax.random.fold_in(own_key, axis), (), 0, length) for axis, length in enumerate(array.shape)]
        where[longest] = (where[longest] + shift) % array.shape[longest]
        spots.append(tuple(where))
    return array.at[spots[0]].set(least).at[spots[1]].set(high)


def with_spikes(values, key, source, target, blocks, factor):
    def block_of(position):
        return (jnp.arange(values.shape[position]) // (values.shape[position] // blocks)).reshape((-1,) + (1,) * (values.ndim - 1 - position))

    one_side = jax.random.permutation(key, blocks)[block_of(target)]
    far = (block_of(target) + blocks // 2) % blocks
    return jnp.where((block_of(source) == one_side) | (block_of(source) == far), factor * values, values)


def shard_levels(stream_key, shape, cuts, low, largest):
    gain = 1.0
    for dim, parts in cuts:
        steps = jax.random.uniform(jax.random.fold_in(jax.random.fold_in(stream_key, 6), dim), (parts,), jnp.float32, low / len(cuts), largest / len(cuts))
        gain = gain * jnp.repeat(jnp.exp(steps), shape[dim] // parts).reshape((-1,) + (1,) * (len(shape) - 1 - dim))
    return gain


def normal_values(own_key, shape, deviation, bound, cuts=(), dtype=jnp.bfloat16):
    values = jax.random.normal(own_key, shape, jnp.float32) * deviation
    if len(cuts) > 0:
        values = shard_levels(own_key, shape, cuts, -0.22, 0.18) * values
    return jnp.clip(values, min=-bound, max=bound).astype(dtype)


def gaussian_with(stream_key, dims, deviation, limit, shards, heavy, kind=jnp.bfloat16):
    values = deviation * jax.random.normal(stream_key, dims, jnp.float32)
    if shards:
        values = values * shard_levels(stream_key, dims, shards, -0.22, 0.18)
    return jnp.clip(with_spikes(values, jax.random.fold_in(stream_key, 3), *heavy), -limit, limit).astype(kind)


def setup_inputs(seed: int = 0) -> dict:
    arg_keys = jax.random.split(jax.random.key(seed), 17)
    return {
        "spectra": normal_values(arg_keys[0], (MB, UTTS, LEN * STACK, MELS), 1.0, 6.0, ((1, 16),)),
        "lengths": draw_lengths(jax.random.fold_in(arg_keys[16], 71), 0),
        "languages": plant(jax.random.randint(arg_keys[2], (MB, UTTS), 0, LANGS), jax.random.fold_in(arg_keys[2], 1), 0, LANGS - 1).astype(jnp.int32),
        "token_masks": draw_token_masks(jax.random.fold_in(arg_keys[16], 71), 0),
        "cotangent": gaussian_with(arg_keys[4], (N_SECTION, MB, UTTS, LEN, VOCAB), 1.0, 6.0, ((0, 2), (2, 16)), (2, 4, 16, 2.0)),
        "feed_in": normal_values(arg_keys[5], (N_SECTION, 2, D, FF), D ** -0.5, 0.25, ((0, 2), (2, 16)), jnp.float32),
        "feed_out": normal_values(arg_keys[6], (N_SECTION, 2, FF, D), (FF // 4) ** -0.5, 0.25, ((0, 2), (2, 16)), jnp.float32),
        "attend_in": normal_values(arg_keys[7], (N_SECTION, D, 3 * D), D ** -0.5, 0.25, ((0, 2), (1, 16)), jnp.float32),
        "attend_out": normal_values(arg_keys[8], (N_SECTION, D, D), (D // 8) ** -0.5, 0.75, ((0, 2), (1, 16)), jnp.float32),
        "conv_in": normal_values(arg_keys[9], (N_SECTION, D, 2 * D), D ** -0.5, 0.25, ((0, 2), (1, 16)), jnp.float32),
        "conv_depth": normal_values(arg_keys[10], (N_SECTION, KERNEL, D), KERNEL ** -0.5, 2.0, ((0, 2), (2, 16)), jnp.float32),
        "conv_out": normal_values(arg_keys[11], (N_SECTION, D, D), (D // 2) ** -0.5, 0.375, ((0, 2), (1, 16)), jnp.float32),
        "norm_gains": jnp.clip(1.0 + 0.18 * jax.random.normal(arg_keys[12], (N_SECTION, 6, D), jnp.float32), 0.1, 1.9),
        "stem_in": normal_values(arg_keys[13], (STACK * MELS, STEMC), (STACK * MELS) ** -0.5, 0.25, ((1, 32),), jnp.float32),
        "stem_out": normal_values(arg_keys[14], (STEMC, D), (STEMC // 2) ** -0.5, 0.5, ((0, 32),), jnp.float32),
        "head_weight": normal_values(arg_keys[15], (D, VOCAB), (D // 4) ** -0.5, 0.5, ((1, 32),), jnp.float32),
    }


@jax.custom_vjp
def low(v):
    return lax.optimization_barrier(v.astype(jnp.bfloat16)).astype(jnp.float32)

@jax.custom_vjp
def low_back(v):
    return v

def low_keep(v):
    return (low(v), None)

def low_pass(kept, grad):
    return (grad,)

def back_keep(v):
    return (v, None)

def back_low(kept, grad):
    return (low(grad),)
low.defvjp(low_keep, low_pass)
low_back.defvjp(back_keep, back_low)
highest = lax.Precision.HIGHEST
epsilon = 1e-05
masked_score = -1e+30

def matmul(left, right):
    return jnp.dot(left, right, precision=highest)

def layer_norm(values, norm_gain):
    centered = values - lax.optimization_barrier(jnp.mean(values, axis=-1, keepdims=True))
    inv_scale = lax.rsqrt(lax.optimization_barrier(jnp.mean(centered * centered, axis=-1, keepdims=True)) + epsilon)
    return centered * inv_scale * norm_gain

def feed_block(values, norm_gain, w_in, w_out):
    normed = low(layer_norm(values, norm_gain))
    hidden = low_back(matmul(normed, w_in))
    return low_back(matmul(low(jax.nn.silu(hidden)), w_out))

def attend(values, norm_gain, w_in, w_out, valid_mask):
    normed = low(layer_norm(values, norm_gain))
    packed = low(low_back(matmul(normed, w_in))).reshape(LEN, 3, HEADS, HDIM)
    scores = low_back(jnp.einsum('qhd,khd->hqk', packed[:, 0], packed[:, 1], precision=highest)) * HDIM ** (-0.5)
    scores = jnp.where(valid_mask[None, None, :] > 0, scores, masked_score)
    attn_probs = jax.nn.softmax(scores, axis=-1)
    mixed_rows = jnp.einsum('hqk,khd->qhd', low(attn_probs), packed[:, 2], precision=highest).reshape(LEN, D)
    return low_back(matmul(low(low_back(mixed_rows)), w_out))

def convolve(values, gain_in, gain_mid, w_in, depth, w_out, valid_mask):
    normed = low(layer_norm(values, gain_in))
    gated_rows = low_back(matmul(normed, w_in))
    glu_rows = gated_rows[:, :D] * jax.nn.sigmoid(gated_rows[:, D:]) * valid_mask[:, None]
    half_kernel = KERNEL // 2
    padded = jnp.pad(glu_rows, ((half_kernel, half_kernel), (0, 0)))
    deep_rows = depth[0] * padded[0:LEN]
    for offset in range(1, KERNEL):
        deep_rows = deep_rows + depth[offset] * padded[offset:offset + LEN]
    active = low(jax.nn.silu(layer_norm(deep_rows, gain_mid)))
    return low_back(matmul(active, w_out))

def conformer(values, valid_mask, weights):
    feed_in, feed_out, attend_in, attend_out, conv_in, conv_depth, conv_out, norm_gains = weights
    stream = values + 0.5 * feed_block(values, norm_gains[0], feed_in[0], feed_out[0])
    stream = stream + attend(stream, norm_gains[1], attend_in, attend_out, valid_mask)
    stream = stream + convolve(stream, norm_gains[2], norm_gains[3], conv_in, conv_depth, conv_out, valid_mask)
    stream = stream + 0.5 * feed_block(stream, norm_gains[4], feed_in[1], feed_out[1])
    return layer_norm(stream, norm_gains[5]) * valid_mask[:, None]

def ctc_head(sent_rows, head_w, allowed, valid_mask):
    logits = low_back(matmul(sent_rows, head_w))
    permit = allowed[None, :] > 0
    top_logit = lax.optimization_barrier(jnp.max(jnp.where(permit, logits, masked_score), axis=-1, keepdims=True))
    exp_total = lax.optimization_barrier(jnp.sum(jnp.exp(jnp.where(permit, logits - top_logit, masked_score)), axis=-1, keepdims=True))
    logsum = top_logit + jnp.log(exp_total)
    return jnp.where(permit, logits - logsum, 0.0) * valid_mask[:, None]

def network(params, frames, valid_mask, allowed, probes):
    stem_w_in, stem_w_out, head_w, first_layer, second_layer = params
    hidden = low(jax.nn.silu(low_back(matmul(frames, stem_w_in))))
    stem_rows = low(low_back(matmul(hidden, stem_w_out) * valid_mask[:, None])) + probes[0]
    act_one = conformer(stem_rows, valid_mask, first_layer)
    sent_one = low(act_one)
    logp_one = ctc_head(sent_one, head_w, allowed, valid_mask)
    act_two = conformer(low_back(sent_one) + probes[1], valid_mask, second_layer)
    logp_two = ctc_head(low(act_two), head_w, allowed, valid_mask)
    return (act_one, act_two, logp_one, logp_two)

def rounded(weight):
    return lax.optimization_barrier(weight.astype(jnp.bfloat16)).astype(jnp.float32)

def reference(spectra, lengths, languages, token_masks, cotangent, feed_in, feed_out, attend_in, attend_out, conv_in, conv_depth, conv_out, norm_gains, stem_in, stem_out, head_weight):
    stacked = (feed_in, feed_out, attend_in, attend_out, conv_in, conv_depth, conv_out, norm_gains)
    layers = tuple((tuple((rounded(weight[number]) for weight in stacked)) for number in range(N_SECTION)))
    params = (rounded(stem_in), rounded(stem_out), rounded(head_weight), layers[0], layers[1])
    utterances = MB * UTTS
    flat_frames = spectra.reshape(utterances, LEN, STACK * MELS)
    flat_lengths = lengths.reshape(utterances)
    flat_languages = languages.reshape(utterances)
    tangents = jnp.swapaxes(cotangent.reshape(N_SECTION, utterances, LEN, VOCAB), 0, 1)
    masks_float = token_masks.astype(jnp.float32)

    def accumulate(totals, pieces):
        frames, length_value, language, tangent = pieces
        valid_mask = (jnp.arange(LEN) < length_value).astype(jnp.float32)
        allowed = masks_float[language]
        frames_float = frames.astype(jnp.float32)

        def forward(params_in, probes):
            return network(params_in, frames_float, valid_mask, allowed, probes)
        probes = (jnp.zeros((LEN, D), jnp.float32), jnp.zeros((LEN, D), jnp.float32))
        outputs, pullback = jax.vjp(forward, params, probes)
        zero_rows = jnp.zeros((LEN, D), jnp.float32)
        grads, probe_grads = pullback((zero_rows, zero_rows, tangent[0].astype(jnp.float32), tangent[1].astype(jnp.float32)))
        totals = jax.tree.map(jnp.add, totals, grads)
        return (totals, (outputs, probe_grads))
    zeros_tree = jax.tree.map(jnp.zeros_like, params)
    totals, (outputs, probe_grads) = lax.scan(accumulate, zeros_tree, (flat_frames, flat_lengths, flat_languages, tangents))
    activations = jnp.stack([outputs[0], outputs[1]]).reshape(N_SECTION, MB, UTTS, LEN, D)
    log_probs = jnp.stack([outputs[2], outputs[3]]).reshape(N_SECTION, MB, UTTS, LEN, VOCAB)
    input_grads = jnp.stack([probe_grads[0], probe_grads[1]]).reshape(N_SECTION, MB, UTTS, LEN, D)
    layer_grads = tuple((jnp.stack([first_grad, second_grad]) for first_grad, second_grad in zip(totals[3], totals[4])))
    return (activations, log_probs, input_grads, layer_grads[0], layer_grads[1], layer_grads[2], layer_grads[3], layer_grads[4], layer_grads[5], layer_grads[6], layer_grads[7], totals[0], totals[1], totals[2])
```

```python
import types

import jax
import jax.numpy as jnp
from jax import lax
from jax.experimental import pallas as pl
from jax.experimental.pallas import tpu as pltpu
from jax.sharding import PartitionSpec as P

D = 512
HEADS = 8
HDIM = 64
FF = 2048
TAPS = 9
EPS = 1e-05
MASKED = -1e30
RB = 512
BOTH = ("section", "dp")
BF = jnp.bfloat16
F32 = jnp.float32

FEED, ATTN, CONV = 256, 128, 96
FLAT = 32
SMALL = 16


def dotn(a, b):
    return lax.dot_general(a, b, (((1,), (0,)), ((), ())), preferred_element_type=F32)


def dotr(a, b):
    return lax.dot_general(a, b, (((1,), (1,)), ((), ())), preferred_element_type=F32)


def dotl(a, b):
    return lax.dot_general(a, b, (((0,), (0,)), ((), ())), preferred_element_type=F32)


def sigmoid(v):
    return 0.5 * jnp.tanh(0.5 * v) + 0.5


def unit_rows(v):
    c = v - jnp.mean(v, axis=-1, keepdims=True)
    r = lax.rsqrt(jnp.mean(c * c, axis=-1, keepdims=True) + EPS)
    return c * r, r


def unit_back(dn, u, r, gain):
    du = dn * gain
    dv = r * (du - jnp.mean(du, axis=-1, keepdims=True) - u * jnp.mean(du * u, axis=-1, keepdims=True))
    return dv, jnp.sum(dn * u, axis=0, keepdims=True)


def row_mask(length, start, rows, columns):
    return (lax.broadcasted_iota(jnp.int32, (rows, columns), 0) + start < length).astype(F32)


def row_loop(body):
    for i in range(512 // RB):
        body(slice(i * RB, i * RB + RB), i * RB)


def piece_of(ids, cr, a, b, zk):
    pc = ids[3] ^ cr
    px = ids[0] ^ (a + pc * (b - a))
    py = ids[2] ^ (b + pc * (a - b))
    pz = ids[1] ^ zk
    return px, pz * 4 + py * 2 + pc


def pieces():
    return [(cr, a, b, zk) for cr in range(2) for a in range(2) for b in range(2) for zk in range(4)]


def start_load(ids, bufs, row, rows, scr, sem, flat=False):
    for cr, a, b, zk in pieces():
        px, d = piece_of(ids, cr, a, b, zk)
        src = bufs[cr * 4 + a * 2 + b].at[zk, row : row + rows]
        if flat:
            dst = scr.at[px * 16 + d]
        else:
            dst = scr.at[d, pl.ds(pl.multiple_of(px * rows, 16), rows)]
        pltpu.make_async_copy(src, dst, sem).start()


def wait_load(scr, sem):
    pltpu.make_async_copy(scr, scr, sem).wait()


def start_store(ids, scr, keep, send, row, rows, sem, flat=False):
    for cr, a, b, zk in pieces():
        px, d = piece_of(ids, cr, a, b, zk)
        if flat:
            src = scr.at[px * 16 + d]
        else:
            src = scr.at[d, pl.ds(pl.multiple_of(px * rows, 16), rows)]
        dst = (send if cr else keep).at[a * 8 + b * 4 + zk, row : row + rows]
        pltpu.make_async_copy(src, dst, sem).start()


def wait_store(scr, sem):
    pltpu.make_async_copy(scr, scr, sem).wait()


def in_block(w, j):
    return w[:, 32 * j : 32 * j + 32, :].reshape(512, 512)


def out_block(w, j):
    return w[4 * j : 4 * j + 4, 128:256, :].reshape(512, 512)


def feed_fwd(x, w, gain, hid, out):
    def body(rs, start):
        v = x[rs, :].astype(F32)
        u, _ = unit_rows(v)
        n = (u * gain).astype(BF)
        total = jnp.zeros((RB, 512), F32)
        for j in range(4):
            h = dotn(n, in_block(w, j))
            hid[rs, 512 * j : 512 * j + 512] = h.astype(BF)
            total = total + dotn((h * sigmoid(h)).astype(BF), out_block(w, j))
        out[rs, :] = v + 0.5 * total

    row_loop(body)


def feed_bwd(dx, x, hid, w, gain, out, gw, small, row, s):
    def body(rs, start):
        g = dx[rs, :]
        v = x[rs, :].astype(F32)
        u, r = unit_rows(v)
        s.n[rs, :] = (u * gain).astype(BF)
        d = (0.5 * g).astype(BF)
        s.d[rs, :] = d
        dn = jnp.zeros((RB, 512), F32)
        for j in range(4):
            h = hid[rs, 512 * j : 512 * j + 512].astype(F32)
            sg = sigmoid(h)
            s.act[rs, 512 * j : 512 * j + 512] = (h * sg).astype(BF)
            dh = (dotr(d, out_block(w, j)) * (sg * (1.0 + h * (1.0 - sg)))).astype(BF)
            s.dh[rs, 512 * j : 512 * j + 512] = dh
            dn = dn + dotr(dh, in_block(w, j))
        dv, gg = unit_back(dn, u, r, gain)
        out[rs, :] = g + dv
        small[row : row + 1, :] += gg

    row_loop(body)
    for j in range(4):
        cols = slice(512 * j, 512 * j + 512)
        gw[:, 32 * j : 32 * j + 32, :] = dotl(s.n[...], s.dh[:, cols]).astype(BF).reshape(16, 32, 512)
        gw[4 * j : 4 * j + 4, 128:256, :] = dotl(s.act[:, cols], s.d[...]).astype(BF).reshape(4, 128, 512)


def lanes_of(half, axis=1, count=1):
    shape = (count, 128) if axis else (128, count)
    return (lax.broadcasted_iota(jnp.int32, shape, axis) + 64 * half) % 128 - 64


def attn_fwd(x, w, gain, length, qkv, ls, mixt, out):
    def project(rs, start):
        u, _ = unit_rows(x[rs, :])
        n = (u * gain).astype(BF)
        for j in range(3):
            qkv[rs, 512 * j : 512 * j + 512] = dotn(n, in_block(w, j)).astype(BF)

    row_loop(project)

    for hp in range(4):
        at = hp * 128
        k = qkv[:, pl.ds(512 + at, 128)].astype(F32)
        vt = qkv[:, pl.ds(1024 + at, 128)].astype(F32).T
        outside = jnp.where(lax.broadcasted_iota(jnp.int32, (512, 128), 0) < length, 0.0, MASKED)
        kx, vx = [], []
        for hh in range(2):
            free = lanes_of(hh)
            kx.append(jnp.where(free < 0, k, jnp.where(free == 0, outside, 0.0)).astype(BF))
            free = lanes_of(hh, 0, 512)
            vx.append(jnp.where(free < 0, vt, jnp.where(free == 0, 1.0, 0.0)).astype(BF))

        def body(rs, start):
            q = qkv[rs, pl.ds(at, 128)].astype(F32) * HDIM**-0.5
            parts = []
            for hh in range(2):
                free = lanes_of(hh)
                qx = jnp.where(free < 0, q, jnp.where(free == 0, 1.0, 0.0)).astype(BF)
                sc = dotr(kx[hh], qx)
                top = jnp.max(sc, axis=0, keepdims=True)
                both = dotn(vx[hh], jnp.exp(sc - top).astype(BF))
                tot = both[64 * (1 - hh) : 64 * (1 - hh) + 1, :]
                parts.append(both * (1.0 / tot))
                ls[pl.ds(hp * 2 + hh, 1), rs] = top + jnp.log(tot)
            mixt[pl.ds(at, 128), rs] = jnp.where(lanes_of(0, 0, RB) < 0, parts[0], parts[1]).astype(BF)

        row_loop(body)

    def project_out(rs, start):
        out[rs, :] = x[rs, :] + dotl(mixt[:, rs], w[:, 96:128, :].reshape(512, 512))

    row_loop(project_out)


def attn_bwd(dx, x, qkv, ls, mixt, w, gain, length, out, gw, small, row, s):
    def first(rs, start):
        u, _ = unit_rows(x[rs, :])
        s.n[rs, :] = (u * gain).astype(BF)
        d = dx[rs, :].astype(BF)
        s.d[rs, :] = d
        s.dm[:, rs] = dotr(w[:, 96:128, :].reshape(512, 512), d).astype(BF)

    row_loop(first)
    gw[:, 96:128, :] = dotn(mixt[...], s.d[...]).astype(BF).reshape(16, 32, 512)

    for hp in range(4):
        at = hp * 128
        s.dq[...] = jnp.zeros((128, 512), F32)
        q = qkv[:, pl.ds(at, 128)].astype(F32) * HDIM**-0.5
        kt = qkv[:, pl.ds(512 + at, 128)].astype(F32).T * HDIM**-0.5
        dmt = s.dm[pl.ds(at, 128), :].astype(F32)
        prod = dmt * mixt[pl.ds(at, 128), :].astype(F32)
        qx, qs, dms, deltas, sums = [], [], [], [], []
        for hh in range(2):
            free = lanes_of(hh)
            qs.append(jnp.where(free < 0, q, 0.0).astype(BF))
            qx.append(jnp.where(free < 0, q, jnp.where(free == 0, 1.0, 0.0)).astype(BF))
            free = lanes_of(hh, 0, 512)
            dms.append(jnp.where(free < 0, dmt, 0.0).astype(BF))
            deltas.append(jnp.sum(prod[64 * hh : 64 * hh + 64, :], axis=0, keepdims=True))
            s.kt[128 * hh : 128 * hh + 128, :] = jnp.where(free < 0, kt, 0.0).astype(BF)
            sums.append(ls[pl.ds(hp * 2 + hh, 1), :])

        def body(rs, start):
            k = qkv[rs, pl.ds(512 + at, 128)].astype(F32)
            v = qkv[rs, pl.ds(1024 + at, 128)]
            outside = jnp.where(lax.broadcasted_iota(jnp.int32, (RB, 128), 0) + start < length, 0.0, MASKED)
            dk = jnp.zeros((RB, 128), F32)
            dv = jnp.zeros((RB, 128), F32)
            for hh in range(2):
                free = lanes_of(hh)
                kx = jnp.where(free < 0, k, jnp.where(free == 0, outside, 0.0)).astype(BF)
                p = jnp.exp(dotr(kx, qx[hh]) - sums[hh])
                ds = (p * (dotn(v, dms[hh]) - deltas[hh])).astype(BF)
                dv = dv + dotr(p.astype(BF), dms[hh])
                dk = dk + dotn(ds, qs[hh])
                s.dq[...] += dotn(s.kt[128 * hh : 128 * hh + 128, rs], ds)
            s.dpk[rs, pl.ds(512 + at, 128)] = dk.astype(BF)
            s.dpk[rs, pl.ds(1024 + at, 128)] = dv.astype(BF)

        row_loop(body)
        s.dpk[:, pl.ds(at, 128)] = s.dq[...].T.astype(BF)

    def last(rs, start):
        u, r = unit_rows(x[rs, :])
        dn = jnp.zeros((RB, 512), F32)
        for j in range(3):
            dn = dn + dotr(s.dpk[rs, 512 * j : 512 * j + 512], in_block(w, j))
        dv, gg = unit_back(dn, u, r, gain)
        out[rs, :] = dx[rs, :] + dv
        small[row : row + 1, :] += gg

    row_loop(last)
    for j in range(3):
        gw[:, 32 * j : 32 * j + 32, :] = (
            dotl(s.n[...], s.dpk[:, 512 * j : 512 * j + 512]).astype(BF).reshape(16, 32, 512)
        )


PAD = 8


def conv_fwd(x, w, prm, length, gated, deep, out, pad):
    pad[0:PAD, :] = jnp.zeros((PAD, 512), F32)
    pad[PAD + 512 : 2 * PAD + 512, :] = jnp.zeros((PAD, 512), F32)

    def first(rs, start):
        u, _ = unit_rows(x[rs, :])
        n = (u * prm[TAPS + 2 : TAPS + 3, :]).astype(BF)
        a = dotn(n, in_block(w, 0))
        b = dotn(n, in_block(w, 1))
        gated[rs, 0:512] = a
        gated[rs, 512:1024] = b
        pad[pl.ds(start + PAD, RB), :] = a * sigmoid(b) * row_mask(length, start, RB, 512)

    row_loop(first)
    for i in range(512 // RB):
        total = jnp.zeros((RB, 512), F32)
        for t in range(TAPS):
            begin = i * RB + PAD - TAPS // 2 + t
            total = total + prm[t : t + 1, :] * pad[begin : begin + RB, :]
        deep[i * RB : i * RB + RB, :] = total

    def last(rs, start):
        u, _ = unit_rows(deep[rs, :])
        m = u * prm[TAPS + 3 : TAPS + 4, :]
        act = (m * sigmoid(m)).astype(BF)
        out[rs, :] = x[rs, :] + dotn(act, w[:, 64:96, :].reshape(512, 512))

    row_loop(last)


def conv_bwd(dx, x, gated, deep, w, prm, length, out, gw, small, s):
    for pad in (s.pad, s.back):
        pad[0:PAD, :] = jnp.zeros((PAD, 512), F32)
        pad[PAD + 512 : 2 * PAD + 512, :] = jnp.zeros((PAD, 512), F32)
    gain_in = prm[TAPS + 2 : TAPS + 3, :]
    gain_mid = prm[TAPS + 3 : TAPS + 4, :]

    def first(rs, start):
        padded = pl.ds(start + PAD, RB)
        d = dx[rs, :].astype(BF)
        s.d[rs, :] = d
        u3, r3 = unit_rows(deep[rs, :])
        m = u3 * gain_mid
        sg = sigmoid(m)
        s.act[rs, :] = (m * sg).astype(BF)
        dmid = dotr(d, w[:, 64:96, :].reshape(512, 512)) * (sg * (1.0 + m * (1.0 - sg)))
        ddeep, gg = unit_back(dmid, u3, r3, gain_mid)
        s.back[padded, :] = ddeep
        small[TAPS + 3 : TAPS + 4, :] += gg
        s.pad[padded, :] = (
            gated[rs, 0:512] * sigmoid(gated[rs, 512:1024]) * row_mask(length, start, RB, 512)
        )

    row_loop(first)
    gw[:, 64:96, :] = dotl(s.act[...], s.d[...]).astype(BF).reshape(16, 32, 512)
    for i in range(512 // RB):
        rows = slice(i * RB, i * RB + RB)
        ddeep = s.back[PAD + i * RB : PAD + i * RB + RB, :]
        dglu = jnp.zeros((RB, 512), F32)
        for t in range(TAPS):
            begin = i * RB + PAD - TAPS // 2 + t
            small[t : t + 1, :] += jnp.sum(ddeep * s.pad[begin : begin + RB, :], axis=0, keepdims=True)
            begin = i * RB + PAD + TAPS // 2 - t
            dglu = dglu + prm[t : t + 1, :] * s.back[begin : begin + RB, :]
        dglu = dglu * row_mask(length, i * RB, RB, 512)
        sg = sigmoid(gated[rows, 512:1024])
        ga = dglu * sg
        s.dga[rows, :] = ga.astype(BF)
        s.dgb[rows, :] = (ga * gated[rows, 0:512] * (1.0 - sg)).astype(BF)

    def last(rs, start):
        u, r = unit_rows(x[rs, :])
        s.n[rs, :] = (u * gain_in).astype(BF)
        dn = dotr(s.dga[rs, :], in_block(w, 0)) + dotr(s.dgb[rs, :], in_block(w, 1))
        dv, gg = unit_back(dn, u, r, gain_in)
        out[rs, :] = dx[rs, :] + dv
        small[TAPS + 2 : TAPS + 3, :] += gg

    row_loop(last)
    gw[:, 0:32, :] = dotl(s.n[...], s.dga[...]).astype(BF).reshape(16, 32, 512)
    gw[:, 32:64, :] = dotl(s.n[...], s.dgb[...]).astype(BF).reshape(16, 32, 512)


def finish_fwd(x4, prm, length, sent):
    def body(rs, start):
        u, _ = unit_rows(x4[rs, :])
        sent[rs, :] = (u * prm[TAPS + 5 : TAPS + 6, :] * row_mask(length, start, RB, 512)).astype(BF)

    row_loop(body)


def head_rows(sent, w, permit):
    logits = dotr(sent, w)
    top = jnp.max(jnp.where(permit, logits, MASKED), axis=-1, keepdims=True)
    e = jnp.exp(jnp.where(permit, logits - top, MASKED))
    return logits, top + jnp.log(jnp.sum(e, axis=-1, keepdims=True))


def head_bwd(x4, sent, w, allowed, cot, prm, length, extra, out, gl, gsent, small):
    permit = allowed[...] > 0
    gain = prm[TAPS + 5 : TAPS + 6, :]

    def body(rs, start):
        hw = w[...].reshape(1024, 512)
        logits, logsum = head_rows(sent[rs, :], hw, permit)
        weighted = jnp.where(permit, cot[rs, :].astype(F32), 0.0) * row_mask(length, start, RB, 1024)
        probs = jnp.exp(jnp.where(permit, logits - logsum, MASKED))
        g = (weighted - probs * jnp.sum(weighted, axis=-1, keepdims=True)).astype(BF)
        gl[rs, :] = g
        gs = dotn(g, hw)
        if extra is not None:
            gs = gs + extra[rs, :].astype(F32)
        u, r = unit_rows(x4[rs, :])
        dv, gg = unit_back(gs * row_mask(length, start, RB, 512), u, r, gain)
        out[rs, :] = dv
        small[TAPS + 5 : TAPS + 6, :] += gg

    row_loop(body)


ANY, VMEM, SMEM = pl.ANY, pltpu.VMEM, pltpu.SMEM


def run(body, micros, ins, outs, scratch):
    flat = []
    for value, space in ins.values():
        flat += [(array, space) for array in (value if isinstance(value, list) else [value])]

    def kernel(*refs):
        left = list(refs)
        ns = types.SimpleNamespace()
        for key, (value, _) in ins.items():
            if isinstance(value, list):
                setattr(ns, key, [left.pop(0) for _ in value])
            else:
                setattr(ns, key, left.pop(0))
        for key in [*outs, *scratch]:
            setattr(ns, key, left.pop(0))
        ns.sems = left.pop(0)
        body(ns)

    result = pl.pallas_call(
        kernel,
        out_shape=[jax.ShapeDtypeStruct(shape, dtype) for shape, dtype, _ in outs.values()],
        in_specs=[pl.BlockSpec(memory_space=space) for _, space in flat],
        out_specs=[pl.BlockSpec(memory_space=space) for _, _, space in outs.values()],
        scratch_shapes=[pltpu.VMEM(shape, dtype) for shape, dtype in scratch.values()] + [pltpu.SemaphoreType.DMA((8,))],
        compiler_params=pltpu.CompilerParams(vmem_limit_bytes=58 * 2**20),
        cost_estimate=pl.CostEstimate(flops=int(micros * 1.1e9), bytes_accessed=2**20, transcendentals=0),
        name=body.__name__,
    )(*[array for array, _ in flat])
    return types.SimpleNamespace(**dict(zip(outs, result)))


ROWS = (512, 512)


def kernel_stem_feed(ids, bufs, frames):
    def stem_feed(k):
        start_load(k.ids, k.bufs, 0, FLAT, k.stem, k.sems.at[0], flat=True)
        start_load(k.ids, k.bufs, FLAT, FEED // 2, k.w, k.sems.at[1])
        wait_load(k.stem, k.sems.at[0])
        stem = k.stem[...].astype(F32)
        for layer in range(2):
            for z in range(4):
                part = jnp.zeros((8, 512), F32)
                for q in range(4):
                    part = part + stem[layer * 16 + z * 4 + q, 24:32, :]
                k.prm[layer, 0:8, 128 * z : 128 * z + 128] = part[:, 0:128]
                k.prm[layer, 8:16, 128 * z : 128 * z + 128] = part[:, 128:256]
        k.win_a[...] = stem[:, 0:8, :].reshape(256, 512).astype(BF)
        k.win_b[...] = stem[:, 8:16, 0:128].reshape(256, 128).astype(BF)
        k.wout[...] = stem[:, 16:24, :].reshape(256, 512).astype(BF)

        def rows(rs, start):
            pre = dotr(k.frames[rs, 0:512], k.win_a[...]) + dotr(k.frames[rs, 512:640], k.win_b[...])
            k.pre[rs, :] = pre
            x = dotn((pre * sigmoid(pre)).astype(BF), k.wout[...])
            k.x0[rs, :] = (x * row_mask(k.ids[4], start, RB, 512)).astype(BF)

        row_loop(rows)
        wait_load(k.w, k.sems.at[1])
        feed_fwd(k.x0, k.w, k.prm[0, TAPS : TAPS + 1, :], k.hid, k.x1)

    return run(
        stem_feed,
        9,
        dict(ids=(ids, SMEM), bufs=(bufs, ANY), frames=(frames, VMEM)),
        dict(
            prm=((2, SMALL, 512), F32, VMEM),
            pre=((512, 256), F32, VMEM),
            win_a=((256, 512), BF, VMEM),
            win_b=((256, 128), BF, VMEM),
            wout=((256, 512), BF, VMEM),
            x0=(ROWS, BF, VMEM),
            hid=((512, FF), BF, VMEM),
            x1=(ROWS, F32, VMEM),
        ),
        dict(stem=((32, FLAT, 512), BF), w=((16, FEED, 512), BF)),
    )


ATTN_OUTS = dict(
    qkv=((512, 1536), BF, VMEM),
    ls=((8, 512), F32, VMEM),
    mixed=(ROWS, BF, VMEM),
    x2=(ROWS, F32, VMEM),
)
CONV_OUTS = dict(
    gated=((512, 1024), F32, VMEM),
    deep=(ROWS, F32, VMEM),
    x3=(ROWS, F32, VMEM),
)


def kernel_rest_first(ids, bufs, prm, x1):
    def rest_first(k):
        start_load(k.ids, k.bufs, 0, ATTN // 2, k.wa, k.sems.at[0])
        start_load(k.ids, k.bufs, ATTN // 2, CONV // 2, k.wc, k.sems.at[1])
        start_load(k.ids, k.bufs, ATTN // 2 + CONV // 2, FEED // 2, k.wf, k.sems.at[2])
        prm = k.prm.at[0]
        wait_load(k.wa, k.sems.at[0])
        attn_fwd(k.x1, k.wa, prm[TAPS + 1 : TAPS + 2, :], k.ids[4], k.qkv, k.ls, k.mixed, k.x2)
        wait_load(k.wc, k.sems.at[1])
        conv_fwd(k.x2, k.wc, prm, k.ids[4], k.gated, k.deep, k.x3, k.pad)
        wait_load(k.wf, k.sems.at[2])
        feed_fwd(k.x3, k.wf, prm[TAPS + 4 : TAPS + 5, :], k.hid, k.x4)
        finish_fwd(k.x4, prm, k.ids[4], k.sent)

    return run(
        rest_first,
        24,
        dict(ids=(ids, SMEM), bufs=(bufs, ANY), prm=(prm, VMEM), x1=(x1, VMEM)),
        ATTN_OUTS
        | CONV_OUTS
        | dict(hid=((512, FF), BF, VMEM), x4=(ROWS, F32, VMEM), sent=(ROWS, BF, VMEM)),
        dict(
            wa=((16, ATTN, 512), BF),
            wc=((16, CONV, 512), BF),
            wf=((16, FEED, 512), BF),
            pad=((512 + 2 * PAD, 512), F32),
        ),
    )


def kernel_first_second(ids, bufs, prm, x0):
    def first_second(k):
        start_load(k.ids, k.bufs, 0, FEED // 2, k.wf, k.sems.at[2])
        start_load(k.ids, k.bufs, FEED // 2, ATTN // 2, k.wa, k.sems.at[0])
        start_load(k.ids, k.bufs, FEED // 2 + ATTN // 2, CONV // 2, k.wc, k.sems.at[1])
        prm = k.prm.at[1]
        wait_load(k.wf, k.sems.at[2])
        feed_fwd(k.x0, k.wf, prm[TAPS : TAPS + 1, :], k.hid, k.x1)
        wait_load(k.wa, k.sems.at[0])
        attn_fwd(k.x1, k.wa, prm[TAPS + 1 : TAPS + 2, :], k.ids[4], k.qkv, k.ls, k.mixed, k.x2)
        wait_load(k.wc, k.sems.at[1])
        conv_fwd(k.x2, k.wc, prm, k.ids[4], k.gated, k.deep, k.x3, k.pad)

    return run(
        first_second,
        24,
        dict(ids=(ids, SMEM), bufs=(bufs, ANY), prm=(prm, VMEM), x0=(x0, VMEM)),
        dict(hid=((512, FF), BF, VMEM), x1=(ROWS, F32, VMEM)) | ATTN_OUTS | CONV_OUTS,
        dict(
            wa=((16, ATTN, 512), BF),
            wc=((16, CONV, 512), BF),
            wf=((16, FEED, 512), BF),
            pad=((512 + 2 * PAD, 512), F32),
        ),
    )


def kernel_turn(ids, feed_bufs, conv_bufs, prm, x3, cot, allowed, x2, gated, deep):
    def turn(k):
        start_load(k.ids, k.fbufs, 0, FEED // 2, k.wf, k.sems.at[0])
        start_load(k.ids, k.fbufs, FEED // 2, FLAT, k.wh, k.sems.at[1], flat=True)
        start_load(k.ids, k.cbufs, FEED // 2 + ATTN // 2, CONV // 2, k.wc, k.sems.at[2])
        prm = k.prm.at[1]
        k.small[...] = jnp.zeros((SMALL, 512), F32)
        wait_load(k.wf, k.sems.at[0])
        feed_fwd(k.x3, k.wf, prm[TAPS + 4 : TAPS + 5, :], k.hid, k.x4)
        finish_fwd(k.x4, prm, k.ids[4], k.sent)
        wait_load(k.wh, k.sems.at[1])
        head_bwd(k.x4, k.sent, k.wh, k.allowed, k.cot, prm, k.ids[4], None, k.dx4, k.gl, None, k.small)
        k.ghead[...] = dotl(k.gl[...], k.sent[...])
        feed_bwd(
            k.dx4,
            k.x3,
            k.hid,
            k.wf,
            prm[TAPS + 4 : TAPS + 5, :],
            k.dx3,
            k.gf,
            k.small,
            TAPS + 4,
            k,
        )
        start_store(k.ids, k.gf, k.keep, k.send, 0, FEED // 2, k.sems.at[3])
        wait_load(k.wc, k.sems.at[2])
        s = types.SimpleNamespace(
            n=k.n, d=k.d, act=k.act.at[:, 0:512], dga=k.dh.at[:, 0:512], dgb=k.dh.at[:, 512:1024], pad=k.pad, back=k.back
        )
        conv_bwd(k.dx3, k.x2, k.gated, k.deep, k.wc, prm, k.ids[4], k.dx2, k.gc, k.small, s)
        start_store(k.ids, k.gc, k.keep, k.send, FEED // 2, CONV // 2, k.sems.at[4])
        wait_store(k.gf, k.sems.at[3])
        wait_store(k.gc, k.sems.at[4])

    rows = FEED // 2 + CONV // 2
    return run(
        turn,
        32,
        dict(
            ids=(ids, SMEM),
            fbufs=(feed_bufs, ANY),
            cbufs=(conv_bufs, ANY),
            prm=(prm, VMEM),
            x3=(x3, VMEM),
            cot=(cot, VMEM),
            allowed=(allowed, VMEM),
            x2=(x2, VMEM),
            gated=(gated, VMEM),
            deep=(deep, VMEM),
        ),
        dict(
            sent=(ROWS, BF, VMEM),
            ghead=((1024, 512), F32, VMEM),
            dx2=(ROWS, F32, VMEM),
            small=((SMALL, 512), F32, VMEM),
            keep=((16, rows, 512), BF, ANY),
            send=((16, rows, 512), BF, ANY),
        ),
        dict(
            wf=((16, FEED, 512), BF),
            wh=((32, FLAT, 512), BF),
            wc=((16, CONV, 512), BF),
            gf=((16, FEED, 512), BF),
            gc=((16, CONV, 512), BF),
            hid=((512, FF), BF),
            x4=(ROWS, F32),
            gl=((512, 1024), BF),
            dx4=(ROWS, F32),
            dx3=(ROWS, F32),
            n=(ROWS, BF),
            d=(ROWS, BF),
            act=((512, FF), BF),
            dh=((512, FF), BF),
            pad=((512 + 2 * PAD, 512), F32),
            back=((512 + 2 * PAD, 512), F32),
        ),
    )


def kernel_back_late(ids, feed_bufs, conv_bufs, head_bufs, prm, x4, sent, cot, allowed, ig, x3, hid, x2, gated, deep, ghead):
    def back_late(k):
        start_load(k.ids, k.hbufs, FEED // 2, FLAT, k.wh, k.sems.at[1], flat=True)
        start_load(k.ids, k.fbufs, ATTN // 2 + CONV // 2, FEED // 2, k.wf, k.sems.at[0])
        start_load(k.ids, k.cbufs, ATTN // 2, CONV // 2, k.wc, k.sems.at[2])
        prm = k.prm.at[0]
        k.small[...] = jnp.zeros((SMALL, 512), F32)
        wait_load(k.wh, k.sems.at[1])
        head_bwd(k.x4, k.sent, k.wh, k.allowed, k.cot, prm, k.ids[4], k.ig, k.dx4, k.gl, None, k.small)
        k.gh[...] = (k.ghead[...] + dotl(k.gl[...], k.sent[...])).astype(BF).reshape(32, FLAT, 512)
        start_store(k.ids, k.gh, k.keep, k.send, FEED // 2 + CONV // 2, FLAT, k.sems.at[5], flat=True)
        wait_load(k.wf, k.sems.at[0])
        feed_bwd(
            k.dx4,
            k.x3,
            k.hid,
            k.wf,
            prm[TAPS + 4 : TAPS + 5, :],
            k.dx3,
            k.gf,
            k.small,
            TAPS + 4,
            k,
        )
        start_store(k.ids, k.gf, k.keep, k.send, 0, FEED // 2, k.sems.at[3])
        wait_load(k.wc, k.sems.at[2])
        s = types.SimpleNamespace(
            n=k.n, d=k.d, act=k.act.at[:, 0:512], dga=k.dh.at[:, 0:512], dgb=k.dh.at[:, 512:1024], pad=k.pad, back=k.back
        )
        conv_bwd(k.dx3, k.x2, k.gated, k.deep, k.wc, prm, k.ids[4], k.dx2, k.gc, k.small, s)
        start_store(k.ids, k.gc, k.keep, k.send, FEED // 2, CONV // 2, k.sems.at[4])
        wait_store(k.gh, k.sems.at[5])
        wait_store(k.gf, k.sems.at[3])
        wait_store(k.gc, k.sems.at[4])

    rows = FEED // 2 + CONV // 2 + FLAT
    return run(
        back_late,
        28,
        dict(
            ids=(ids, SMEM),
            fbufs=(feed_bufs, ANY),
            cbufs=(conv_bufs, ANY),
            hbufs=(head_bufs, ANY),
            prm=(prm, VMEM),
            x4=(x4, VMEM),
            sent=(sent, VMEM),
            cot=(cot, VMEM),
            allowed=(allowed, VMEM),
            ig=(ig, VMEM),
            x3=(x3, VMEM),
            hid=(hid, VMEM),
            x2=(x2, VMEM),
            gated=(gated, VMEM),
            deep=(deep, VMEM),
            ghead=(ghead, VMEM),
        ),
        dict(
            dx2=(ROWS, F32, VMEM),
            small=((SMALL, 512), F32, VMEM),
            keep=((16, rows, 512), BF, ANY),
            send=((16, rows, 512), BF, ANY),
        ),
        dict(
            wf=((16, FEED, 512), BF),
            wh=((32, FLAT, 512), BF),
            wc=((16, CONV, 512), BF),
            gf=((16, FEED, 512), BF),
            gc=((16, CONV, 512), BF),
            gh=((32, FLAT, 512), BF),
            gl=((512, 1024), BF),
            dx4=(ROWS, F32),
            dx3=(ROWS, F32),
            n=(ROWS, BF),
            d=(ROWS, BF),
            act=((512, FF), BF),
            dh=((512, FF), BF),
            pad=((512 + 2 * PAD, 512), F32),
            back=((512 + 2 * PAD, 512), F32),
        ),
    )


def kernel_back_early(layer, ids, attn_bufs, attn_row, feed_bufs, feed_row, prm, dx2, x1, qkv, ls, mixed, x0, hid, stem):
    def back_early_stem(k):
        start_load(k.ids, k.abufs, attn_row, ATTN // 2, k.wa, k.sems.at[0])
        start_load(k.ids, k.fbufs, feed_row, FEED // 2, k.wf, k.sems.at[1])
        prm = k.prm.at[layer]
        k.small[...] = jnp.zeros((SMALL, 512), F32)
        wait_load(k.wa, k.sems.at[0])
        s = types.SimpleNamespace(n=k.n, d=k.d, dm=k.dm, dpk=k.act.at[:, 0:1536], dq=k.dq, kt=k.kt)
        attn_bwd(
            k.dx2, k.x1, k.qkv, k.ls, k.mixed, k.wa, prm[TAPS + 1 : TAPS + 2, :], k.ids[4], k.dx1, k.ga, k.small, TAPS + 1, s
        )
        start_store(k.ids, k.ga, k.keep, k.send, 0, ATTN // 2, k.sems.at[2])
        wait_load(k.wf, k.sems.at[1])
        feed_bwd(
            k.dx1,
            k.x0,
            k.hid,
            k.wf,
            prm[TAPS : TAPS + 1, :],
            k.ig,
            k.gf,
            k.small,
            TAPS,
            k,
        )
        start_store(k.ids, k.gf, k.keep, k.send, ATTN // 2, FEED // 2, k.sems.at[3])
        if stem is not None:

            def rows(rs, start):
                d = (k.ig[rs, :] * row_mask(k.ids[4], start, RB, 512)).astype(BF)
                k.d[rs, :] = d
                pre = k.pre[rs, :]
                sg = sigmoid(pre)
                k.n[rs, 0:256] = (pre * sg).astype(BF)
                k.n[rs, 256:512] = (dotr(d, k.wout[...]) * (sg * (1.0 + pre * (1.0 - sg)))).astype(BF)

            row_loop(rows)
            k.gs[:, 0:8, :] = dotl(k.n[:, 256:512], k.frames[:, 0:512]).reshape(32, 8, 512)
            k.gs[:, 8:16, 0:128] = dotl(k.n[:, 256:512], k.frames[:, 512:640]).reshape(32, 8, 128)
            k.gs[:, 8:16, 128:512] = jnp.zeros((32, 8, 384), F32)
            k.gs[:, 16:24, :] = dotl(k.n[:, 0:256], k.d[...]).reshape(32, 8, 512)
            first = k.small[...] + k.small_first[...]
            for number, total in enumerate((first, k.small_second[...])):
                for z in range(4):
                    lanes = slice(128 * z, 128 * z + 128)
                    block = jnp.concatenate([total[0:8, lanes], total[8:16, lanes], jnp.zeros((8, 256), F32)], axis=1)
                    for q in range(4):
                        k.gs[number * 16 + z * 4 + q, 24:32, :] = block
            k.gsb[...] = k.gs[...].astype(BF)
            start_store(k.ids, k.gsb, k.keep, k.send, ATTN // 2 + FEED // 2, FLAT, k.sems.at[4], flat=True)
            wait_store(k.gsb, k.sems.at[4])
        wait_store(k.ga, k.sems.at[2])
        wait_store(k.gf, k.sems.at[3])

    rows = ATTN // 2 + FEED // 2 + (0 if stem is None else FLAT)
    ins = dict(
        ids=(ids, SMEM),
        abufs=(attn_bufs, ANY),
        fbufs=(feed_bufs, ANY),
        prm=(prm, VMEM),
        dx2=(dx2, VMEM),
        x1=(x1, VMEM),
        qkv=(qkv, VMEM),
        ls=(ls, VMEM),
        mixed=(mixed, VMEM),
        x0=(x0, VMEM),
        hid=(hid, VMEM),
    )
    scratch = dict(
        wf=((16, FEED, 512), BF),
        wa=((16, ATTN, 512), BF),
        gf=((16, FEED, 512), BF),
        ga=((16, ATTN, 512), BF),
        dx1=(ROWS, F32),
        n=(ROWS, BF),
        d=(ROWS, BF),
        dm=(ROWS, BF),
        act=((512, FF), BF),
        dh=((512, FF), BF),
        dq=((128, 512), F32),
        kt=((256, 512), BF),
    )
    if stem is not None:
        ins |= {key: (value, VMEM) for key, value in stem.items()}
        scratch |= dict(gs=((32, FLAT, 512), F32), gsb=((32, FLAT, 512), BF))
    return run(
        back_early_stem,
        31,
        ins,
        dict(
            ig=(ROWS, F32, VMEM),
            small=((SMALL, 512), F32, VMEM),
            keep=((16, rows, 512), BF, ANY),
            send=((16, rows, 512), BF, ANY),
        ),
        scratch,
    )


def kernel_outputs(ids, head_bufs, own, other, allowed, lengths):
    def outputs(k):
        start_load(k.ids, k.hbufs, FEED // 2, FLAT, k.wh, k.sems.at[0], flat=True)
        wait_load(k.wh, k.sems.at[0])

        @pl.loop(0, 2)
        def _(batch):
            length = k.lengths[batch]
            permit = k.allowed[pl.ds(batch, 1), :] > 0

            def rows(rs, start):
                mine = (batch == k.ids[0]).astype(F32)
                sent = (k.own[rs, :].astype(F32) * mine + k.other[rs, :].astype(F32) * (1.0 - mine)).astype(BF)
                logits, logsum = head_rows(sent, k.wh[...].reshape(1024, 512), permit)
                ok = row_mask(length, start, RB, 1024)
                k.logp[batch, rs, :] = jnp.where(permit, logits - logsum, 0.0) * ok
                k.acts[batch, rs, :] = sent.astype(F32)

            row_loop(rows)

    return run(
        outputs,
        9,
        dict(
            ids=(ids, SMEM),
            lengths=(lengths, SMEM),
            hbufs=(head_bufs, ANY),
            own=(own, VMEM),
            other=(other, VMEM),
            allowed=(allowed, VMEM),
        ),
        dict(logp=((2, 512, 1024), F32, VMEM), acts=((2, 512, 512), F32, VMEM)),
        dict(wh=((32, FLAT, 512), BF)),
    )


def pack_feed(w_in, w_out):
    return jnp.concatenate([w_in.reshape(32, 4, 512).transpose(1, 0, 2).reshape(128, 512), w_out])


def pack_attn(w_in, w_out):
    return jnp.concatenate([w_in.reshape(32, 3, 512).transpose(1, 0, 2).reshape(96, 512), w_out])


def pack_conv(w_in, w_out):
    return jnp.concatenate([w_in.reshape(32, 2, 512).transpose(1, 0, 2).reshape(64, 512), w_out])


def unpack_in(rows, blocks):
    return rows[: 32 * blocks].reshape(blocks, 32, 512).transpose(1, 0, 2).reshape(32, 512 * blocks)


def pack_stem(stem_in, stem_out, depth, gains, quarter):
    turned = stem_in.T
    small = jnp.concatenate([depth, gains, jnp.zeros((1, 32), depth.dtype)])
    spread = lax.dynamic_update_slice(jnp.zeros((16, 128), depth.dtype), small, (0, 32 * quarter))
    return jnp.concatenate(
        [
            turned[:, :512],
            jnp.pad(turned[:, 512:], ((0, 0), (0, 384))),
            stem_out,
            jnp.concatenate([spread[:8], spread[8:], jnp.zeros((8, 256), depth.dtype)], axis=1),
        ]
    )


def unpack_stem(rows, quarter):
    turned = jnp.concatenate([rows[0:8], rows[8:16, :128]], axis=1)
    spread = jnp.concatenate([rows[24:32, 0:128], rows[24:32, 128:256]])
    small = lax.dynamic_slice(spread, (0, 32 * quarter), (16, 32))
    return turned.T, rows[16:24], small[:TAPS], small[TAPS : TAPS + 6]


def permutation(target):
    pairs = []
    for x in range(2):
        for d in range(16):
            tx, tz, ty, tc = target(x, d // 4, (d // 2) % 2, d % 2)
            pairs.append((x * 16 + d, tx * 16 + tz * 4 + ty * 2 + tc))
    return pairs


def across(value, target):
    return lax.ppermute(value, BOTH, permutation(target))


def over_x(value):
    return across(value, lambda x, z, y, c: (1 - x, z, y, c))


def over_core(value):
    return across(value, lambda x, z, y, c: (x, z, y, 1 - c))


def over_z(value, k):
    return across(value, lambda x, z, y, c: (x, z ^ k, y, c))


def over_a(value):
    return across(value, lambda x, z, y, c: (1 - x, z, y, c) if c == 0 else (x, z, 1 - y, c))


def over_b(value):
    return across(value, lambda x, z, y, c: (1 - x, z, y, c) if c == 1 else (x, z, 1 - y, c))


def fence(*values):
    return lax.optimization_barrier(values)


def z_parts(own):
    return [own] + [over_z(own, k) for k in (1, 2, 3)]


def ab_parts(quad):
    return over_a(quad), over_b(quad)


def core_parts(quad, ra, rb, rab):
    return [quad, rb, ra, rab] + [over_core(v) for v in (quad, rb, ra, rab)]


def add(*values):
    total = values[0].astype(F32)
    for value in values[1:]:
        total = total + value.astype(F32)
    return total


def halves(kept, came):
    cut = kept.shape[0] // 2
    return add(kept[:cut], came[:cut]).astype(BF), add(kept[cut:], came[cut:]).astype(BF)


def quarters(kept, came):
    return [add(kept[k], came[k]).astype(BF) for k in range(4)]


def z_sum(parts):
    return add(parts[0], *[over_z(parts[k], k) for k in (1, 2, 3)])


def pick(first, own, other):
    return jnp.where(first, own, other), jnp.where(first, other, own)


def on_device(fast, *args):
    (spectra, lengths, languages, token_masks, cotangent) = args[:5]
    masters = args[5:]
    sec = lax.axis_index("section")
    dp = lax.axis_index("dp")
    first = sec == 0
    low = [m.astype(BF) for m in masters]
    if fast:
        ids = jnp.stack([sec, dp // 4, (dp // 2) % 2, dp % 2, lengths[sec, 0]]).astype(jnp.int32)
        own = own_pieces(low, sec, dp, first)
    else:
        ids = jnp.stack([sec * 0, sec * 0, sec * 0, sec * 0, lengths[sec, 0]]).astype(jnp.int32)
        chunks = gather_plain(low)
    frames = lax.dynamic_index_in_dim(spectra, sec, 0, keepdims=False).reshape(512, -1)
    allowed_both = jnp.concatenate(
        [lax.dynamic_slice_in_dim(token_masks, languages[m, 0], 1, 0) for m in range(2)]
    ).astype(F32)
    allowed = lax.dynamic_slice_in_dim(allowed_both, sec, 1, 0)
    swap = lambda v: lax.ppermute(v, "section", [(0, 1), (1, 0)])
    cots = cotangent[0, :, 0]
    cot_own = lax.dynamic_index_in_dim(cots, sec, 0, keepdims=False)
    cot_other = swap(lax.dynamic_index_in_dim(cots, 1 - sec, 0, keepdims=False))
    cot_first, cot_second = pick(first, cot_own, cot_other)

    if fast:
        chunks = [None] * 4
        quad0 = jnp.stack(z_parts(own[0]))
        a0, b0 = ab_parts(quad0)
        quad1 = jnp.stack(z_parts(own[1]))
        chunks[0] = core_parts(quad0, a0, b0, over_b(a0))
        quad1, own[2], *chunks[0] = fence(quad1, own[2], *chunks[0])
        a1, b1 = ab_parts(quad1)
        quad2 = jnp.stack(z_parts(own[2]))
    ka = kernel_stem_feed(ids, chunks[0], frames)
    prm = ka.prm
    if fast:
        ka.x1, quad1, a1, b1, quad2, own[3] = fence(ka.x1, quad1, a1, b1, quad2, own[3])
        chunks[1] = core_parts(quad1, a1, b1, over_b(a1))
        ka.x1, *chunks[1] = fence(ka.x1, *chunks[1])
        a2, b2 = ab_parts(quad2)
        quad3 = jnp.stack(z_parts(own[3]))
    kb = kernel_rest_first(ids, chunks[1], prm, ka.x1)
    if fast:
        kb.sent, quad2, a2, b2, quad3 = fence(kb.sent, quad2, a2, b2, quad3)
        chunks[2] = core_parts(quad2, a2, b2, over_b(a2))
        kb.sent, *chunks[2] = fence(kb.sent, *chunks[2])
        a3, b3 = ab_parts(quad3)
    kc = kernel_first_second(ids, chunks[2], prm, kb.sent)
    if fast:
        kc.x3, quad3, a3, b3 = fence(kc.x3, quad3, a3, b3)
        chunks[3] = core_parts(quad3, a3, b3, over_b(a3))
    kd = kernel_turn(ids, chunks[3], chunks[2], prm, kc.x3, cot_second, allowed, kc.x2, kc.gated, kc.deep)
    to_send = jnp.where(first, kd.sent, kb.sent)
    own_sent = jnp.where(first, kb.sent, kd.sent)
    other_sent = swap(to_send)
    if fast:
        came0 = over_core(kd.send)
    ke = kernel_back_early(
        1, ids, chunks[2], FEED // 2, chunks[2], 0, prm, kd.dx2, kc.x1, kc.qkv, kc.ls, kc.mixed,
        kb.sent, kc.hid, None,
    )
    ig_second = ke.ig.astype(BF)
    if fast:
        other_sent, came0, ke.send, ig_second = fence(other_sent, came0, ke.send, ig_second)
        near0, far0 = halves(kd.keep, came0)
        came0 = over_a(far0)
        came1 = over_core(ke.send)
    kf = kernel_back_late(
        ids, chunks[1], chunks[1], chunks[3], prm, kb.x4, kb.sent, cot_first, allowed, ig_second,
        kb.x3, kb.hid, kb.x2, kb.gated, kb.deep, kd.ghead,
    )
    if fast:
        came0, came1, kf.send, kf.dx2 = fence(came0, came1, kf.send, kf.dx2)
        near0, far0 = halves(near0, came0)
        near1, far1 = halves(ke.keep, came1)
        came0 = over_b(far0)
        came1 = over_a(far1)
        came2 = over_core(kf.send)
    stem = dict(
        pre=ka.pre,
        wout=ka.wout,
        frames=frames,
        small_first=kf.small,
        small_second=kd.small + ke.small,
    )
    kg = kernel_back_early(
        0, ids, chunks[1], 0, chunks[0], FLAT, prm, kf.dx2, ka.x1, kb.qkv, kb.ls, kb.mixed, ka.x0,
        ka.hid, stem,
    )
    if fast:
        came0, came1, came2, kg.send = fence(came0, came1, came2, kg.send)
        near2, far2 = halves(kf.keep, came2)
        near1, far1 = halves(near1, came1)
        came3 = over_core(kg.send)
        came2 = over_a(far2)
        came1 = over_b(far1)
        sum0 = z_sum(quarters(near0, came0))
        near3, far3 = halves(kg.keep, came3)
        near2, far2 = halves(near2, came2)
        came3 = over_a(far3)
        came2 = over_b(far2)
        sum1 = z_sum(quarters(near1, came1))
        sum2 = z_sum(quarters(near2, came2))
        near3, far3 = halves(near3, came3)
        came3 = over_b(far3)
        sum3 = z_sum(quarters(near3, came3))
    other_grad = swap(jnp.where(first, ke.ig, kg.ig).astype(BF)).astype(F32)
    own_grad = jnp.where(first, kg.ig, ke.ig)
    input_grads = jnp.stack(pick(first, own_grad, other_grad))[None, :, None]
    ko = kernel_outputs_of(fast, ids, sec, chunks[3], own_sent, other_sent, allowed_both, lengths)
    activations = ko.acts[None, :, None]
    log_probs = ko.logp[None, :, None]
    if fast:
        shards = own_shards(sum0, sum1, sum2, sum3, dp, first)
    else:
        shards = reduce_plain([(k.keep, k.send) for k in (kd, ke, kf, kg)])
    return (activations, log_probs, input_grads, *shards)


def kernel_outputs_of(fast, ids, sec, head_bufs, own, other, allowed, lengths):
    if not fast:
        mine, theirs = own, other
        flip = sec == 1
        own, other = jnp.where(flip, theirs, mine), jnp.where(flip, mine, theirs)
    return kernel_outputs(ids, head_bufs, own, other, allowed, lengths[:, 0])


def own_pieces(low, sec, dp, first):
    feed_in, feed_out, attend_in, attend_out, conv_in, depth, conv_out, gains, stem_in, stem_out, head = low
    feeds = [pack_feed(feed_in[0, j], feed_out[0, j]).reshape(2, FEED // 2, 512) for j in range(2)]
    attn = pack_attn(attend_in[0], attend_out[0]).reshape(2, ATTN // 2, 512)
    conv = pack_conv(conv_in[0], conv_out[0]).reshape(2, CONV // 2, 512)
    stem = pack_stem(stem_in, stem_out, depth[0], gains[0], dp % 4)

    def spread(both):
        mine = lax.dynamic_index_in_dim(both, sec, 0, keepdims=False)
        theirs = over_x(lax.dynamic_index_in_dim(both, 1 - sec, 0, keepdims=False))
        return pick(first, mine, theirs)

    feed_first, feed_second = spread(feeds[0])
    rest_first, rest_second = spread(jnp.concatenate([attn, conv, feeds[1]], axis=1))
    edge = ATTN // 2 + CONV // 2
    return [
        jnp.concatenate([stem, feed_first]),
        rest_first,
        jnp.concatenate([feed_second, rest_second[:edge]]),
        jnp.concatenate([rest_second[edge:], head.T]),
    ]


def own_shards(second_late, second_early, first_late, first_early, dp, first):
    edge, early = FEED // 2 + CONV // 2, ATTN // 2 + FEED // 2

    def join(of_first, of_second):
        own = jnp.where(first, of_first, of_second)
        other = over_x(jnp.where(first, of_second, of_first).astype(BF)).astype(F32)
        return jnp.stack(pick(first, own, other))

    late = join(first_late[:edge], second_late)
    earlier = join(first_early[:early], second_early)
    half = lambda part, begin, rows: part[:, begin : begin + rows].reshape(2 * rows, 512)
    feeds = [half(earlier, ATTN // 2, FEED // 2), half(late, 0, FEED // 2)]
    attn = half(earlier, 0, ATTN // 2)
    conv = half(late, FEED // 2, CONV // 2)
    head = first_late[edge:]
    g_stem_in, g_stem_out, g_depth, g_gains = unpack_stem(first_early[early:], dp % 4)
    return (
        jnp.stack([unpack_in(f, 4) for f in feeds])[None],
        jnp.stack([f[128:] for f in feeds])[None],
        unpack_in(attn, 3)[None],
        attn[96:][None],
        unpack_in(conv, 2)[None],
        g_depth[None],
        conv[64:][None],
        g_gains[None],
        g_stem_in,
        g_stem_out,
        head.T,
    )


def spread_order():
    order = []
    for cr, a, b, zk in pieces():
        px, py = (b, a) if cr else (a, b)
        order.append(px * 16 + zk * 4 + py * 2 + cr)
    return order


def gather_plain(low):
    axes = (2, 2, 1, 1, 1, 2, 1, 2)
    whole = []
    for weight, axis in zip(low[:8], axes):
        axis = 2 if weight.ndim == 4 else axis
        part = lax.all_gather(weight[0], "dp", axis=axis - 1, tiled=True)
        whole.append(lax.all_gather(part, "section", axis=0))
    feed_in, feed_out, attend_in, attend_out, conv_in, depth, conv_out, gains = whole
    stem_in = lax.all_gather(low[8], BOTH, axis=1, tiled=True)
    stem_out = lax.all_gather(low[9], BOTH, axis=0, tiled=True)
    head = lax.all_gather(low[10], BOTH, axis=1, tiled=True)
    order = spread_order()

    def layer(l):
        rows = lambda w, n: w.reshape(16, n, w.shape[-1])
        feeds = [jax.vmap(pack_feed)(rows(feed_in[l, j], 32), rows(feed_out[l, j], 128)) for j in range(2)]
        attn = jax.vmap(pack_attn)(rows(attend_in[l], 32), rows(attend_out[l], 32))
        conv = jax.vmap(pack_conv)(rows(conv_in[l], 32), rows(conv_out[l], 32))
        cut = lambda w: w.reshape(16, 2, w.shape[1] // 2, 512).transpose(1, 0, 2, 3).reshape(32, w.shape[1] // 2, 512)
        return [cut(w) for w in (feeds[0], attn, conv, feeds[1])]

    one, two = layer(0), layer(1)
    columns = lambda w, n: w.reshape(*w.shape[:-1], n, w.shape[-1] // n)
    small = lambda w: jnp.moveaxis(columns(w, 16), 2, 1).reshape(32, w.shape[1], 32)
    stem = jax.vmap(pack_stem)(
        jnp.moveaxis(columns(stem_in, 32), 1, 0),
        stem_out.reshape(32, 8, 512),
        small(depth),
        small(gains),
        jnp.arange(32) % 4,
    )
    head = head.T.reshape(32, 32, 512)
    chunks = ([stem, one[0]], one[1:], [two[0], two[1], two[2]], [two[3], head])
    placed = []
    for parts in chunks:
        joined = jnp.concatenate(parts, axis=1)
        placed.append([jnp.stack([joined[p] for p in order[4 * i : 4 * i + 4]]) for i in range(8)])
    return placed


def reduce_plain(grads):
    order = spread_order()
    place = [order.index(p) for p in range(32)]
    chunks = []
    for keep, send in grads:
        both = jnp.concatenate([keep, send])
        chunks.append(jnp.stack([both[q] for q in place]).astype(F32))
    edge, early = FEED // 2 + CONV // 2, ATTN // 2 + FEED // 2
    whole = []
    for late, earlier in ((chunks[2], chunks[3]), (chunks[0], chunks[1])):
        glue = lambda part, begin, rows: (
            part[:, begin : begin + rows].reshape(2, 16, rows, 512).transpose(1, 0, 2, 3).reshape(16, 2 * rows, 512)
        )
        feeds = [glue(earlier, ATTN // 2, FEED // 2), glue(late, 0, FEED // 2)]
        attn, conv = glue(earlier, 0, ATTN // 2), glue(late, FEED // 2, CONV // 2)
        spread = lambda w, n: jax.vmap(lambda rows: unpack_in(rows, n))(w).reshape(512, 512 * n)
        whole.append(
            (
                jnp.stack([spread(f, 4) for f in feeds]),
                jnp.stack([f[:, 128:].reshape(FF, 512) for f in feeds]),
                spread(attn, 3),
                attn[:, 96:].reshape(512, 512),
                spread(conv, 2),
                conv[:, 64:].reshape(512, 512),
            )
        )
    head = chunks[2][:, edge:].reshape(1024, 512).T
    g_stem_in, g_stem_out, g_depth, g_gains = jax.vmap(unpack_stem)(chunks[3][:, early:], jnp.arange(32) % 4)
    g_stem_in = jnp.moveaxis(g_stem_in, 0, 1).reshape(640, 256)
    g_stem_out = g_stem_out.reshape(256, 512)
    lanes = lambda w: jnp.moveaxis(w.reshape(2, 16, w.shape[1], 32), 1, 2).reshape(2, w.shape[1], 512)
    g_depth, g_gains = lanes(g_depth), lanes(g_gains)
    stacked = [jnp.stack([whole[0][i], whole[1][i]]) for i in range(6)]

    def shard(value, axis):
        value = lax.psum_scatter(value, "section", scatter_dimension=0, tiled=True)
        return lax.psum_scatter(value, "dp", scatter_dimension=axis, tiled=True)

    return (
        shard(stacked[0], 2),
        shard(stacked[1], 2),
        shard(stacked[2], 1),
        shard(stacked[3], 1),
        shard(stacked[4], 1),
        shard(g_depth, 2),
        shard(stacked[5], 1),
        shard(g_gains, 2),
        lax.psum_scatter(g_stem_in, BOTH, scatter_dimension=1, tiled=True),
        lax.psum_scatter(g_stem_out, BOTH, scatter_dimension=0, tiled=True),
        lax.psum_scatter(head, BOTH, scatter_dimension=1, tiled=True),
    )


def solution(mesh):
    fast = dict(mesh.shape) == {"section": 2, "dp": 16}

    def body(*args):
        return on_device(fast, *args)

    layer_specs = (
        P("section", None, "dp", None),
        P("section", None, "dp", None),
        P("section", "dp", None),
        P("section", "dp", None),
        P("section", "dp", None),
        P("section", None, "dp"),
        P("section", "dp", None),
        P("section", None, "dp"),
        P(None, BOTH),
        P(BOTH, None),
        P(None, BOTH),
    )
    rows = P("section", None, "dp", None, None)
    return jax.shard_map(
        body,
        mesh=mesh,
        in_specs=(P(None, "dp", None, None), P(None, "dp"), P(None, "dp"), P(), rows) + layer_specs,
        out_specs=(rows, rows, rows) + layer_specs,
        check_vma=False,
    )
```

```python
import types

import jax
import jax.numpy as jnp
from jax import lax
from jax.experimental import pallas as pl
from jax.experimental.pallas import tpu as pltpu
from jax.sharding import PartitionSpec as P

D = 512
HEADS = 8
HDIM = 64
FF = 2048
TAPS = 9
EPS = 1e-05
MASKED = -1e30
RB = 512
BOTH = ("section", "dp")
BF = jnp.bfloat16
F32 = jnp.float32

FEED, ATTN, CONV = 256, 128, 96
FLAT = 32
SMALL = 16


def dotn(a, b):
    return lax.dot_general(a, b, (((1,), (0,)), ((), ())), preferred_element_type=F32)


def dotr(a, b):
    return lax.dot_general(a, b, (((1,), (1,)), ((), ())), preferred_element_type=F32)


def dotl(a, b):
    return lax.dot_general(a, b, (((0,), (0,)), ((), ())), preferred_element_type=F32)


def sigmoid(v):
    return 0.5 * jnp.tanh(0.5 * v) + 0.5


def unit_rows(v):
    c = v - jnp.mean(v, axis=-1, keepdims=True)
    r = lax.rsqrt(jnp.mean(c * c, axis=-1, keepdims=True) + EPS)
    return c * r, r


def unit_back(dn, u, r, gain):
    du = dn * gain
    dv = r * (du - jnp.mean(du, axis=-1, keepdims=True) - u * jnp.mean(du * u, axis=-1, keepdims=True))
    return dv, jnp.sum(dn * u, axis=0, keepdims=True)


def row_mask(length, start, rows, columns):
    return (lax.broadcasted_iota(jnp.int32, (rows, columns), 0) + start < length).astype(F32)


def row_loop(body):
    for i in range(512 // RB):
        body(slice(i * RB, i * RB + RB), i * RB)


def piece_of(ids, cr, a, b, zk):
    pc = ids[3] ^ cr
    px = ids[0] ^ (a + pc * (b - a))
    py = ids[2] ^ (b + pc * (a - b))
    pz = ids[1] ^ zk
    return px, pz * 4 + py * 2 + pc


def pieces():
    return [(cr, a, b, zk) for cr in range(2) for a in range(2) for b in range(2) for zk in range(4)]


def start_load(ids, bufs, row, rows, scr, sem, flat=False):
    for cr, a, b, zk in pieces():
        px, d = piece_of(ids, cr, a, b, zk)
        src = bufs[cr * 4 + a * 2 + b].at[zk, row : row + rows]
        if flat:
            dst = scr.at[px * 16 + d]
        else:
            dst = scr.at[d, pl.ds(pl.multiple_of(px * rows, 16), rows)]
        pltpu.make_async_copy(src, dst, sem).start()


def wait_load(scr, sem):
    pltpu.make_async_copy(scr, scr, sem).wait()


def start_store(ids, scr, keep, send, row, rows, sem, flat=False):
    for cr, a, b, zk in pieces():
        px, d = piece_of(ids, cr, a, b, zk)
        if flat:
            src = scr.at[px * 16 + d]
        else:
            src = scr.at[d, pl.ds(pl.multiple_of(px * rows, 16), rows)]
        dst = (send if cr else keep).at[a * 8 + b * 4 + zk, row : row + rows]
        pltpu.make_async_copy(src, dst, sem).start()


def wait_store(scr, sem):
    pltpu.make_async_copy(scr, scr, sem).wait()


def in_block(w, j):
    return w[:, 32 * j : 32 * j + 32, :].reshape(512, 512)


def out_block(w, j):
    return w[4 * j : 4 * j + 4, 128:256, :].reshape(512, 512)


def feed_fwd(x, w, gain, hid, out):
    def body(rs, start):
        v = x[rs, :].astype(F32)
        u, _ = unit_rows(v)
        n = (u * gain).astype(BF)
        total = jnp.zeros((RB, 512), F32)
        for j in range(4):
            h = dotn(n, in_block(w, j))
            hid[rs, 512 * j : 512 * j + 512] = h.astype(BF)
            total = total + dotn((h * sigmoid(h)).astype(BF), out_block(w, j))
        out[rs, :] = v + 0.5 * total

    row_loop(body)


def feed_bwd(dx, x, hid, w, gain, out, gw, small, row, s):
    def body(rs, start):
        g = dx[rs, :]
        v = x[rs, :].astype(F32)
        u, r = unit_rows(v)
        s.n[rs, :] = (u * gain).astype(BF)
        d = (0.5 * g).astype(BF)
        s.d[rs, :] = d
        dn = jnp.zeros((RB, 512), F32)
        for j in range(4):
            h = hid[rs, 512 * j : 512 * j + 512].astype(F32)
            sg = sigmoid(h)
            s.act[rs, 512 * j : 512 * j + 512] = (h * sg).astype(BF)
            dh = (dotr(d, out_block(w, j)) * (sg * (1.0 + h * (1.0 - sg)))).astype(BF)
            s.dh[rs, 512 * j : 512 * j + 512] = dh
            dn = dn + dotr(dh, in_block(w, j))
        dv, gg = unit_back(dn, u, r, gain)
        out[rs, :] = g + dv
        small[row : row + 1, :] += gg

    row_loop(body)
    for j in range(4):
        cols = slice(512 * j, 512 * j + 512)
        gw[:, 32 * j : 32 * j + 32, :] = dotl(s.n[...], s.dh[:, cols]).astype(BF).reshape(16, 32, 512)
        gw[4 * j : 4 * j + 4, 128:256, :] = dotl(s.act[:, cols], s.d[...]).astype(BF).reshape(4, 128, 512)


def lanes_of(half, axis=1, count=1):
    shape = (count, 128) if axis else (128, count)
    return (lax.broadcasted_iota(jnp.int32, shape, axis) + 64 * half) % 128 - 64


def attn_fwd(x, w, gain, length, qkv, ls, mixt, out):
    def project(rs, start):
        u, _ = unit_rows(x[rs, :])
        n = (u * gain).astype(BF)
        for j in range(3):
            qkv[rs, 512 * j : 512 * j + 512] = dotn(n, in_block(w, j)).astype(BF)

    row_loop(project)

    for hp in range(4):
        at = hp * 128
        k = qkv[:, pl.ds(512 + at, 128)].astype(F32)
        vt = qkv[:, pl.ds(1024 + at, 128)].astype(F32).T
        outside = jnp.where(lax.broadcasted_iota(jnp.int32, (512, 128), 0) < length, 0.0, MASKED)
        kx, vx = [], []
        for hh in range(2):
            free = lanes_of(hh)
            kx.append(jnp.where(free < 0, k, jnp.where(free == 0, outside, 0.0)).astype(BF))
            free = lanes_of(hh, 0, 512)
            vx.append(jnp.where(free < 0, vt, jnp.where(free == 0, 1.0, 0.0)).astype(BF))

        def body(rs, start):
            q = qkv[rs, pl.ds(at, 128)].astype(F32) * HDIM**-0.5
            parts = []
            for hh in range(2):
                free = lanes_of(hh)
                qx = jnp.where(free < 0, q, jnp.where(free == 0, 1.0, 0.0)).astype(BF)
                sc = dotr(kx[hh], qx)
                top = jnp.max(sc, axis=0, keepdims=True)
                both = dotn(vx[hh], jnp.exp(sc - top).astype(BF))
                tot = both[64 * (1 - hh) : 64 * (1 - hh) + 1, :]
                parts.append(both * (1.0 / tot))
                ls[pl.ds(hp * 2 + hh, 1), rs] = top + jnp.log(tot)
            mixt[pl.ds(at, 128), rs] = jnp.where(lanes_of(0, 0, RB) < 0, parts[0], parts[1]).astype(BF)

        row_loop(body)

    def project_out(rs, start):
        out[rs, :] = x[rs, :] + dotl(mixt[:, rs], w[:, 96:128, :].reshape(512, 512))

    row_loop(project_out)


def attn_bwd(dx, x, qkv, ls, mixt, w, gain, length, out, gw, small, row, s):
    def first(rs, start):
        u, _ = unit_rows(x[rs, :])
        s.n[rs, :] = (u * gain).astype(BF)
        d = dx[rs, :].astype(BF)
        s.d[rs, :] = d
        s.dm[:, rs] = dotr(w[:, 96:128, :].reshape(512, 512), d).astype(BF)

    row_loop(first)
    gw[:, 96:128, :] = dotn(mixt[...], s.d[...]).astype(BF).reshape(16, 32, 512)

    for hp in range(4):
        at = hp * 128
        s.dq[...] = jnp.zeros((128, 512), F32)
        q = qkv[:, pl.ds(at, 128)].astype(F32) * HDIM**-0.5
        kt = qkv[:, pl.ds(512 + at, 128)].astype(F32).T * HDIM**-0.5
        dmt = s.dm[pl.ds(at, 128), :].astype(F32)
        prod = dmt * mixt[pl.ds(at, 128), :].astype(F32)
        qx, qs, dms, deltas, sums = [], [], [], [], []
        for hh in range(2):
            free = lanes_of(hh)
            qs.append(jnp.where(free < 0, q, 0.0).astype(BF))
            qx.append(jnp.where(free < 0, q, jnp.where(free == 0, 1.0, 0.0)).astype(BF))
            free = lanes_of(hh, 0, 512)
            dms.append(jnp.where(free < 0, dmt, 0.0).astype(BF))
            deltas.append(jnp.sum(prod[64 * hh : 64 * hh + 64, :], axis=0, keepdims=True))
            s.kt[128 * hh : 128 * hh + 128, :] = jnp.where(free < 0, kt, 0.0).astype(BF)
            sums.append(ls[pl.ds(hp * 2 + hh, 1), :])

        def body(rs, start):
            k = qkv[rs, pl.ds(512 + at, 128)].astype(F32)
            v = qkv[rs, pl.ds(1024 + at, 128)]
            outside = jnp.where(lax.broadcasted_iota(jnp.int32, (RB, 128), 0) + start < length, 0.0, MASKED)
            dk = jnp.zeros((RB, 128), F32)
            dv = jnp.zeros((RB, 128), F32)
            for hh in range(2):
                free = lanes_of(hh)
                kx = jnp.where(free < 0, k, jnp.where(free == 0, outside, 0.0)).astype(BF)
                p = jnp.exp(dotr(kx, qx[hh]) - sums[hh])
                ds = (p * (dotn(v, dms[hh]) - deltas[hh])).astype(BF)
                dv = dv + dotr(p.astype(BF), dms[hh])
                dk = dk + dotn(ds, qs[hh])
                s.dq[...] += dotn(s.kt[128 * hh : 128 * hh + 128, rs], ds)
            s.dpk[rs, pl.ds(512 + at, 128)] = dk.astype(BF)
            s.dpk[rs, pl.ds(1024 + at, 128)] = dv.astype(BF)

        row_loop(body)
        s.dpk[:, pl.ds(at, 128)] = s.dq[...].T.astype(BF)

    def last(rs, start):
        u, r = unit_rows(x[rs, :])
        dn = jnp.zeros((RB, 512), F32)
        for j in range(3):
            dn = dn + dotr(s.dpk[rs, 512 * j : 512 * j + 512], in_block(w, j))
        dv, gg = unit_back(dn, u, r, gain)
        out[rs, :] = dx[rs, :] + dv
        small[row : row + 1, :] += gg

    row_loop(last)
    for j in range(3):
        gw[:, 32 * j : 32 * j + 32, :] = (
            dotl(s.n[...], s.dpk[:, 512 * j : 512 * j + 512]).astype(BF).reshape(16, 32, 512)
        )


PAD = 8


def conv_fwd(x, w, prm, length, gated, deep, out, pad):
    pad[0:PAD, :] = jnp.zeros((PAD, 512), F32)
    pad[PAD + 512 : 2 * PAD + 512, :] = jnp.zeros((PAD, 512), F32)

    def first(rs, start):
        u, _ = unit_rows(x[rs, :])
        n = (u * prm[TAPS + 2 : TAPS + 3, :]).astype(BF)
        a = dotn(n, in_block(w, 0))
        b = dotn(n, in_block(w, 1))
        gated[rs, 0:512] = a
        gated[rs, 512:1024] = b
        pad[pl.ds(start + PAD, RB), :] = a * sigmoid(b) * row_mask(length, start, RB, 512)

    row_loop(first)
    for i in range(512 // RB):
        total = jnp.zeros((RB, 512), F32)
        for t in range(TAPS):
            begin = i * RB + PAD - TAPS // 2 + t
            total = total + prm[t : t + 1, :] * pad[begin : begin + RB, :]
        deep[i * RB : i * RB + RB, :] = total

    def last(rs, start):
        u, _ = unit_rows(deep[rs, :])
        m = u * prm[TAPS + 3 : TAPS + 4, :]
        act = (m * sigmoid(m)).astype(BF)
        out[rs, :] = x[rs, :] + dotn(act, w[:, 64:96, :].reshape(512, 512))

    row_loop(last)


def conv_bwd(dx, x, gated, deep, w, prm, length, out, gw, small, s):
    for pad in (s.pad, s.back):
        pad[0:PAD, :] = jnp.zeros((PAD, 512), F32)
        pad[PAD + 512 : 2 * PAD + 512, :] = jnp.zeros((PAD, 512), F32)
    gain_in = prm[TAPS + 2 : TAPS + 3, :]
    gain_mid = prm[TAPS + 3 : TAPS + 4, :]

    def first(rs, start):
        padded = pl.ds(start + PAD, RB)
        d = dx[rs, :].astype(BF)
        s.d[rs, :] = d
        u3, r3 = unit_rows(deep[rs, :])
        m = u3 * gain_mid
        sg = sigmoid(m)
        s.act[rs, :] = (m * sg).astype(BF)
        dmid = dotr(d, w[:, 64:96, :].reshape(512, 512)) * (sg * (1.0 + m * (1.0 - sg)))
        ddeep, gg = unit_back(dmid, u3, r3, gain_mid)
        s.back[padded, :] = ddeep
        small[TAPS + 3 : TAPS + 4, :] += gg
        s.pad[padded, :] = (
            gated[rs, 0:512] * sigmoid(gated[rs, 512:1024]) * row_mask(length, start, RB, 512)
        )

    row_loop(first)
    gw[:, 64:96, :] = dotl(s.act[...], s.d[...]).astype(BF).reshape(16, 32, 512)
    for i in range(512 // RB):
        rows = slice(i * RB, i * RB + RB)
        ddeep = s.back[PAD + i * RB : PAD + i * RB + RB, :]
        dglu = jnp.zeros((RB, 512), F32)
        for t in range(TAPS):
            begin = i * RB + PAD - TAPS // 2 + t
            small[t : t + 1, :] += jnp.sum(ddeep * s.pad[begin : begin + RB, :], axis=0, keepdims=True)
            begin = i * RB + PAD + TAPS // 2 - t
            dglu = dglu + prm[t : t + 1, :] * s.back[begin : begin + RB, :]
        dglu = dglu * row_mask(length, i * RB, RB, 512)
        sg = sigmoid(gated[rows, 512:1024])
        ga = dglu * sg
        s.dga[rows, :] = ga.astype(BF)
        s.dgb[rows, :] = (ga * gated[rows, 0:512] * (1.0 - sg)).astype(BF)

    def last(rs, start):
        u, r = unit_rows(x[rs, :])
        s.n[rs, :] = (u * gain_in).astype(BF)
        dn = dotr(s.dga[rs, :], in_block(w, 0)) + dotr(s.dgb[rs, :], in_block(w, 1))
        dv, gg = unit_back(dn, u, r, gain_in)
        out[rs, :] = dx[rs, :] + dv
        small[TAPS + 2 : TAPS + 3, :] += gg

    row_loop(last)
    gw[:, 0:32, :] = dotl(s.n[...], s.dga[...]).astype(BF).reshape(16, 32, 512)
    gw[:, 32:64, :] = dotl(s.n[...], s.dgb[...]).astype(BF).reshape(16, 32, 512)


def finish_fwd(x4, prm, length, sent):
    def body(rs, start):
        u, _ = unit_rows(x4[rs, :])
        sent[rs, :] = (u * prm[TAPS + 5 : TAPS + 6, :] * row_mask(length, start, RB, 512)).astype(BF)

    row_loop(body)


def head_rows(sent, w, permit):
    logits = dotr(sent, w)
    top = jnp.max(jnp.where(permit, logits, MASKED), axis=-1, keepdims=True)
    e = jnp.exp(jnp.where(permit, logits - top, MASKED))
    return logits, top + jnp.log(jnp.sum(e, axis=-1, keepdims=True))


def head_bwd(x4, sent, w, allowed, cot, prm, length, extra, out, gl, small):
    permit = allowed[...] > 0
    gain = prm[TAPS + 5 : TAPS + 6, :]

    def body(rs, start):
        hw = w[...].reshape(1024, 512)
        logits, logsum = head_rows(sent[rs, :], hw, permit)
        weighted = jnp.where(permit, cot[rs, :].astype(F32), 0.0) * row_mask(length, start, RB, 1024)
        probs = jnp.exp(jnp.where(permit, logits - logsum, MASKED))
        g = (weighted - probs * jnp.sum(weighted, axis=-1, keepdims=True)).astype(BF)
        gl[rs, :] = g
        gs = dotn(g, hw)
        if extra is not None:
            gs = gs + extra[rs, :].astype(BF).astype(F32)
        u, r = unit_rows(x4[rs, :])
        dv, gg = unit_back(gs * row_mask(length, start, RB, 512), u, r, gain)
        out[rs, :] = dv
        small[TAPS + 5 : TAPS + 6, :] += gg

    row_loop(body)


ANY, VMEM, SMEM = pl.ANY, pltpu.VMEM, pltpu.SMEM
LATE = object()


class Late:
    def __init__(self, source, held, sem):
        self.copy, self.held, self.going, self.here = pltpu.make_async_copy(source, held, sem), held, False, False

    def go(self):
        self.going = True
        self.copy.start()

    def get(self):
        if not self.going:
            self.go()
        if not self.here:
            self.copy.wait()
        self.here = True
        return self.held


class Soon:
    def __init__(self, held, target, sem):
        self.copy, self.held, self.going = pltpu.make_async_copy(held, target, sem), held, False

    def go(self):
        self.going = True
        self.copy.start()

    def end(self):
        if not self.going:
            self.go()
        self.copy.wait()


def run(body, micros, ins, outs, scratch):
    flat, held = [], []
    for value, space in ins.values():
        flat += [(array, ANY if space is LATE else space) for array in (value if isinstance(value, list) else [value])]
        if space is LATE:
            held.append((value.shape, value.dtype))
    held += [(shape, dtype) for shape, dtype, space in outs.values() if space is LATE]

    def kernel(*refs):
        left = list(refs)
        ns = types.SimpleNamespace()
        waiting, soon = [], []
        for key, (value, space) in ins.items():
            if isinstance(value, list):
                setattr(ns, key, [left.pop(0) for _ in value])
            else:
                setattr(ns, key, left.pop(0))
        for key in [*outs, *scratch]:
            setattr(ns, key, left.pop(0))
        ns.sems = left.pop()
        number = 8
        for key, (_, space) in ins.items():
            if space is LATE:
                setattr(ns, key, Late(getattr(ns, key), left.pop(0), ns.sems.at[number]))
                number += 1
        for key, (_, _, space) in outs.items():
            if space is LATE:
                soon.append(Soon(left.pop(0), getattr(ns, key), ns.sems.at[number]))
                setattr(ns, key, soon[-1])
                number += 1
        body(ns)
        for result in soon:
            result.end()

    result = pl.pallas_call(
        kernel,
        out_shape=[jax.ShapeDtypeStruct(shape, dtype) for shape, dtype, _ in outs.values()],
        in_specs=[pl.BlockSpec(memory_space=space) for _, space in flat],
        out_specs=[pl.BlockSpec(memory_space=ANY if space is LATE else space) for _, _, space in outs.values()],
        scratch_shapes=[pltpu.VMEM(shape, dtype) for shape, dtype in [*scratch.values(), *held]]
        + [pltpu.SemaphoreType.DMA((8 + len(held),))],
        compiler_params=pltpu.CompilerParams(vmem_limit_bytes=58 * 2**20),
        cost_estimate=pl.CostEstimate(flops=int(micros * 1.1e9), bytes_accessed=2**20, transcendentals=0),
        name=body.__name__,
    )(*[array for array, _ in flat])
    return types.SimpleNamespace(**dict(zip(outs, result)))


ROWS = (512, 512)
WF, WA, WC, WH = ((16, FEED, 512), BF), ((16, ATTN, 512), BF), ((16, CONV, 512), BF), ((32, FLAT, 512), BF)
PADDED = ((512 + 2 * PAD, 512), F32)
LATE_ROWS = ATTN // 2 + CONV // 2


def gain_of(prm, number):
    return prm[TAPS + number : TAPS + number + 1, :]


def kernel_stem_feed(ids, bufs, frames):
    def stem_feed(k):
        start_load(k.ids, k.bufs, 0, FLAT, k.stem, k.sems.at[0], flat=True)
        k.frames.go()
        start_load(k.ids, k.bufs, FLAT, FEED // 2, k.w, k.sems.at[1])
        wait_load(k.stem, k.sems.at[0])
        stem = k.stem[...].astype(F32)
        for layer in range(2):
            for z in range(4):
                part = jnp.zeros((8, 512), F32)
                for q in range(4):
                    part = part + stem[layer * 16 + z * 4 + q, 24:32, :]
                k.prm[layer, 0:8, 128 * z : 128 * z + 128] = part[:, 0:128]
                k.prm[layer, 8:16, 128 * z : 128 * z + 128] = part[:, 128:256]
        win_a = stem[:, 0:8, :].reshape(256, 512).astype(BF)
        win_b = stem[:, 8:16, 0:128].reshape(256, 128).astype(BF)
        k.wout[...] = stem[:, 16:24, :].reshape(256, 512).astype(BF)
        frames, x0, x1, hid, pre = k.frames.get(), k.x0.held, k.x1.held, k.hid.held, k.pre.held

        def rows(rs, start):
            p = dotr(frames[rs, 0:512], win_a) + dotr(frames[rs, 512:640], win_b)
            pre[rs, :] = p
            x = dotn((p * sigmoid(p)).astype(BF), k.wout[...])
            x0[rs, :] = (x * row_mask(k.ids[4], start, RB, 512)).astype(BF)

        row_loop(rows)
        k.pre.go()
        k.x0.go()
        wait_load(k.w, k.sems.at[1])
        feed_fwd(x0, k.w, gain_of(k.prm.at[0], 0), hid, x1)

    return run(
        stem_feed,
        9,
        dict(ids=(ids, SMEM), bufs=(bufs, ANY), frames=(frames, LATE)),
        dict(
            prm=((2, SMALL, 512), F32, VMEM),
            pre=((512, 256), F32, LATE),
            wout=((256, 512), BF, VMEM),
            x0=(ROWS, BF, LATE),
            hid=((512, FF), BF, LATE),
            x1=(ROWS, F32, LATE),
        ),
        dict(stem=WH, w=WF),
    )


ATTN_OUTS = dict(qkv=((512, 1536), BF, LATE), ls=((8, 512), F32, VMEM), mixed=(ROWS, BF, LATE), x2=(ROWS, F32, LATE))
CONV_OUTS = dict(gated=((512, 1024), F32, LATE), deep=(ROWS, F32, LATE), x3=(ROWS, F32, LATE))


def attn_conv(k, x1, prm):
    wait_load(k.wa, k.sems.at[0])
    attn_fwd(x1, k.wa, gain_of(prm, 1), k.ids[4], k.qkv.held, k.ls, k.mixed.held, k.x2.held)
    for result in (k.qkv, k.mixed, k.x2):
        result.go()
    wait_load(k.wc, k.sems.at[1])
    conv_fwd(k.x2.held, k.wc, prm, k.ids[4], k.gated.held, k.deep.held, k.x3.held, k.pad)
    for result in (k.gated, k.deep, k.x3):
        result.go()


def kernel_rest_first(ids, bufs, prm, x1):
    def rest_first(k):
        k.x1.go()
        start_load(k.ids, k.bufs, 0, ATTN // 2, k.wa, k.sems.at[0])
        start_load(k.ids, k.bufs, ATTN // 2, CONV // 2, k.wc, k.sems.at[1])
        start_load(k.ids, k.bufs, LATE_ROWS, FEED // 2, k.wf, k.sems.at[2])
        prm = k.prm.at[0]
        attn_conv(k, k.x1.get(), prm)
        wait_load(k.wf, k.sems.at[2])
        feed_fwd(k.x3.held, k.wf, gain_of(prm, 4), k.hid.held, k.x4.held)
        k.hid.go()
        k.x4.go()
        finish_fwd(k.x4.held, prm, k.ids[4], k.sent)

    return run(
        rest_first,
        20,
        dict(ids=(ids, SMEM), bufs=(bufs, ANY), prm=(prm, VMEM), x1=(x1, LATE)),
        ATTN_OUTS | CONV_OUTS | dict(hid=((512, FF), BF, LATE), x4=(ROWS, F32, LATE), sent=(ROWS, BF, VMEM)),
        dict(wa=WA, wc=WC, wf=WF, pad=PADDED),
    )


def kernel_first_second(ids, bufs, prm, x0):
    def first_second(k):
        start_load(k.ids, k.bufs, 0, FEED // 2, k.wf, k.sems.at[2])
        start_load(k.ids, k.bufs, FEED // 2, ATTN // 2, k.wa, k.sems.at[0])
        start_load(k.ids, k.bufs, FEED // 2 + ATTN // 2, CONV // 2, k.wc, k.sems.at[1])
        prm = k.prm.at[1]
        wait_load(k.wf, k.sems.at[2])
        feed_fwd(k.x0, k.wf, gain_of(prm, 0), k.hid.held, k.x1.held)
        k.hid.go()
        k.x1.go()
        attn_conv(k, k.x1.held, prm)

    return run(
        first_second,
        20,
        dict(ids=(ids, SMEM), bufs=(bufs, ANY), prm=(prm, VMEM), x0=(x0, VMEM)),
        dict(hid=((512, FF), BF, LATE), x1=(ROWS, F32, LATE)) | ATTN_OUTS | CONV_OUTS,
        dict(wa=WA, wc=WC, wf=WF, pad=PADDED),
    )


def start_cot(k, layer):
    @pl.when(k.ids[5] == layer)
    def _():
        pltpu.make_async_copy(k.cots.at[k.ids[5]], k.cot, k.sems.at[2]).start()

    @pl.when(k.ids[5] != layer)
    def _():
        for number, part in enumerate(k.cot_other):
            pltpu.make_async_copy(part, k.cot.at[256 * number : 256 * number + 256], k.sems.at[2]).start()


FEED_SCRATCH = dict(n=(ROWS, BF), d=(ROWS, BF), act=((512, FF), BF), dh=((512, FF), BF), wf=WF, gf=WF)
HEAD_SCRATCH = dict(wh=WH, cot=((512, 1024), BF), gl=((512, 1024), BF), dx4=(ROWS, F32))


def kernel_turn(ids, bufs, prm, x3, cots, cot_other, allowed):
    def turn(k):
        k.x3.go()
        start_load(k.ids, k.bufs, 0, FEED // 2, k.wf, k.sems.at[0])
        start_load(k.ids, k.bufs, FEED // 2, FLAT, k.wh, k.sems.at[1], flat=True)
        start_cot(k, 1)
        prm = k.prm.at[1]
        k.small[...] = jnp.zeros((SMALL, 512), F32)
        x3 = k.x3.get()
        wait_load(k.wf, k.sems.at[0])
        feed_fwd(x3, k.wf, gain_of(prm, 4), k.hid, k.x4)
        finish_fwd(k.x4, prm, k.ids[4], k.sent)
        wait_load(k.wh, k.sems.at[1])
        wait_load(k.cot, k.sems.at[2])
        head_bwd(k.x4, k.sent, k.wh, k.allowed, k.cot, prm, k.ids[4], None, k.dx4, k.gl, k.small)
        k.ghead.held[...] = dotl(k.gl[...], k.sent[...])
        k.ghead.go()
        feed_bwd(k.dx4, x3, k.hid, k.wf, gain_of(prm, 4), k.dx3.held, k.gf, k.small, TAPS + 4, k)
        start_store(k.ids, k.gf, k.keep, k.send, 0, FEED // 2, k.sems.at[3])
        wait_store(k.gf, k.sems.at[3])

    rows = FEED // 2
    return run(
        turn,
        22,
        dict(
            ids=(ids, SMEM),
            bufs=(bufs, ANY),
            prm=(prm, VMEM),
            x3=(x3, LATE),
            cots=(cots, ANY),
            cot_other=(cot_other, ANY),
            allowed=(allowed, VMEM),
        ),
        dict(
            sent=(ROWS, BF, VMEM),
            ghead=((1024, 512), F32, LATE),
            dx3=(ROWS, F32, LATE),
            small=((SMALL, 512), F32, VMEM),
            keep=((16, rows, 512), BF, ANY),
            send=((16, rows, 512), BF, ANY),
        ),
        FEED_SCRATCH | HEAD_SCRATCH | dict(hid=((512, FF), BF), x4=(ROWS, F32)),
    )


def kernel_late(ids, bufs, head_bufs, prm, x4, sent, cots, cot_other, allowed, ig, x3, hid, ghead):
    def late(k):
        start_load(k.ids, k.hbufs, FEED // 2, FLAT, k.wh, k.sems.at[1], flat=True)
        start_cot(k, 0)
        k.x4.go()
        k.ig.go()
        start_load(k.ids, k.bufs, LATE_ROWS, FEED // 2, k.wf, k.sems.at[0])
        for operand in (k.ghead, k.x3, k.hid):
            operand.go()
        prm = k.prm.at[0]
        k.small[...] = jnp.zeros((SMALL, 512), F32)
        wait_load(k.wh, k.sems.at[1])
        wait_load(k.cot, k.sems.at[2])
        head_bwd(k.x4.get(), k.sent, k.wh, k.allowed, k.cot, prm, k.ids[4], k.ig.get(), k.dx4, k.gl, k.small)
        k.gh[...] = (k.ghead.get()[...] + dotl(k.gl[...], k.sent[...])).astype(BF).reshape(32, FLAT, 512)
        start_store(k.ids, k.gh, k.keep, k.send, FEED // 2, FLAT, k.sems.at[4], flat=True)
        wait_load(k.wf, k.sems.at[0])
        feed_bwd(k.dx4, k.x3.get(), k.hid.get(), k.wf, gain_of(prm, 4), k.dx3.held, k.gf, k.small, TAPS + 4, k)
        start_store(k.ids, k.gf, k.keep, k.send, 0, FEED // 2, k.sems.at[3])
        wait_store(k.gh, k.sems.at[4])
        wait_store(k.gf, k.sems.at[3])

    rows = FEED // 2 + FLAT
    return run(
        late,
        17,
        dict(
            ids=(ids, SMEM),
            bufs=(bufs, ANY),
            hbufs=(head_bufs, ANY),
            prm=(prm, VMEM),
            x4=(x4, LATE),
            sent=(sent, VMEM),
            cots=(cots, ANY),
            cot_other=(cot_other, ANY),
            allowed=(allowed, VMEM),
            ig=(ig, LATE),
            x3=(x3, LATE),
            hid=(hid, LATE),
            ghead=(ghead, LATE),
        ),
        dict(
            dx3=(ROWS, F32, LATE),
            small=((SMALL, 512), F32, VMEM),
            keep=((16, rows, 512), BF, ANY),
            send=((16, rows, 512), BF, ANY),
        ),
        FEED_SCRATCH | HEAD_SCRATCH | dict(gh=WH),
    )


def kernel_mid(layer, ids, bufs, row, prm, dx3, x2, gated, deep, x1, qkv, ls, mixed):
    def mid(k):
        for operand in (k.dx3, k.deep):
            operand.go()
        start_load(k.ids, k.bufs, row + ATTN // 2, CONV // 2, k.wc, k.sems.at[1])
        for operand in (k.gated, k.x2):
            operand.go()
        start_load(k.ids, k.bufs, row, ATTN // 2, k.wa, k.sems.at[0])
        for operand in (k.x1, k.mixed, k.qkv):
            operand.go()
        prm = k.prm.at[layer]
        k.small[...] = jnp.zeros((SMALL, 512), F32)
        wait_load(k.wc, k.sems.at[1])
        s = types.SimpleNamespace(
            n=k.n, d=k.d, act=k.act.at[:, 0:512], dga=k.dh.at[:, 0:512], dgb=k.dh.at[:, 512:1024], pad=k.pad, back=k.back
        )
        conv_bwd(k.dx3.get(), k.x2.get(), k.gated.get(), k.deep.get(), k.wc, prm, k.ids[4], k.dx2, k.gc, k.small, s)
        start_store(k.ids, k.gc, k.keep, k.send, ATTN // 2, CONV // 2, k.sems.at[3])
        wait_load(k.wa, k.sems.at[0])
        s = types.SimpleNamespace(n=k.n, d=k.d, dm=k.dm, dpk=k.act, dq=k.dq, kt=k.kt)
        attn_bwd(
            k.dx2, k.x1.get(), k.qkv.get(), k.ls, k.mixed.get(), k.wa, gain_of(prm, 1), k.ids[4], k.dx1.held, k.ga,
            k.small, TAPS + 1, s,
        )
        start_store(k.ids, k.ga, k.keep, k.send, 0, ATTN // 2, k.sems.at[2])
        wait_store(k.gc, k.sems.at[3])
        wait_store(k.ga, k.sems.at[2])

    return run(
        mid,
        21,
        dict(
            ids=(ids, SMEM),
            bufs=(bufs, ANY),
            prm=(prm, VMEM),
            dx3=(dx3, LATE),
            x2=(x2, LATE),
            gated=(gated, LATE),
            deep=(deep, LATE),
            x1=(x1, LATE),
            qkv=(qkv, LATE),
            ls=(ls, VMEM),
            mixed=(mixed, LATE),
        ),
        dict(
            dx1=(ROWS, F32, LATE),
            small=((SMALL, 512), F32, VMEM),
            keep=((16, LATE_ROWS, 512), BF, ANY),
            send=((16, LATE_ROWS, 512), BF, ANY),
        ),
        dict(
            wa=WA,
            wc=WC,
            ga=WA,
            gc=WC,
            dx2=(ROWS, F32),
            n=(ROWS, BF),
            d=(ROWS, BF),
            dm=(ROWS, BF),
            act=((512, 1536), BF),
            dh=((512, 1024), BF),
            pad=PADDED,
            back=PADDED,
            dq=((128, 512), F32),
            kt=((256, 512), BF),
        ),
    )


def kernel_early(layer, ids, bufs, row, prm, dx1, x0, hid, stem):
    def early(k):
        k.dx1.go()
        k.x0.go()
        start_load(k.ids, k.bufs, row, FEED // 2, k.wf, k.sems.at[1])
        k.hid.go()
        if stem is not None:
            k.pre.go()
            k.frames.go()
        prm = k.prm.at[layer]
        k.small[...] = jnp.zeros((SMALL, 512), F32)
        wait_load(k.wf, k.sems.at[1])
        ig = k.ig.held
        feed_bwd(k.dx1.get(), k.x0.get(), k.hid.get(), k.wf, gain_of(prm, 0), ig, k.gf, k.small, TAPS, k)
        k.ig.go()
        start_store(k.ids, k.gf, k.keep, k.send, 0, FEED // 2, k.sems.at[3])
        if stem is not None:
            pre, frames = k.pre.get(), k.frames.get()

            def rows(rs, start):
                d = (ig[rs, :] * row_mask(k.ids[4], start, RB, 512)).astype(BF)
                k.d[rs, :] = d
                p = pre[rs, :]
                sg = sigmoid(p)
                k.n[rs, 0:256] = (p * sg).astype(BF)
                k.n[rs, 256:512] = (dotr(d, k.wout[...]) * (sg * (1.0 + p * (1.0 - sg)))).astype(BF)

            row_loop(rows)
            k.gs[:, 0:8, :] = dotl(k.n[:, 256:512], frames[:, 0:512]).reshape(32, 8, 512)
            k.gs[:, 8:16, 0:128] = dotl(k.n[:, 256:512], frames[:, 512:640]).reshape(32, 8, 128)
            k.gs[:, 8:16, 128:512] = jnp.zeros((32, 8, 384), F32)
            k.gs[:, 16:24, :] = dotl(k.n[:, 0:256], k.d[...]).reshape(32, 8, 512)
            first, second = k.small[...], jnp.zeros((SMALL, 512), F32)
            for part in k.smalls[:2]:
                first = first + part[...]
            for part in k.smalls[2:]:
                second = second + part[...]
            for number, total in enumerate((first, second)):
                for z in range(4):
                    lanes = slice(128 * z, 128 * z + 128)
                    block = jnp.concatenate([total[0:8, lanes], total[8:16, lanes], jnp.zeros((8, 256), F32)], axis=1)
                    for q in range(4):
                        k.gs[number * 16 + z * 4 + q, 24:32, :] = block
            k.gsb[...] = k.gs[...].astype(BF)
            start_store(k.ids, k.gsb, k.keep, k.send, FEED // 2, FLAT, k.sems.at[4], flat=True)
            wait_store(k.gsb, k.sems.at[4])
        wait_store(k.gf, k.sems.at[3])

    rows = FEED // 2 + (0 if stem is None else FLAT)
    ins = dict(
        ids=(ids, SMEM),
        bufs=(bufs, ANY),
        prm=(prm, VMEM),
        dx1=(dx1, LATE),
        x0=(x0, LATE),
        hid=(hid, LATE),
    )
    scratch = dict(FEED_SCRATCH)
    if stem is not None:
        pre, wout, frames, smalls = stem
        ins |= dict(pre=(pre, LATE), wout=(wout, VMEM), frames=(frames, LATE), smalls=(smalls, VMEM))
        scratch |= dict(gs=((32, FLAT, 512), F32), gsb=WH)
    return run(
        early,
        13 if stem is not None else 10,
        ins,
        dict(
            ig=(ROWS, F32, LATE),
            small=((SMALL, 512), F32, VMEM),
            keep=((16, rows, 512), BF, ANY),
            send=((16, rows, 512), BF, ANY),
        ),
        scratch,
    )


def kernel_outputs(ids, head_bufs, sent_first, sent_second, other, allowed, lengths):
    def outputs(k):
        start_load(k.ids, k.hbufs, FEED // 2, FLAT, k.wh, k.sems.at[0], flat=True)
        for sec in range(2):

            @pl.when(k.ids[5] == sec)
            def _():
                pltpu.make_async_copy(k.second if sec else k.first, k.sent.at[sec], k.sems.at[1]).start()
                pltpu.make_async_copy(k.other, k.sent.at[1 - sec], k.sems.at[1]).start()

        wait_load(k.sent, k.sems.at[1])
        wait_load(k.wh, k.sems.at[0])
        for batch in range(2):
            permit = k.allowed[batch : batch + 1, :] > 0
            sent = k.sent[batch]
            logits, logsum = head_rows(sent, k.wh[...].reshape(1024, 512), permit)
            ok = row_mask(k.lengths[batch], 0, 512, 1024)
            k.logp.held[batch] = jnp.where(permit, logits - logsum, 0.0) * ok
            k.acts.held[batch] = sent.astype(F32)

    return run(
        outputs,
        9,
        dict(
            ids=(ids, SMEM),
            lengths=(lengths, SMEM),
            hbufs=(head_bufs, ANY),
            first=(sent_first, ANY),
            second=(sent_second, ANY),
            other=(other, ANY),
            allowed=(allowed, VMEM),
        ),
        dict(logp=((2, 512, 1024), F32, LATE), acts=((2, 512, 512), F32, LATE)),
        dict(wh=WH, sent=((2, 512, 512), BF)),
    )


def kernel_grads(ids, first, second, other):
    def grads(k):
        sec = k.ids[5]
        k.out.held[1 - sec] = k.other[...].astype(F32)

        @pl.when(sec == 0)
        def _():
            k.out.held[0] = k.first[...]

        @pl.when(sec != 0)
        def _():
            k.out.held[1] = k.second[...]

    return run(
        grads,
        3,
        dict(ids=(ids, SMEM), first=(first, VMEM), second=(second, VMEM), other=(other, VMEM)),
        dict(out=((2, 512, 512), F32, LATE)),
        dict(),
    ).out


def pack_feed(w_in, w_out):
    return jnp.concatenate([w_in.reshape(32, 4, 512).transpose(1, 0, 2).reshape(128, 512), w_out])


def pack_attn(w_in, w_out):
    return jnp.concatenate([w_in.reshape(32, 3, 512).transpose(1, 0, 2).reshape(96, 512), w_out])


def pack_conv(w_in, w_out):
    return jnp.concatenate([w_in.reshape(32, 2, 512).transpose(1, 0, 2).reshape(64, 512), w_out])


def unpack_in(rows, blocks):
    return rows[: 32 * blocks].reshape(blocks, 32, 512).transpose(1, 0, 2).reshape(32, 512 * blocks)


def pack_stem(stem_in, stem_out, depth, gains, quarter):
    turned = stem_in.T
    small = jnp.concatenate([depth, gains, jnp.zeros((1, 32), depth.dtype)])
    spread = lax.dynamic_update_slice(jnp.zeros((16, 128), depth.dtype), small, (0, 32 * quarter))
    return jnp.concatenate(
        [
            turned[:, :512],
            jnp.pad(turned[:, 512:], ((0, 0), (0, 384))),
            stem_out,
            jnp.concatenate([spread[:8], spread[8:], jnp.zeros((8, 256), depth.dtype)], axis=1),
        ]
    )


def unpack_stem(rows, quarter):
    turned = jnp.concatenate([rows[0:8], rows[8:16, :128]], axis=1)
    spread = jnp.concatenate([rows[24:32, 0:128], rows[24:32, 128:256]])
    small = lax.dynamic_slice(spread, (0, 32 * quarter), (16, 32))
    return turned.T, rows[16:24], small[:TAPS], small[TAPS : TAPS + 6]


def permutation(target):
    pairs = []
    for x in range(2):
        for d in range(16):
            tx, tz, ty, tc = target(x, d // 4, (d // 2) % 2, d % 2)
            pairs.append((x * 16 + d, tx * 16 + tz * 4 + ty * 2 + tc))
    return pairs


def across(value, target):
    return lax.ppermute(value, BOTH, permutation(target))


def over_x(value):
    return across(value, lambda x, z, y, c: (1 - x, z, y, c))


def over_core(value):
    return across(value, lambda x, z, y, c: (x, z, y, 1 - c))


def over_z(value, k):
    return across(value, lambda x, z, y, c: (x, z ^ k, y, c))


def over_a(value):
    return across(value, lambda x, z, y, c: (1 - x, z, y, c) if c == 0 else (x, z, 1 - y, c))


def over_b(value):
    return across(value, lambda x, z, y, c: (1 - x, z, y, c) if c == 1 else (x, z, 1 - y, c))


def fence(*values):
    return lax.optimization_barrier(values)


def z_parts(own):
    return [own] + [over_z(own, k) for k in (1, 2, 3)]


def ab_parts(quad):
    return over_a(quad), over_b(quad)


def core_parts(quad, ra, rb, rab):
    return [quad, rb, ra, rab] + [over_core(v) for v in (quad, rb, ra, rab)]


def add(*values):
    total = values[0].astype(F32)
    for value in values[1:]:
        total = total + value.astype(F32)
    return total


def halves(kept, came):
    cut = kept.shape[0] // 2
    return add(kept[:cut], came[:cut]).astype(BF), add(kept[cut:], came[cut:]).astype(BF)


def quarters(kept, came):
    return [add(kept[k], came[k]).astype(BF) for k in range(4)]


def z_sum(parts):
    return add(parts[0], *[over_z(parts[k], k) for k in (1, 2, 3)])


def pick(first, own, other):
    return jnp.where(first, own, other), jnp.where(first, other, own)


def on_device(fast, *args):
    (spectra, lengths, languages, token_masks, cotangent) = args[:5]
    masters = args[5:]
    sec = lax.axis_index("section")
    dp = lax.axis_index("dp")
    first = sec == 0
    low = [m.astype(BF) for m in masters]
    swap = lambda v: lax.ppermute(v, "section", [(0, 1), (1, 0)])
    cots = cotangent[0, :, 0]
    cot_send = lax.dynamic_index_in_dim(cots, 1 - sec, 0, keepdims=False)
    place = [sec, dp // 4, (dp // 2) % 2, dp % 2] if fast else [sec * 0] * 4
    ids = jnp.stack(place + [lengths[sec, 0], sec]).astype(jnp.int32)
    frames = lax.dynamic_index_in_dim(spectra, sec, 0, keepdims=False).reshape(512, -1)
    allowed_both = jnp.concatenate(
        [lax.dynamic_slice_in_dim(token_masks, languages[m, 0], 1, 0) for m in range(2)]
    ).astype(F32)
    allowed = lax.dynamic_slice_in_dim(allowed_both, sec, 1, 0)
    if fast:
        chunks = [None] * 4
        own_first, rest = own_pieces(low, sec, dp, first)
        early_cot, late_cot = cot_send[:256], cot_send[256:]
        own_first, rest, early_cot = fence(own_first, rest, early_cot)
        z0 = z_parts(own_first)
        own = own_rest(rest, low, sec, first)
        early_cot = swap(early_cot)
        *z0, own[0], early_cot = fence(*z0, own[0], early_cot)
        quad0 = jnp.stack(z0)
        a0, b0 = ab_parts(quad0)
        z1 = z_parts(own[0])
        quad0, a0, b0, *z1 = fence(quad0, a0, b0, *z1)
        ab0 = over_b(a0)
        core0 = [over_core(v) for v in (quad0, b0, a0)]
        quad1 = jnp.stack(z1)
        quad1, ab0, frames, *core0 = fence(quad1, ab0, frames, *core0)
        a1, b1 = ab_parts(quad1)
        chunks[0] = [quad0, b0, a0, ab0] + core0 + [over_core(ab0)]
        *chunks[0], own[1] = fence(*chunks[0], own[1])
        z2 = z_parts(own[1])
    else:
        chunks = gather_plain(low)
        early_cot, late_cot = swap(cot_send[:256]), swap(cot_send[256:])
    ka = kernel_stem_feed(ids, chunks[0], frames)
    prm = ka.prm
    if fast:
        ka.x1, quad1, a1, b1, *z2 = fence(ka.x1, quad1, a1, b1, *z2)
        ab1 = over_b(a1)
        core1 = [over_core(v) for v in (quad1, b1, a1)]
        quad2 = jnp.stack(z2)
        ab1, quad2, *core1 = fence(ab1, quad2, *core1)
        a2, b2 = ab_parts(quad2)
        chunks[1] = [quad1, b1, a1, ab1] + core1 + [over_core(ab1)]
        *chunks[1], own[2] = fence(*chunks[1], own[2])
        z3 = z_parts(own[2])
    kb = kernel_rest_first(ids, chunks[1], prm, ka.x1)
    if fast:
        kb.sent, quad2, a2, b2, *z3 = fence(kb.sent, quad2, a2, b2, *z3)
        ab2 = over_b(a2)
        core2 = [over_core(v) for v in (quad2, b2, a2)]
        quad3 = jnp.stack(z3)
        ab2, quad3, late_cot, *core2 = fence(ab2, quad3, late_cot, *core2)
        a3, b3 = ab_parts(quad3)
        late_cot = swap(late_cot)
        chunks[2] = [quad2, b2, a2, ab2] + core2 + [over_core(ab2)]
        chunks[2] = list(fence(*chunks[2]))
    kc = kernel_first_second(ids, chunks[2], prm, kb.sent)
    if fast:
        kc.x3, quad3, a3, b3, late_cot = fence(kc.x3, quad3, a3, b3, late_cot)
        chunks[3] = [quad3, b3, a3] + [over_b(a3)]
        chunks[3] += [over_core(v) for v in chunks[3]]
    cot_other = [early_cot, late_cot]
    kd = kernel_turn(ids, chunks[3], prm, kc.x3, cots, cot_other, allowed)
    other_sent = swap(jnp.where(first, kd.sent, kb.sent))
    came = [None] * 6
    near, far, parts = [None] * 6, [None] * 6, [None] * 6

    def begin(n, kernel):
        near[n], far[n] = halves(kernel.keep, over_core(kernel.send))
        came[n] = over_a(far[n])

    def go_on(n):
        near[n], far[n] = halves(near[n], came[n])
        came[n] = over_b(far[n])

    def gather_parts(n):
        parts[n] = quarters(near[n], came[n])

    if fast:
        begin(0, kd)
    ke = kernel_mid(1, ids, chunks[2], FEED // 2, prm, kd.dx3, kc.x2, kc.gated, kc.deep, kc.x1, kc.qkv, kc.ls, kc.mixed)
    if fast:
        came[0], other_sent, ke.send, ke.dx1 = fence(came[0], other_sent, ke.send, ke.dx1)
        go_on(0)
        begin(1, ke)
    kf = kernel_early(1, ids, chunks[2], 0, prm, ke.dx1, kb.sent, kc.hid, None)
    if fast:
        came[0], came[1], kf.send, kf.ig = fence(came[0], came[1], kf.send, kf.ig)
        gather_parts(0)
        go_on(1)
        begin(2, kf)
    kg = kernel_late(
        ids, chunks[1], chunks[3], prm, kb.x4, kb.sent, cots, cot_other, allowed, kf.ig, kb.x3, kb.hid, kd.ghead
    )
    if fast:
        came[1], came[2], kg.send, kg.dx3 = fence(came[1], came[2], kg.send, kg.dx3)
        gather_parts(1)
        go_on(2)
        begin(3, kg)
        sums_a = z_sum([jnp.concatenate([p, q]) for p, q in zip(parts[0], parts[1])])
    kh = kernel_mid(0, ids, chunks[1], 0, prm, kg.dx3, kb.x2, kb.gated, kb.deep, ka.x1, kb.qkv, kb.ls, kb.mixed)
    if fast:
        came[2], came[3], sums_a, kh.send, kh.dx1 = fence(came[2], came[3], sums_a, kh.send, kh.dx1)
        gather_parts(2)
        go_on(3)
        begin(4, kh)
        sum_2 = z_sum(parts[2])
    stem = (ka.pre, ka.wout, frames, [kg.small, kh.small, kd.small, ke.small, kf.small])
    ki = kernel_early(0, ids, chunks[0], FLAT, prm, kh.dx1, ka.x0, ka.hid, stem)
    if fast:
        came[3], came[4], sum_2, ki.send, ki.ig, other_sent = fence(came[3], came[4], sum_2, ki.send, ki.ig, other_sent)
        gather_parts(3)
        go_on(4)
        begin(5, ki)
        sum_3 = z_sum(parts[3])
    ko = kernel_outputs(ids, chunks[3], kb.sent, kd.sent, other_sent, allowed_both, lengths[:, 0])
    if fast:
        came[4], came[5], sum_3, ki.ig, ko.acts, ko.logp = fence(came[4], came[5], sum_3, ki.ig, ko.acts, ko.logp)
        gather_parts(4)
        go_on(5)
        sum_4 = z_sum(parts[4])
        came[5], sum_4, ki.ig = fence(came[5], sum_4, ki.ig)
        gather_parts(5)
        shards = own_shards(sums_a, sum_2, sum_3, sum_4, z_sum(parts[5]), dp, first)
    else:
        shards = reduce_plain([(k.keep, k.send) for k in (kd, ke, kf, kg, kh, ki)])
    other_grad = swap(jnp.where(first, kf.ig, ki.ig).astype(BF))
    input_grads = kernel_grads(ids, ki.ig, kf.ig, other_grad)[None, :, None]
    activations = ko.acts[None, :, None]
    log_probs = ko.logp[None, :, None]
    return (activations, log_probs, input_grads, *shards)


def own_half(both, sec, first):
    mine = lax.dynamic_index_in_dim(both, sec, 0, keepdims=False)
    theirs = over_x(lax.dynamic_index_in_dim(both, 1 - sec, 0, keepdims=False))
    return pick(first, mine, theirs)


def own_pieces(low, sec, dp, first):
    feed_in, feed_out = low[:2]
    stem = pack_stem(low[8], low[9], low[5][0], low[7][0], dp % 4)
    feed_first, feed_second = own_half(pack_feed(feed_in[0, 0], feed_out[0, 0]).reshape(2, FEED // 2, 512), sec, first)
    return jnp.concatenate([stem, feed_first]), feed_second


def own_rest(feed_second, low, sec, first):
    feed_in, feed_out, attend_in, attend_out, conv_in, _, conv_out = low[:7]
    feed = pack_feed(feed_in[0, 1], feed_out[0, 1]).reshape(2, FEED // 2, 512)
    attn = pack_attn(attend_in[0], attend_out[0]).reshape(2, ATTN // 2, 512)
    conv = pack_conv(conv_in[0], conv_out[0]).reshape(2, CONV // 2, 512)
    rest_first, rest_second = own_half(jnp.concatenate([attn, conv, feed], axis=1), sec, first)
    return [
        rest_first,
        jnp.concatenate([feed_second, rest_second[:LATE_ROWS]]),
        jnp.concatenate([rest_second[LATE_ROWS:], low[10].T]),
    ]


def own_shards(sums_a, sum_2, sum_3, sum_4, sum_5, dp, first):
    half = FEED // 2
    head, early_first, stem = sum_3[half:], sum_5[:half], sum_5[half:]

    def join(of_first, of_second):
        own = jnp.where(first, of_first, of_second)
        other = over_x(jnp.where(first, of_second, of_first).astype(BF)).astype(F32)
        return jnp.stack(pick(first, own, other))

    rest = join(jnp.concatenate([sum_3[:half], sum_4]), sums_a)
    late, rest = rest[:, :half].reshape(FEED, 512), rest[:, half:]
    early = join(early_first, sum_2).reshape(FEED, 512)
    attn = rest[:, : ATTN // 2].reshape(ATTN, 512)
    conv = rest[:, ATTN // 2 : LATE_ROWS].reshape(CONV, 512)
    feeds = [early, late]
    g_stem_in, g_stem_out, g_depth, g_gains = unpack_stem(stem, dp % 4)
    return (
        jnp.stack([unpack_in(f, 4) for f in feeds])[None],
        jnp.stack([f[128:] for f in feeds])[None],
        unpack_in(attn, 3)[None],
        attn[96:][None],
        unpack_in(conv, 2)[None],
        g_depth[None],
        conv[64:][None],
        g_gains[None],
        g_stem_in,
        g_stem_out,
        head.T,
    )


def spread_order():
    order = []
    for cr, a, b, zk in pieces():
        px, py = (b, a) if cr else (a, b)
        order.append(px * 16 + zk * 4 + py * 2 + cr)
    return order


def gather_plain(low):
    axes = (2, 2, 1, 1, 1, 2, 1, 2)
    whole = []
    for weight, axis in zip(low[:8], axes):
        axis = 2 if weight.ndim == 4 else axis
        part = lax.all_gather(weight[0], "dp", axis=axis - 1, tiled=True)
        whole.append(lax.all_gather(part, "section", axis=0))
    feed_in, feed_out, attend_in, attend_out, conv_in, depth, conv_out, gains = whole
    stem_in = lax.all_gather(low[8], BOTH, axis=1, tiled=True)
    stem_out = lax.all_gather(low[9], BOTH, axis=0, tiled=True)
    head = lax.all_gather(low[10], BOTH, axis=1, tiled=True)
    order = spread_order()

    def layer(l):
        rows = lambda w, n: w.reshape(16, n, w.shape[-1])
        feeds = [jax.vmap(pack_feed)(rows(feed_in[l, j], 32), rows(feed_out[l, j], 128)) for j in range(2)]
        attn = jax.vmap(pack_attn)(rows(attend_in[l], 32), rows(attend_out[l], 32))
        conv = jax.vmap(pack_conv)(rows(conv_in[l], 32), rows(conv_out[l], 32))
        cut = lambda w: w.reshape(16, 2, w.shape[1] // 2, 512).transpose(1, 0, 2, 3).reshape(32, w.shape[1] // 2, 512)
        return [cut(w) for w in (feeds[0], attn, conv, feeds[1])]

    one, two = layer(0), layer(1)
    columns = lambda w, n: w.reshape(*w.shape[:-1], n, w.shape[-1] // n)
    small = lambda w: jnp.moveaxis(columns(w, 16), 2, 1).reshape(32, w.shape[1], 32)
    stem = jax.vmap(pack_stem)(
        jnp.moveaxis(columns(stem_in, 32), 1, 0),
        stem_out.reshape(32, 8, 512),
        small(depth),
        small(gains),
        jnp.arange(32) % 4,
    )
    head = head.T.reshape(32, 32, 512)
    chunks = ([stem, one[0]], one[1:], [two[0], two[1], two[2]], [two[3], head])
    placed = []
    for parts in chunks:
        joined = jnp.concatenate(parts, axis=1)
        placed.append([jnp.stack([joined[p] for p in order[4 * i : 4 * i + 4]]) for i in range(8)])
    return placed


def reduce_plain(grads):
    order = spread_order()
    place = [order.index(p) for p in range(32)]
    chunks = []
    for keep, send in grads:
        both = jnp.concatenate([keep, send])
        chunks.append(jnp.stack([both[q] for q in place]).astype(F32))
    half = FEED // 2
    whole = []
    for late, mid, early in (chunks[3:], chunks[:3]):
        glue = lambda part, begin, rows: (
            part[:, begin : begin + rows].reshape(2, 16, rows, 512).transpose(1, 0, 2, 3).reshape(16, 2 * rows, 512)
        )
        feeds = [glue(early, 0, half), glue(late, 0, half)]
        attn, conv = glue(mid, 0, ATTN // 2), glue(mid, ATTN // 2, CONV // 2)
        spread = lambda w, n: jax.vmap(lambda rows: unpack_in(rows, n))(w).reshape(512, 512 * n)
        whole.append(
            (
                jnp.stack([spread(f, 4) for f in feeds]),
                jnp.stack([f[:, 128:].reshape(FF, 512) for f in feeds]),
                spread(attn, 3),
                attn[:, 96:].reshape(512, 512),
                spread(conv, 2),
                conv[:, 64:].reshape(512, 512),
            )
        )
    head = chunks[3][:, half:].reshape(1024, 512).T
    g_stem_in, g_stem_out, g_depth, g_gains = jax.vmap(unpack_stem)(chunks[5][:, half:], jnp.arange(32) % 4)
    g_stem_in = jnp.moveaxis(g_stem_in, 0, 1).reshape(640, 256)
    g_stem_out = g_stem_out.reshape(256, 512)
    lanes = lambda w: jnp.moveaxis(w.reshape(2, 16, w.shape[1], 32), 1, 2).reshape(2, w.shape[1], 512)
    g_depth, g_gains = lanes(g_depth), lanes(g_gains)
    stacked = [jnp.stack([whole[0][i], whole[1][i]]) for i in range(6)]

    def shard(value, axis):
        value = lax.psum_scatter(value, "section", scatter_dimension=0, tiled=True)
        return lax.psum_scatter(value, "dp", scatter_dimension=axis, tiled=True)

    return (
        shard(stacked[0], 2),
        shard(stacked[1], 2),
        shard(stacked[2], 1),
        shard(stacked[3], 1),
        shard(stacked[4], 1),
        shard(g_depth, 2),
        shard(stacked[5], 1),
        shard(g_gains, 2),
        lax.psum_scatter(g_stem_in, BOTH, scatter_dimension=1, tiled=True),
        lax.psum_scatter(g_stem_out, BOTH, scatter_dimension=0, tiled=True),
        lax.psum_scatter(head, BOTH, scatter_dimension=1, tiled=True),
    )


def solution(mesh):
    fast = dict(mesh.shape) == {"section": 2, "dp": 16}

    def body(*args):
        return on_device(fast, *args)

    layer_specs = (
        P("section", None, "dp", None),
        P("section", None, "dp", None),
        P("section", "dp", None),
        P("section", "dp", None),
        P("section", "dp", None),
        P("section", None, "dp"),
        P("section", "dp", None),
        P("section", None, "dp"),
        P(None, BOTH),
        P(BOTH, None),
        P(None, BOTH),
    )
    rows = P("section", None, "dp", None, None)
    return jax.shard_map(
        body,
        mesh=mesh,
        in_specs=(P(None, "dp", None, None), P(None, "dp"), P(None, "dp"), P(), rows) + layer_specs,
        out_specs=(rows, rows, rows) + layer_specs,
        check_vma=False,
    )
```

```python
import types

import jax
import jax.numpy as jnp
from jax import lax
from jax.experimental import pallas as pl
from jax.experimental.pallas import tpu as pltpu
from jax.sharding import PartitionSpec as P

D = 512
HEADS = 8
HDIM = 64
FF = 2048
TAPS = 9
EPS = 1e-05
MASKED = -1e30
RB = 512
BOTH = ("section", "dp")
BF = jnp.bfloat16
F32 = jnp.float32

FEED, ATTN, CONV = 256, 128, 96
FLAT = 32
SMALL = 16


def dotn(a, b):
    return lax.dot_general(a, b, (((1,), (0,)), ((), ())), preferred_element_type=F32)


def dotr(a, b):
    return lax.dot_general(a, b, (((1,), (1,)), ((), ())), preferred_element_type=F32)


def dotl(a, b):
    return lax.dot_general(a, b, (((0,), (0,)), ((), ())), preferred_element_type=F32)


def sigmoid(v):
    return 0.5 * jnp.tanh(0.5 * v) + 0.5


def unit_rows(v):
    c = v - jnp.mean(v, axis=-1, keepdims=True)
    r = lax.rsqrt(jnp.mean(c * c, axis=-1, keepdims=True) + EPS)
    return c * r, r


def unit_back(dn, u, r, gain):
    du = dn * gain
    dv = r * (du - jnp.mean(du, axis=-1, keepdims=True) - u * jnp.mean(du * u, axis=-1, keepdims=True))
    return dv, jnp.sum(dn * u, axis=0, keepdims=True)


def row_mask(length, start, rows, columns):
    return (lax.broadcasted_iota(jnp.int32, (rows, columns), 0) + start < length).astype(F32)


def row_loop(body):
    for i in range(512 // RB):
        body(slice(i * RB, i * RB + RB), i * RB)


def piece_of(ids, cr, a, b, zk):
    pc = ids[3] ^ cr
    px = ids[0] ^ (a + pc * (b - a))
    py = ids[2] ^ (b + pc * (a - b))
    pz = ids[1] ^ zk
    return px, pz * 4 + py * 2 + pc


def pieces():
    return [(cr, a, b, zk) for cr in range(2) for a in range(2) for b in range(2) for zk in range(4)]


def start_load(ids, bufs, row, rows, scr, sem, flat=False):
    for cr, a, b, zk in pieces():
        px, d = piece_of(ids, cr, a, b, zk)
        if len(bufs) == 4:
            begin = row + a * (bufs[0].shape[1] // 2)
            src = bufs[cr * 2 + b].at[zk, begin : begin + rows]
        else:
            src = bufs[cr * 4 + a * 2 + b].at[zk, row : row + rows]
        if flat:
            dst = scr.at[px * 16 + d]
        else:
            dst = scr.at[d, pl.ds(pl.multiple_of(px * rows, 16), rows)]
        pltpu.make_async_copy(src, dst, sem).start()


def wait_load(scr, sem):
    pltpu.make_async_copy(scr, scr, sem).wait()


def start_store(ids, scr, keep, send, row, rows, sem, flat=False):
    for cr, a, b, zk in pieces():
        px, d = piece_of(ids, cr, a, b, zk)
        if flat:
            src = scr.at[px * 16 + d]
        else:
            src = scr.at[d, pl.ds(pl.multiple_of(px * rows, 16), rows)]
        dst = (send if cr else keep).at[a * 8 + b * 4 + zk, row : row + rows]
        pltpu.make_async_copy(src, dst, sem).start()


def wait_store(scr, sem):
    pltpu.make_async_copy(scr, scr, sem).wait()


def in_block(w, j):
    return w[:, 32 * j : 32 * j + 32, :].reshape(512, 512)


def out_block(w, j):
    return w[4 * j : 4 * j + 4, 128:256, :].reshape(512, 512)


def feed_fwd(x, w, gain, hid, out):
    def body(rs, start):
        v = x[rs, :].astype(F32)
        u, _ = unit_rows(v)
        n = (u * gain).astype(BF)
        total = jnp.zeros((RB, 512), F32)
        for j in range(4):
            h = dotn(n, in_block(w, j))
            hid[rs, 512 * j : 512 * j + 512] = h.astype(BF)
            total = total + dotn((h * sigmoid(h)).astype(BF), out_block(w, j))
        out[rs, :] = v + 0.5 * total

    row_loop(body)


def feed_bwd(dx, x, hid, w, gain, out, gw, small, row, s):
    def body(rs, start):
        g = dx[rs, :]
        v = x[rs, :].astype(F32)
        u, r = unit_rows(v)
        s.n[rs, :] = (u * gain).astype(BF)
        d = (0.5 * g).astype(BF)
        s.d[rs, :] = d
        dn = jnp.zeros((RB, 512), F32)
        for j in range(4):
            h = hid[rs, 512 * j : 512 * j + 512].astype(F32)
            sg = sigmoid(h)
            s.act[rs, 512 * j : 512 * j + 512] = (h * sg).astype(BF)
            dh = (dotr(d, out_block(w, j)) * (sg * (1.0 + h * (1.0 - sg)))).astype(BF)
            s.dh[rs, 512 * j : 512 * j + 512] = dh
            dn = dn + dotr(dh, in_block(w, j))
        dv, gg = unit_back(dn, u, r, gain)
        out[rs, :] = g + dv
        small[row : row + 1, :] += gg

    row_loop(body)
    for j in range(4):
        cols = slice(512 * j, 512 * j + 512)
        gw[:, 32 * j : 32 * j + 32, :] = dotl(s.n[...], s.dh[:, cols]).astype(BF).reshape(16, 32, 512)
        gw[4 * j : 4 * j + 4, 128:256, :] = dotl(s.act[:, cols], s.d[...]).astype(BF).reshape(4, 128, 512)


def lanes_of(half, axis=1, count=1):
    shape = (count, 128) if axis else (128, count)
    return (lax.broadcasted_iota(jnp.int32, shape, axis) + 64 * half) % 128 - 64


def attn_fwd(x, w, gain, length, qkv, ls, mixt, out):
    def project(rs, start):
        u, _ = unit_rows(x[rs, :])
        n = (u * gain).astype(BF)
        for j in range(3):
            qkv[rs, 512 * j : 512 * j + 512] = dotn(n, in_block(w, j)).astype(BF)

    row_loop(project)

    for hp in range(4):
        at = hp * 128
        k = qkv[:, pl.ds(512 + at, 128)].astype(F32)
        vt = qkv[:, pl.ds(1024 + at, 128)].astype(F32).T
        outside = jnp.where(lax.broadcasted_iota(jnp.int32, (512, 128), 0) < length, 0.0, MASKED)
        kx, vx = [], []
        for hh in range(2):
            free = lanes_of(hh)
            kx.append(jnp.where(free < 0, k, jnp.where(free == 0, outside, 0.0)).astype(BF))
            free = lanes_of(hh, 0, 512)
            vx.append(jnp.where(free < 0, vt, jnp.where(free == 0, 1.0, 0.0)).astype(BF))

        def body(rs, start):
            q = qkv[rs, pl.ds(at, 128)].astype(F32) * HDIM**-0.5
            parts = []
            for hh in range(2):
                free = lanes_of(hh)
                qx = jnp.where(free < 0, q, jnp.where(free == 0, 1.0, 0.0)).astype(BF)
                sc = dotr(kx[hh], qx)
                top = jnp.max(sc, axis=0, keepdims=True)
                both = dotn(vx[hh], jnp.exp(sc - top).astype(BF))
                tot = both[64 * (1 - hh) : 64 * (1 - hh) + 1, :]
                parts.append(both * (1.0 / tot))
                ls[pl.ds(hp * 2 + hh, 1), rs] = top + jnp.log(tot)
            mixt[pl.ds(at, 128), rs] = jnp.where(lanes_of(0, 0, RB) < 0, parts[0], parts[1]).astype(BF)

        row_loop(body)

    def project_out(rs, start):
        out[rs, :] = x[rs, :] + dotl(mixt[:, rs], w[:, 96:128, :].reshape(512, 512))

    row_loop(project_out)


def attn_bwd(dx, x, qkv, ls, mixt, w, gain, length, out, gw, small, row, s):
    def first(rs, start):
        u, _ = unit_rows(x[rs, :])
        s.n[rs, :] = (u * gain).astype(BF)
        d = dx[rs, :].astype(BF)
        s.d[rs, :] = d
        s.dm[:, rs] = dotr(w[:, 96:128, :].reshape(512, 512), d).astype(BF)

    row_loop(first)
    gw[:, 96:128, :] = dotn(mixt[...], s.d[...]).astype(BF).reshape(16, 32, 512)

    for hp in range(4):
        at = hp * 128
        s.dq[...] = jnp.zeros((128, 512), F32)
        q = qkv[:, pl.ds(at, 128)].astype(F32) * HDIM**-0.5
        kt = qkv[:, pl.ds(512 + at, 128)].astype(F32).T * HDIM**-0.5
        dmt = s.dm[pl.ds(at, 128), :].astype(F32)
        prod = dmt * mixt[pl.ds(at, 128), :].astype(F32)
        qx, qs, dms, deltas, sums = [], [], [], [], []
        for hh in range(2):
            free = lanes_of(hh)
            qs.append(jnp.where(free < 0, q, 0.0).astype(BF))
            qx.append(jnp.where(free < 0, q, jnp.where(free == 0, 1.0, 0.0)).astype(BF))
            free = lanes_of(hh, 0, 512)
            dms.append(jnp.where(free < 0, dmt, 0.0).astype(BF))
            deltas.append(jnp.sum(prod[64 * hh : 64 * hh + 64, :], axis=0, keepdims=True))
            s.kt[128 * hh : 128 * hh + 128, :] = jnp.where(free < 0, kt, 0.0).astype(BF)
            sums.append(ls[pl.ds(hp * 2 + hh, 1), :])

        def body(rs, start):
            k = qkv[rs, pl.ds(512 + at, 128)].astype(F32)
            v = qkv[rs, pl.ds(1024 + at, 128)]
            outside = jnp.where(lax.broadcasted_iota(jnp.int32, (RB, 128), 0) + start < length, 0.0, MASKED)
            dk = jnp.zeros((RB, 128), F32)
            dv = jnp.zeros((RB, 128), F32)
            for hh in range(2):
                free = lanes_of(hh)
                kx = jnp.where(free < 0, k, jnp.where(free == 0, outside, 0.0)).astype(BF)
                p = jnp.exp(dotr(kx, qx[hh]) - sums[hh])
                ds = (p * (dotn(v, dms[hh]) - deltas[hh])).astype(BF)
                dv = dv + dotr(p.astype(BF), dms[hh])
                dk = dk + dotn(ds, qs[hh])
                s.dq[...] += dotn(s.kt[128 * hh : 128 * hh + 128, rs], ds)
            s.dpk[rs, pl.ds(512 + at, 128)] = dk.astype(BF)
            s.dpk[rs, pl.ds(1024 + at, 128)] = dv.astype(BF)

        row_loop(body)
        s.dpk[:, pl.ds(at, 128)] = s.dq[...].T.astype(BF)

    def last(rs, start):
        u, r = unit_rows(x[rs, :])
        dn = jnp.zeros((RB, 512), F32)
        for j in range(3):
            dn = dn + dotr(s.dpk[rs, 512 * j : 512 * j + 512], in_block(w, j))
        dv, gg = unit_back(dn, u, r, gain)
        out[rs, :] = dx[rs, :] + dv
        small[row : row + 1, :] += gg

    row_loop(last)
    for j in range(3):
        gw[:, 32 * j : 32 * j + 32, :] = (
            dotl(s.n[...], s.dpk[:, 512 * j : 512 * j + 512]).astype(BF).reshape(16, 32, 512)
        )


PAD = 8


def conv_fwd(x, w, prm, length, gated, deep, out, pad):
    pad[0:PAD, :] = jnp.zeros((PAD, 512), F32)
    pad[PAD + 512 : 2 * PAD + 512, :] = jnp.zeros((PAD, 512), F32)

    def first(rs, start):
        u, _ = unit_rows(x[rs, :])
        n = (u * prm[TAPS + 2 : TAPS + 3, :]).astype(BF)
        a = dotn(n, in_block(w, 0))
        b = dotn(n, in_block(w, 1))
        gated[rs, 0:512] = a
        gated[rs, 512:1024] = b
        pad[pl.ds(start + PAD, RB), :] = a * sigmoid(b) * row_mask(length, start, RB, 512)

    row_loop(first)
    for i in range(512 // RB):
        total = jnp.zeros((RB, 512), F32)
        for t in range(TAPS):
            begin = i * RB + PAD - TAPS // 2 + t
            total = total + prm[t : t + 1, :] * pad[begin : begin + RB, :]
        deep[i * RB : i * RB + RB, :] = total

    def last(rs, start):
        u, _ = unit_rows(deep[rs, :])
        m = u * prm[TAPS + 3 : TAPS + 4, :]
        act = (m * sigmoid(m)).astype(BF)
        out[rs, :] = x[rs, :] + dotn(act, w[:, 64:96, :].reshape(512, 512))

    row_loop(last)


def conv_bwd(dx, x, gated, deep, w, prm, length, out, gw, small, s):
    s.back[0:PAD, :] = jnp.zeros((PAD, 512), F32)
    s.back[PAD + 512 : 2 * PAD + 512, :] = jnp.zeros((PAD, 512), F32)
    gain_in = prm[TAPS + 2 : TAPS + 3, :]
    gain_mid = prm[TAPS + 3 : TAPS + 4, :]

    def first(rs, start):
        padded = pl.ds(start + PAD, RB)
        d = dx[rs, :].astype(BF)
        s.d[rs, :] = d
        u3, r3 = unit_rows(deep[rs, :])
        m = u3 * gain_mid
        sg = sigmoid(m)
        s.act[rs, :] = (m * sg).astype(BF)
        dmid = dotr(d, w[:, 64:96, :].reshape(512, 512)) * (sg * (1.0 + m * (1.0 - sg)))
        ddeep, gg = unit_back(dmid, u3, r3, gain_mid)
        s.back[padded, :] = ddeep
        small[TAPS + 3 : TAPS + 4, :] += gg
        s.glu[rs, :] = (
            gated[rs, 0:512] * sigmoid(gated[rs, 512:1024]) * row_mask(length, start, RB, 512)
        )

    row_loop(first)
    gw[:, 64:96, :] = dotl(s.act[...], s.d[...]).astype(BF).reshape(16, 32, 512)
    for i in range(512 // RB):
        rows = slice(i * RB, i * RB + RB)
        glu = s.glu[rows, :]
        dglu = jnp.zeros((RB, 512), F32)
        for t in range(TAPS):
            begin = i * RB + PAD + TAPS // 2 - t
            later = s.back[begin : begin + RB, :]
            small[t : t + 1, :] += jnp.sum(glu * later, axis=0, keepdims=True)
            dglu = dglu + prm[t : t + 1, :] * later
        dglu = dglu * row_mask(length, i * RB, RB, 512)
        sg = sigmoid(gated[rows, 512:1024])
        ga = dglu * sg
        s.dga[rows, :] = ga.astype(BF)
        s.dgb[rows, :] = (ga * gated[rows, 0:512] * (1.0 - sg)).astype(BF)

    def last(rs, start):
        u, r = unit_rows(x[rs, :])
        s.n[rs, :] = (u * gain_in).astype(BF)
        dn = dotr(s.dga[rs, :], in_block(w, 0)) + dotr(s.dgb[rs, :], in_block(w, 1))
        dv, gg = unit_back(dn, u, r, gain_in)
        out[rs, :] = dx[rs, :] + dv
        small[TAPS + 2 : TAPS + 3, :] += gg

    row_loop(last)
    gw[:, 0:32, :] = dotl(s.n[...], s.dga[...]).astype(BF).reshape(16, 32, 512)
    gw[:, 32:64, :] = dotl(s.n[...], s.dgb[...]).astype(BF).reshape(16, 32, 512)


def finish_fwd(x4, prm, length, sent):
    def body(rs, start):
        u, _ = unit_rows(x4[rs, :])
        sent[rs, :] = (u * prm[TAPS + 5 : TAPS + 6, :] * row_mask(length, start, RB, 512)).astype(BF)

    row_loop(body)


def head_rows(sent, w, permit):
    logits = dotr(sent, w)
    top = jnp.max(jnp.where(permit, logits, MASKED), axis=-1, keepdims=True)
    e = jnp.exp(jnp.where(permit, logits - top, MASKED))
    return logits, top + jnp.log(jnp.sum(e, axis=-1, keepdims=True))


def head_bwd(x4, sent, w, allowed, cot, prm, length, extra, out, gl, small):
    permit = allowed[...] > 0
    gain = prm[TAPS + 5 : TAPS + 6, :]

    def body(rs, start):
        hw = w[...].reshape(1024, 512)
        logits, logsum = head_rows(sent[rs, :], hw, permit)
        weighted = jnp.where(permit, cot[rs, :].astype(F32), 0.0) * row_mask(length, start, RB, 1024)
        probs = jnp.exp(jnp.where(permit, logits - logsum, MASKED))
        g = (weighted - probs * jnp.sum(weighted, axis=-1, keepdims=True)).astype(BF)
        gl[rs, :] = g
        gs = dotn(g, hw)
        if extra is not None:
            gs = gs + extra[rs, :].astype(BF).astype(F32)
        u, r = unit_rows(x4[rs, :])
        dv, gg = unit_back(gs * row_mask(length, start, RB, 512), u, r, gain)
        out[rs, :] = dv
        small[TAPS + 5 : TAPS + 6, :] += gg

    row_loop(body)


ANY, VMEM, SMEM = pl.ANY, pltpu.VMEM, pltpu.SMEM
LATE = object()


class Late:
    def __init__(self, source, held, sem):
        self.copy, self.held, self.going, self.here = pltpu.make_async_copy(source, held, sem), held, False, False

    def go(self):
        self.going = True
        self.copy.start()

    def get(self):
        if not self.going:
            self.go()
        if not self.here:
            self.copy.wait()
        self.here = True
        return self.held


class Soon:
    def __init__(self, held, target, sem):
        self.copy, self.held, self.going = pltpu.make_async_copy(held, target, sem), held, False

    def go(self):
        self.going = True
        self.copy.start()

    def end(self):
        if not self.going:
            self.go()
        self.copy.wait()


def run(body, micros, ins, outs, scratch):
    flat, held = [], []
    for value, space in ins.values():
        flat += [(array, ANY if space is LATE else space) for array in (value if isinstance(value, list) else [value])]
        if space is LATE:
            held.append((value.shape, value.dtype))
    held += [(shape, dtype) for shape, dtype, space in outs.values() if space is LATE]

    def kernel(*refs):
        left = list(refs)
        ns = types.SimpleNamespace()
        waiting, soon = [], []
        for key, (value, space) in ins.items():
            if isinstance(value, list):
                setattr(ns, key, [left.pop(0) for _ in value])
            else:
                setattr(ns, key, left.pop(0))
        for key in [*outs, *scratch]:
            setattr(ns, key, left.pop(0))
        ns.sems = left.pop()
        number = 8
        for key, (_, space) in ins.items():
            if space is LATE:
                setattr(ns, key, Late(getattr(ns, key), left.pop(0), ns.sems.at[number]))
                number += 1
        for key, (_, _, space) in outs.items():
            if space is LATE:
                soon.append(Soon(left.pop(0), getattr(ns, key), ns.sems.at[number]))
                setattr(ns, key, soon[-1])
                number += 1
        body(ns)
        for result in soon:
            result.end()

    result = pl.pallas_call(
        kernel,
        out_shape=[jax.ShapeDtypeStruct(shape, dtype) for shape, dtype, _ in outs.values()],
        in_specs=[pl.BlockSpec(memory_space=space) for _, space in flat],
        out_specs=[pl.BlockSpec(memory_space=ANY if space is LATE else space) for _, _, space in outs.values()],
        scratch_shapes=[pltpu.VMEM(shape, dtype) for shape, dtype in [*scratch.values(), *held]]
        + [pltpu.SemaphoreType.DMA((8 + len(held),))],
        compiler_params=pltpu.CompilerParams(vmem_limit_bytes=55 * 2**20),
        cost_estimate=pl.CostEstimate(flops=int(micros * 1.1e9), bytes_accessed=2**20, transcendentals=0),
        name=body.__name__,
    )(*[array for array, _ in flat])
    return types.SimpleNamespace(**dict(zip(outs, result)))


ROWS = (512, 512)
WF, WA, WC, WH = ((16, FEED, 512), BF), ((16, ATTN, 512), BF), ((16, CONV, 512), BF), ((32, FLAT, 512), BF)
PADDED = ((512 + 2 * PAD, 512), F32)
LATE_ROWS = ATTN // 2 + CONV // 2


def gain_of(prm, number):
    return prm[TAPS + number : TAPS + number + 1, :]


def kernel_stem_feed(ids, bufs, frames):
    def stem_feed(k):
        start_load(k.ids, k.bufs, 0, FLAT, k.stem, k.sems.at[0], flat=True)
        k.frames.go()
        start_load(k.ids, k.bufs, FLAT, FEED // 2, k.w, k.sems.at[1])
        wait_load(k.stem, k.sems.at[0])
        stem = k.stem[...].astype(F32)
        for layer in range(2):
            for z in range(4):
                part = jnp.zeros((8, 512), F32)
                for q in range(4):
                    part = part + stem[layer * 16 + z * 4 + q, 24:32, :]
                k.prm[layer, 0:8, 128 * z : 128 * z + 128] = part[:, 0:128]
                k.prm[layer, 8:16, 128 * z : 128 * z + 128] = part[:, 128:256]
        win_a = stem[:, 0:8, :].reshape(256, 512).astype(BF)
        win_b = stem[:, 8:16, 0:128].reshape(256, 128).astype(BF)
        k.wout[...] = stem[:, 16:24, :].reshape(256, 512).astype(BF)
        frames, x0, x1, hid, pre = k.frames.get(), k.x0.held, k.x1.held, k.hid.held, k.pre.held

        def rows(rs, start):
            p = dotr(frames[rs, 0:512], win_a) + dotr(frames[rs, 512:640], win_b)
            pre[rs, :] = p
            x = dotn((p * sigmoid(p)).astype(BF), k.wout[...])
            x0[rs, :] = (x * row_mask(k.ids[4], start, RB, 512)).astype(BF)

        row_loop(rows)
        k.pre.go()
        k.x0.go()
        wait_load(k.w, k.sems.at[1])
        feed_fwd(x0, k.w, gain_of(k.prm.at[0], 0), hid, x1)

    return run(
        stem_feed,
        9,
        dict(ids=(ids, SMEM), bufs=(bufs, ANY), frames=(frames, LATE)),
        dict(
            prm=((2, SMALL, 512), F32, VMEM),
            pre=((512, 256), F32, LATE),
            wout=((256, 512), BF, VMEM),
            x0=(ROWS, BF, LATE),
            hid=((512, FF), BF, LATE),
            x1=(ROWS, F32, LATE),
        ),
        dict(stem=WH, w=WF),
    )


ATTN_OUTS = dict(qkv=((512, 1536), BF, LATE), ls=((8, 512), F32, VMEM), mixed=(ROWS, BF, LATE), x2=(ROWS, F32, LATE))
CONV_OUTS = dict(gated=((512, 1024), F32, LATE), deep=(ROWS, F32, LATE), x3=(ROWS, F32, LATE))


def attn_conv(k, x1, prm):
    wait_load(k.wa, k.sems.at[0])
    attn_fwd(x1, k.wa, gain_of(prm, 1), k.ids[4], k.qkv.held, k.ls, k.mixed.held, k.x2.held)
    for result in (k.qkv, k.mixed, k.x2):
        result.go()
    wait_load(k.wc, k.sems.at[1])
    conv_fwd(k.x2.held, k.wc, prm, k.ids[4], k.gated.held, k.deep.held, k.x3.held, k.pad)
    for result in (k.gated, k.deep, k.x3):
        result.go()


def kernel_rest_first(ids, bufs, prm, x1):
    def rest_first(k):
        k.x1.go()
        start_load(k.ids, k.bufs, 0, ATTN // 2, k.wa, k.sems.at[0])
        start_load(k.ids, k.bufs, ATTN // 2, CONV // 2, k.wc, k.sems.at[1])
        start_load(k.ids, k.bufs, LATE_ROWS, FEED // 2, k.wf, k.sems.at[2])
        prm = k.prm.at[0]
        attn_conv(k, k.x1.get(), prm)
        wait_load(k.wf, k.sems.at[2])
        feed_fwd(k.x3.held, k.wf, gain_of(prm, 4), k.hid.held, k.x4.held)
        k.hid.go()
        k.x4.go()
        finish_fwd(k.x4.held, prm, k.ids[4], k.sent)

    return run(
        rest_first,
        20,
        dict(ids=(ids, SMEM), bufs=(bufs, ANY), prm=(prm, VMEM), x1=(x1, LATE)),
        ATTN_OUTS | CONV_OUTS | dict(hid=((512, FF), BF, LATE), x4=(ROWS, F32, LATE), sent=(ROWS, BF, VMEM)),
        dict(wa=WA, wc=WC, wf=WF, pad=PADDED),
    )


def kernel_first_second(ids, bufs, prm, x0):
    def first_second(k):
        start_load(k.ids, k.bufs, 0, FEED // 2, k.wf, k.sems.at[2])
        start_load(k.ids, k.bufs, FEED // 2, ATTN // 2, k.wa, k.sems.at[0])
        start_load(k.ids, k.bufs, FEED // 2 + ATTN // 2, CONV // 2, k.wc, k.sems.at[1])
        prm = k.prm.at[1]
        wait_load(k.wf, k.sems.at[2])
        feed_fwd(k.x0, k.wf, gain_of(prm, 0), k.hid.held, k.x1.held)
        k.hid.go()
        k.x1.go()
        attn_conv(k, k.x1.held, prm)

    return run(
        first_second,
        20,
        dict(ids=(ids, SMEM), bufs=(bufs, ANY), prm=(prm, VMEM), x0=(x0, VMEM)),
        dict(hid=((512, FF), BF, LATE), x1=(ROWS, F32, LATE)) | ATTN_OUTS | CONV_OUTS,
        dict(wa=WA, wc=WC, wf=WF, pad=PADDED),
    )


def start_cot(k, layer):
    @pl.when(k.ids[5] == layer)
    def _():
        pltpu.make_async_copy(k.cots.at[k.ids[5]], k.cot, k.sems.at[2]).start()

    @pl.when(k.ids[5] != layer)
    def _():
        at = 0
        for part in k.cot_other:
            pltpu.make_async_copy(part, k.cot.at[at : at + part.shape[0]], k.sems.at[2]).start()
            at += part.shape[0]


FEED_SCRATCH = dict(n=(ROWS, BF), d=(ROWS, BF), act=((512, FF), BF), dh=((512, FF), BF), wf=WF, gf=WF)
HEAD_SCRATCH = dict(wh=WH, cot=((512, 1024), BF), gl=((512, 1024), BF), dx4=(ROWS, F32))


def kernel_turn(ids, bufs, prm, x3, cots, cot_other, allowed):
    def turn(k):
        k.x3.go()
        start_load(k.ids, k.bufs, 0, FEED // 2, k.wf, k.sems.at[0])
        start_load(k.ids, k.bufs, FEED // 2, FLAT, k.wh, k.sems.at[1], flat=True)
        start_cot(k, 1)
        prm = k.prm.at[1]
        k.small[...] = jnp.zeros((SMALL, 512), F32)
        x3 = k.x3.get()
        wait_load(k.wf, k.sems.at[0])
        feed_fwd(x3, k.wf, gain_of(prm, 4), k.hid, k.x4)
        finish_fwd(k.x4, prm, k.ids[4], k.sent)
        wait_load(k.wh, k.sems.at[1])
        wait_load(k.cot, k.sems.at[2])
        head_bwd(k.x4, k.sent, k.wh, k.allowed, k.cot, prm, k.ids[4], None, k.dx4, k.gl, k.small)
        k.ghead.held[...] = dotl(k.gl[...], k.sent[...])
        k.ghead.go()
        feed_bwd(k.dx4, x3, k.hid, k.wf, gain_of(prm, 4), k.dx3.held, k.gf, k.small, TAPS + 4, k)
        start_store(k.ids, k.gf, k.keep, k.send, 0, FEED // 2, k.sems.at[3])
        wait_store(k.gf, k.sems.at[3])

    rows = FEED // 2
    return run(
        turn,
        22,
        dict(
            ids=(ids, SMEM),
            bufs=(bufs, ANY),
            prm=(prm, VMEM),
            x3=(x3, LATE),
            cots=(cots, ANY),
            cot_other=(cot_other, ANY),
            allowed=(allowed, VMEM),
        ),
        dict(
            sent=(ROWS, BF, VMEM),
            ghead=((1024, 512), F32, LATE),
            dx3=(ROWS, F32, LATE),
            small=((SMALL, 512), F32, VMEM),
            keep=((16, rows, 512), BF, ANY),
            send=((16, rows, 512), BF, ANY),
        ),
        FEED_SCRATCH | HEAD_SCRATCH | dict(hid=((512, FF), BF), x4=(ROWS, F32)),
    )


def kernel_late(ids, bufs, head_bufs, prm, x4, sent, cots, cot_other, allowed, ig, x3, hid, ghead):
    def late(k):
        start_load(k.ids, k.hbufs, FEED // 2, FLAT, k.wh, k.sems.at[1], flat=True)
        start_cot(k, 0)
        k.x4.go()
        k.ig.go()
        start_load(k.ids, k.bufs, LATE_ROWS, FEED // 2, k.wf, k.sems.at[0])
        for operand in (k.ghead, k.x3, k.hid):
            operand.go()
        prm = k.prm.at[0]
        k.small[...] = jnp.zeros((SMALL, 512), F32)
        wait_load(k.wh, k.sems.at[1])
        wait_load(k.cot, k.sems.at[2])
        head_bwd(k.x4.get(), k.sent, k.wh, k.allowed, k.cot, prm, k.ids[4], k.ig.get(), k.dx4, k.gl, k.small)
        k.gh[...] = (k.ghead.get()[...] + dotl(k.gl[...], k.sent[...])).astype(BF).reshape(32, FLAT, 512)
        start_store(k.ids, k.gh, k.keep, k.send, FEED // 2, FLAT, k.sems.at[4], flat=True)
        wait_load(k.wf, k.sems.at[0])
        feed_bwd(k.dx4, k.x3.get(), k.hid.get(), k.wf, gain_of(prm, 4), k.dx3.held, k.gf, k.small, TAPS + 4, k)
        start_store(k.ids, k.gf, k.keep, k.send, 0, FEED // 2, k.sems.at[3])
        wait_store(k.gh, k.sems.at[4])
        wait_store(k.gf, k.sems.at[3])

    rows = FEED // 2 + FLAT
    return run(
        late,
        17,
        dict(
            ids=(ids, SMEM),
            bufs=(bufs, ANY),
            hbufs=(head_bufs, ANY),
            prm=(prm, VMEM),
            x4=(x4, LATE),
            sent=(sent, VMEM),
            cots=(cots, ANY),
            cot_other=(cot_other, ANY),
            allowed=(allowed, VMEM),
            ig=(ig, LATE),
            x3=(x3, LATE),
            hid=(hid, LATE),
            ghead=(ghead, LATE),
        ),
        dict(
            dx3=(ROWS, F32, LATE),
            small=((SMALL, 512), F32, VMEM),
            keep=((16, rows, 512), BF, ANY),
            send=((16, rows, 512), BF, ANY),
        ),
        FEED_SCRATCH | HEAD_SCRATCH | dict(gh=WH),
    )


def kernel_mid(layer, ids, bufs, row, prm, dx3, x2, gated, deep, x1, qkv, ls, mixed):
    def mid(k):
        for operand in (k.dx3, k.deep):
            operand.go()
        start_load(k.ids, k.bufs, row + ATTN // 2, CONV // 2, k.wc, k.sems.at[1])
        for operand in (k.gated, k.x2):
            operand.go()
        start_load(k.ids, k.bufs, row, ATTN // 2, k.wa, k.sems.at[0])
        for operand in (k.x1, k.mixed, k.qkv):
            operand.go()
        prm = k.prm.at[layer]
        k.small[...] = jnp.zeros((SMALL, 512), F32)
        wait_load(k.wc, k.sems.at[1])
        s = types.SimpleNamespace(
            n=k.n, d=k.d, act=k.act.at[:, 0:512], dga=k.dh.at[:, 0:512], dgb=k.dh.at[:, 512:1024], glu=k.glu, back=k.back
        )
        conv_bwd(k.dx3.get(), k.x2.get(), k.gated.get(), k.deep.get(), k.wc, prm, k.ids[4], k.dx2, k.gc, k.small, s)
        start_store(k.ids, k.gc, k.keep, k.send, ATTN // 2, CONV // 2, k.sems.at[3])
        wait_load(k.wa, k.sems.at[0])
        s = types.SimpleNamespace(n=k.n, d=k.d, dm=k.dm, dpk=k.act, dq=k.dq, kt=k.kt)
        attn_bwd(
            k.dx2, k.x1.get(), k.qkv.get(), k.ls, k.mixed.get(), k.wa, gain_of(prm, 1), k.ids[4], k.dx1.held, k.ga,
            k.small, TAPS + 1, s,
        )
        start_store(k.ids, k.ga, k.keep, k.send, 0, ATTN // 2, k.sems.at[2])
        wait_store(k.gc, k.sems.at[3])
        wait_store(k.ga, k.sems.at[2])

    return run(
        mid,
        21,
        dict(
            ids=(ids, SMEM),
            bufs=(bufs, ANY),
            prm=(prm, VMEM),
            dx3=(dx3, LATE),
            x2=(x2, LATE),
            gated=(gated, LATE),
            deep=(deep, LATE),
            x1=(x1, LATE),
            qkv=(qkv, LATE),
            ls=(ls, VMEM),
            mixed=(mixed, LATE),
        ),
        dict(
            dx1=(ROWS, F32, LATE),
            small=((SMALL, 512), F32, VMEM),
            keep=((16, LATE_ROWS, 512), BF, ANY),
            send=((16, LATE_ROWS, 512), BF, ANY),
        ),
        dict(
            wa=WA,
            wc=WC,
            ga=WA,
            gc=WC,
            dx2=(ROWS, F32),
            n=(ROWS, BF),
            d=(ROWS, BF),
            dm=(ROWS, BF),
            act=((512, 1536), BF),
            dh=((512, 1024), BF),
            glu=(ROWS, F32),
            back=PADDED,
            dq=((128, 512), F32),
            kt=((256, 512), BF),
        ),
    )


def kernel_early(layer, ids, bufs, row, prm, dx1, x0, hid, stem):
    def early(k):
        k.dx1.go()
        k.x0.go()
        start_load(k.ids, k.bufs, row, FEED // 2, k.wf, k.sems.at[1])
        k.hid.go()
        if stem is not None:
            k.pre.go()
            k.frames.go()
        prm = k.prm.at[layer]
        k.small[...] = jnp.zeros((SMALL, 512), F32)
        wait_load(k.wf, k.sems.at[1])
        ig = k.ig.held
        feed_bwd(k.dx1.get(), k.x0.get(), k.hid.get(), k.wf, gain_of(prm, 0), ig, k.gf, k.small, TAPS, k)
        k.ig.go()
        start_store(k.ids, k.gf, k.keep, k.send, 0, FEED // 2, k.sems.at[3])
        if stem is not None:
            pre, frames = k.pre.get(), k.frames.get()

            def rows(rs, start):
                d = (ig[rs, :] * row_mask(k.ids[4], start, RB, 512)).astype(BF)
                k.d[rs, :] = d
                p = pre[rs, :]
                sg = sigmoid(p)
                k.n[rs, 0:256] = (p * sg).astype(BF)
                k.n[rs, 256:512] = (dotr(d, k.wout[...]) * (sg * (1.0 + p * (1.0 - sg)))).astype(BF)

            row_loop(rows)
            k.gs[:, 0:8, :] = dotl(k.n[:, 256:512], frames[:, 0:512]).reshape(32, 8, 512)
            k.gs[:, 8:16, 0:128] = dotl(k.n[:, 256:512], frames[:, 512:640]).reshape(32, 8, 128)
            k.gs[:, 8:16, 128:512] = jnp.zeros((32, 8, 384), F32)
            k.gs[:, 16:24, :] = dotl(k.n[:, 0:256], k.d[...]).reshape(32, 8, 512)
            first, second = k.small[...], jnp.zeros((SMALL, 512), F32)
            for part in k.smalls[:2]:
                first = first + part[...]
            for part in k.smalls[2:]:
                second = second + part[...]
            for number, total in enumerate((first, second)):
                for z in range(4):
                    lanes = slice(128 * z, 128 * z + 128)
                    block = jnp.concatenate([total[0:8, lanes], total[8:16, lanes], jnp.zeros((8, 256), F32)], axis=1)
                    for q in range(4):
                        k.gs[number * 16 + z * 4 + q, 24:32, :] = block
            k.gsb[...] = k.gs[...].astype(BF)
            start_store(k.ids, k.gsb, k.keep, k.send, FEED // 2, FLAT, k.sems.at[4], flat=True)
            wait_store(k.gsb, k.sems.at[4])
        wait_store(k.gf, k.sems.at[3])

    rows = FEED // 2 + (0 if stem is None else FLAT)
    ins = dict(
        ids=(ids, SMEM),
        bufs=(bufs, ANY),
        prm=(prm, VMEM),
        dx1=(dx1, LATE),
        x0=(x0, LATE),
        hid=(hid, LATE),
    )
    scratch = dict(FEED_SCRATCH)
    if stem is not None:
        pre, wout, frames, smalls = stem
        ins |= dict(pre=(pre, LATE), wout=(wout, VMEM), frames=(frames, LATE), smalls=(smalls, VMEM))
        scratch |= dict(gs=((32, FLAT, 512), F32), gsb=WH)
    return run(
        early,
        13 if stem is not None else 10,
        ins,
        dict(
            ig=(ROWS, F32, LATE),
            small=((SMALL, 512), F32, VMEM),
            keep=((16, rows, 512), BF, ANY),
            send=((16, rows, 512), BF, ANY),
        ),
        scratch,
    )


def kernel_outputs(ids, head_bufs, sent_first, sent_second, other, allowed, lengths):
    def outputs(k):
        start_load(k.ids, k.hbufs, FEED // 2, FLAT, k.wh, k.sems.at[0], flat=True)
        for sec in range(2):

            @pl.when(k.ids[5] == sec)
            def _():
                pltpu.make_async_copy(k.second if sec else k.first, k.sent.at[sec], k.sems.at[1]).start()
                pltpu.make_async_copy(k.other, k.sent.at[1 - sec], k.sems.at[1]).start()

        wait_load(k.sent, k.sems.at[1])
        wait_load(k.wh, k.sems.at[0])
        for batch in range(2):
            permit = k.allowed[batch : batch + 1, :] > 0
            sent = k.sent[batch]
            logits, logsum = head_rows(sent, k.wh[...].reshape(1024, 512), permit)
            ok = row_mask(k.lengths[batch], 0, 512, 1024)
            k.logp.held[batch] = jnp.where(permit, logits - logsum, 0.0) * ok
            k.acts.held[batch] = sent.astype(F32)

    return run(
        outputs,
        9,
        dict(
            ids=(ids, SMEM),
            lengths=(lengths, SMEM),
            hbufs=(head_bufs, ANY),
            first=(sent_first, ANY),
            second=(sent_second, ANY),
            other=(other, ANY),
            allowed=(allowed, VMEM),
        ),
        dict(logp=((2, 512, 1024), F32, LATE), acts=((2, 512, 512), F32, LATE)),
        dict(wh=WH, sent=((2, 512, 512), BF)),
    )


def kernel_grads(ids, first, second, other):
    def grads(k):
        sec = k.ids[5]
        k.out.held[1 - sec] = k.other[...].astype(F32)

        @pl.when(sec == 0)
        def _():
            k.out.held[0] = k.first[...]

        @pl.when(sec != 0)
        def _():
            k.out.held[1] = k.second[...]

    return run(
        grads,
        3,
        dict(ids=(ids, SMEM), first=(first, VMEM), second=(second, VMEM), other=(other, VMEM)),
        dict(out=((2, 512, 512), F32, LATE)),
        dict(),
    ).out


def pack_feed(w_in, w_out):
    return jnp.concatenate([w_in.reshape(32, 4, 512).transpose(1, 0, 2).reshape(128, 512), w_out])


def pack_attn(w_in, w_out):
    return jnp.concatenate([w_in.reshape(32, 3, 512).transpose(1, 0, 2).reshape(96, 512), w_out])


def pack_conv(w_in, w_out):
    return jnp.concatenate([w_in.reshape(32, 2, 512).transpose(1, 0, 2).reshape(64, 512), w_out])


def unpack_in(rows, blocks):
    return rows[: 32 * blocks].reshape(blocks, 32, 512).transpose(1, 0, 2).reshape(32, 512 * blocks)


def pack_stem(stem_in, stem_out, depth, gains, quarter):
    turned = stem_in.T
    small = jnp.concatenate([depth, gains, jnp.zeros((1, 32), depth.dtype)])
    spread = lax.dynamic_update_slice(jnp.zeros((16, 128), depth.dtype), small, (0, 32 * quarter))
    return jnp.concatenate(
        [
            turned[:, :512],
            jnp.pad(turned[:, 512:], ((0, 0), (0, 384))),
            stem_out,
            jnp.concatenate([spread[:8], spread[8:], jnp.zeros((8, 256), depth.dtype)], axis=1),
        ]
    )


def unpack_stem(rows, quarter):
    turned = jnp.concatenate([rows[0:8], rows[8:16, :128]], axis=1)
    spread = jnp.concatenate([rows[24:32, 0:128], rows[24:32, 128:256]])
    small = lax.dynamic_slice(spread, (0, 32 * quarter), (16, 32))
    return turned.T, rows[16:24], small[:TAPS], small[TAPS : TAPS + 6]


def permutation(target):
    pairs = []
    for x in range(2):
        for d in range(16):
            tx, tz, ty, tc = target(x, d // 4, (d // 2) % 2, d % 2)
            pairs.append((x * 16 + d, tx * 16 + tz * 4 + ty * 2 + tc))
    return pairs


def across(value, target):
    return lax.ppermute(value, BOTH, permutation(target))


def over_x(value):
    return across(value, lambda x, z, y, c: (1 - x, z, y, c))


def over_core(value):
    return across(value, lambda x, z, y, c: (x, z, y, 1 - c))


def over_z(value, k):
    return across(value, lambda x, z, y, c: (x, z ^ k, y, c))


def over_a(value):
    return across(value, lambda x, z, y, c: (1 - x, z, y, c) if c == 0 else (x, z, 1 - y, c))


def over_b(value):
    return across(value, lambda x, z, y, c: (1 - x, z, y, c) if c == 1 else (x, z, 1 - y, c))


def fence(*values):
    return lax.optimization_barrier(values)


def z_parts(own):
    return [own] + [over_z(own, k) for k in (1, 2, 3)]


def ab_parts(quad):
    return over_a(quad), over_b(quad)


def core_parts(quad, ra, rb, rab):
    return [quad, rb, ra, rab] + [over_core(v) for v in (quad, rb, ra, rab)]


def add(*values):
    total = values[0].astype(F32)
    for value in values[1:]:
        total = total + value.astype(F32)
    return total


def halves(kept, came):
    cut = kept.shape[0] // 2
    return add(kept[:cut], came[:cut]).astype(BF), add(kept[cut:], came[cut:]).astype(BF)


def quarters(kept, came):
    return [add(kept[k], came[k]).astype(BF) for k in range(4)]


def z_sum(parts):
    return add(parts[0], *[over_z(parts[k], k) for k in (1, 2, 3)])


def pick(first, own, other):
    return jnp.where(first, own, other), jnp.where(first, other, own)


def on_device(fast, *args):
    (spectra, lengths, languages, token_masks, cotangent) = args[:5]
    masters = args[5:]
    sec = lax.axis_index("section")
    dp = lax.axis_index("dp")
    first = sec == 0
    low = [m.astype(BF) for m in masters]
    swap = lambda v: lax.ppermute(v, "section", [(0, 1), (1, 0)])
    cots = cotangent[0, :, 0]
    cot_send = lax.dynamic_index_in_dim(cots, 1 - sec, 0, keepdims=False)
    place = [sec, dp // 4, (dp // 2) % 2, dp % 2] if fast else [sec * 0] * 4
    ids = jnp.stack(place + [lengths[sec, 0], sec]).astype(jnp.int32)
    frames = lax.dynamic_index_in_dim(spectra, sec, 0, keepdims=False).reshape(512, -1)
    allowed_both = jnp.concatenate(
        [lax.dynamic_slice_in_dim(token_masks, languages[m, 0], 1, 0) for m in range(2)]
    ).astype(F32)
    allowed = lax.dynamic_slice_in_dim(allowed_both, sec, 1, 0)
    if fast:
        chunks = [None] * 4
        own_first, rest = own_pieces(low, sec, dp, first)
        early_cot, late_cot = cot_send[:320], cot_send[320:]
        own_first, rest, early_cot = fence(own_first, rest, early_cot)
        z0 = z_parts(own_first)
        own = own_rest(rest, low, sec, first)
        early_cot = swap(early_cot)
        *z0, own[0], early_cot = fence(*z0, own[0], early_cot)
        quad0 = jnp.stack(z0)
        a0, b0 = ab_parts(quad0)
        z1 = z_parts(own[0])
        quad0, a0, b0, own[2], *z1 = fence(quad0, a0, b0, own[2], *z1)
        pair3 = jnp.concatenate([own[2], over_a(own[2])])
        ab0 = over_b(a0)
        core0 = [over_core(v) for v in (quad0, b0, a0)]
        quad1 = jnp.stack(z1)
        quad1, ab0, frames, pair3, *core0 = fence(quad1, ab0, frames, pair3, *core0)
        a1, b1 = ab_parts(quad1)
        chunks[0] = [quad0, b0, a0, ab0] + core0 + [over_core(ab0)]
        *chunks[0], own[1] = fence(*chunks[0], own[1])
        z2 = z_parts(own[1])
    else:
        chunks = gather_plain(low)
        early_cot, late_cot = swap(cot_send[:320]), swap(cot_send[320:])
    ka = kernel_stem_feed(ids, chunks[0], frames)
    prm = ka.prm
    if fast:
        ka.x1, quad1, a1, b1, pair3, *z2 = fence(ka.x1, quad1, a1, b1, pair3, *z2)
        mid3 = over_z(pair3, 2)
        ab1 = over_b(a1)
        core1 = [over_core(v) for v in (quad1, b1, a1)]
        quad2 = jnp.stack(z2)
        ab1, quad2, pair3, mid3, *core1 = fence(ab1, quad2, pair3, mid3, *core1)
        a2, b2 = ab_parts(quad2)
        chunks[1] = [quad1, b1, a1, ab1] + core1 + [over_core(ab1)]
        *chunks[1], pair3 = fence(*chunks[1], pair3)
        far3, near3 = over_z(pair3, 3), over_z(pair3, 1)
    kb = kernel_rest_first(ids, chunks[1], prm, ka.x1)
    if fast:
        kb.sent, quad2, a2, b2, near3, far3, pair3 = fence(kb.sent, quad2, a2, b2, near3, far3, pair3)
        ab2 = over_b(a2)
        oct3 = jnp.stack([pair3, near3, mid3, far3])
        core2 = [over_core(v) for v in (quad2, b2, a2)]
        ab2, oct3, late_cot, *core2 = fence(ab2, oct3, late_cot, *core2)
        b3 = over_b(oct3)
        late_cot = swap(late_cot)
        chunks[2] = [quad2, b2, a2, ab2] + core2 + [over_core(ab2)]
        chunks[2] = list(fence(*chunks[2]))
        core3 = over_core(oct3)
    kc = kernel_first_second(ids, chunks[2], prm, kb.sent)
    if fast:
        kc.x3, oct3, b3, core3, late_cot = fence(kc.x3, oct3, b3, core3, late_cot)
        chunks[3] = [oct3, b3, core3, over_core(b3)]
    cot_other = [early_cot, late_cot]
    kd = kernel_turn(ids, chunks[3], prm, kc.x3, cots, cot_other, allowed)
    other_sent = swap(jnp.where(first, kd.sent, kb.sent))
    came = [None] * 6
    near, far, parts = [None] * 6, [None] * 6, [None] * 6

    def begin(n, kernel):
        near[n], far[n] = halves(kernel.keep, over_core(kernel.send))
        came[n] = over_a(far[n])

    def go_on(n):
        near[n], far[n] = halves(near[n], came[n])
        came[n] = over_b(far[n])

    def gather_parts(n):
        parts[n] = quarters(near[n], came[n])

    if fast:
        begin(0, kd)
    ke = kernel_mid(1, ids, chunks[2], FEED // 2, prm, kd.dx3, kc.x2, kc.gated, kc.deep, kc.x1, kc.qkv, kc.ls, kc.mixed)
    if fast:
        came[0], other_sent, ke.send, ke.dx1 = fence(came[0], other_sent, ke.send, ke.dx1)
        go_on(0)
        begin(1, ke)
    kf = kernel_early(1, ids, chunks[2], 0, prm, ke.dx1, kb.sent, kc.hid, None)
    if fast:
        came[0], came[1], kf.send, kf.ig = fence(came[0], came[1], kf.send, kf.ig)
        gather_parts(0)
        go_on(1)
        begin(2, kf)
    kg = kernel_late(
        ids, chunks[1], chunks[3], prm, kb.x4, kb.sent, cots, cot_other, allowed, kf.ig, kb.x3, kb.hid, kd.ghead
    )
    if fast:
        came[1], came[2], kg.send, kg.dx3 = fence(came[1], came[2], kg.send, kg.dx3)
        gather_parts(1)
        go_on(2)
        begin(3, kg)
        sums_a = z_sum([jnp.concatenate([p, q]) for p, q in zip(parts[0], parts[1])])
    kh = kernel_mid(0, ids, chunks[1], 0, prm, kg.dx3, kb.x2, kb.gated, kb.deep, ka.x1, kb.qkv, kb.ls, kb.mixed)
    if fast:
        came[2], came[3], sums_a, kh.send, kh.dx1 = fence(came[2], came[3], sums_a, kh.send, kh.dx1)
        gather_parts(2)
        go_on(3)
        begin(4, kh)
        sum_2 = z_sum(parts[2])
    stem = (ka.pre, ka.wout, frames, [kg.small, kh.small, kd.small, ke.small, kf.small])
    ki = kernel_early(0, ids, chunks[0], FLAT, prm, kh.dx1, ka.x0, ka.hid, stem)
    if fast:
        came[3], came[4], sum_2, ki.send, ki.ig, other_sent = fence(came[3], came[4], sum_2, ki.send, ki.ig, other_sent)
        gather_parts(3)
        go_on(4)
        begin(5, ki)
        sum_3 = z_sum(parts[3])
    ko = kernel_outputs(ids, chunks[3], kb.sent, kd.sent, other_sent, allowed_both, lengths[:, 0])
    if fast:
        came[4], came[5], sum_3, ki.ig, ko.acts, ko.logp = fence(came[4], came[5], sum_3, ki.ig, ko.acts, ko.logp)
        gather_parts(4)
        go_on(5)
        sum_4 = z_sum(parts[4])
        late = join(sum_3[: FEED // 2], sums_a[: FEED // 2], first).reshape(FEED, 512)
        head = sum_3[FEED // 2 :].T
        came[5], sum_4, ki.ig, late, head = fence(came[5], sum_4, ki.ig, late, head)
        gather_parts(5)
        sum_5 = z_sum(parts[5])
        late_in, late_out = unpack_in(late, 4), late[128:]
    other_grad = swap(jnp.where(first, kf.ig, ki.ig).astype(BF))
    if fast:
        sum_5, other_grad, late_in, late_out = fence(sum_5, other_grad, late_in, late_out)
        shards = all_shards(late_in, late_out, head, sums_a, sum_2, sum_4, sum_5, dp, first)
    else:
        shards = reduce_plain([(k.keep, k.send) for k in (kd, ke, kf, kg, kh, ki)])
    input_grads = kernel_grads(ids, ki.ig, kf.ig, other_grad)[None, :, None]
    activations = ko.acts[None, :, None]
    log_probs = ko.logp[None, :, None]
    return (activations, log_probs, input_grads, *shards)


def own_half(both, sec, first):
    mine = lax.dynamic_index_in_dim(both, sec, 0, keepdims=False)
    theirs = over_x(lax.dynamic_index_in_dim(both, 1 - sec, 0, keepdims=False))
    return pick(first, mine, theirs)


def own_pieces(low, sec, dp, first):
    feed_in, feed_out = low[:2]
    stem = pack_stem(low[8], low[9], low[5][0], low[7][0], dp % 4)
    feed_first, feed_second = own_half(pack_feed(feed_in[0, 0], feed_out[0, 0]).reshape(2, FEED // 2, 512), sec, first)
    return jnp.concatenate([stem, feed_first]), feed_second


def own_rest(feed_second, low, sec, first):
    feed_in, feed_out, attend_in, attend_out, conv_in, _, conv_out = low[:7]
    feed = pack_feed(feed_in[0, 1], feed_out[0, 1]).reshape(2, FEED // 2, 512)
    attn = pack_attn(attend_in[0], attend_out[0]).reshape(2, ATTN // 2, 512)
    conv = pack_conv(conv_in[0], conv_out[0]).reshape(2, CONV // 2, 512)
    rest_first, rest_second = own_half(jnp.concatenate([attn, conv, feed], axis=1), sec, first)
    return [
        rest_first,
        jnp.concatenate([feed_second, rest_second[:LATE_ROWS]]),
        jnp.concatenate([rest_second[LATE_ROWS:], low[10].T]),
    ]


def join(of_first, of_second, first):
    own = jnp.where(first, of_first, of_second)
    other = over_x(jnp.where(first, of_second, of_first).astype(BF)).astype(F32)
    return jnp.stack(pick(first, own, other))


def all_shards(late_in, late_out, head, sums_a, sum_2, sum_4, sum_5, dp, first):
    half = FEED // 2
    both = join(jnp.concatenate([sum_4, sum_5[:half]]), jnp.concatenate([sums_a[half:], sum_2]), first)
    attn = both[:, : ATTN // 2].reshape(ATTN, 512)
    conv = both[:, ATTN // 2 : LATE_ROWS].reshape(CONV, 512)
    early = both[:, LATE_ROWS:].reshape(FEED, 512)
    g_stem_in, g_stem_out, g_depth, g_gains = unpack_stem(sum_5[half:], dp % 4)
    return (
        jnp.stack([unpack_in(early, 4), late_in])[None],
        jnp.stack([early[128:], late_out])[None],
        unpack_in(attn, 3)[None],
        attn[96:][None],
        unpack_in(conv, 2)[None],
        g_depth[None],
        conv[64:][None],
        g_gains[None],
        g_stem_in,
        g_stem_out,
        head,
    )


def spread_order():
    order = []
    for cr, a, b, zk in pieces():
        px, py = (b, a) if cr else (a, b)
        order.append(px * 16 + zk * 4 + py * 2 + cr)
    return order


def gather_plain(low):
    axes = (2, 2, 1, 1, 1, 2, 1, 2)
    whole = []
    for weight, axis in zip(low[:8], axes):
        axis = 2 if weight.ndim == 4 else axis
        part = lax.all_gather(weight[0], "dp", axis=axis - 1, tiled=True)
        whole.append(lax.all_gather(part, "section", axis=0))
    feed_in, feed_out, attend_in, attend_out, conv_in, depth, conv_out, gains = whole
    stem_in = lax.all_gather(low[8], BOTH, axis=1, tiled=True)
    stem_out = lax.all_gather(low[9], BOTH, axis=0, tiled=True)
    head = lax.all_gather(low[10], BOTH, axis=1, tiled=True)
    order = spread_order()

    def layer(l):
        rows = lambda w, n: w.reshape(16, n, w.shape[-1])
        feeds = [jax.vmap(pack_feed)(rows(feed_in[l, j], 32), rows(feed_out[l, j], 128)) for j in range(2)]
        attn = jax.vmap(pack_attn)(rows(attend_in[l], 32), rows(attend_out[l], 32))
        conv = jax.vmap(pack_conv)(rows(conv_in[l], 32), rows(conv_out[l], 32))
        cut = lambda w: w.reshape(16, 2, w.shape[1] // 2, 512).transpose(1, 0, 2, 3).reshape(32, w.shape[1] // 2, 512)
        return [cut(w) for w in (feeds[0], attn, conv, feeds[1])]

    one, two = layer(0), layer(1)
    columns = lambda w, n: w.reshape(*w.shape[:-1], n, w.shape[-1] // n)
    small = lambda w: jnp.moveaxis(columns(w, 16), 2, 1).reshape(32, w.shape[1], 32)
    stem = jax.vmap(pack_stem)(
        jnp.moveaxis(columns(stem_in, 32), 1, 0),
        stem_out.reshape(32, 8, 512),
        small(depth),
        small(gains),
        jnp.arange(32) % 4,
    )
    head = head.T.reshape(32, 32, 512)
    chunks = ([stem, one[0]], one[1:], [two[0], two[1], two[2]], [two[3], head])
    placed = []
    for parts in chunks:
        joined = jnp.concatenate(parts, axis=1)
        placed.append([jnp.stack([joined[p] for p in order[4 * i : 4 * i + 4]]) for i in range(8)])
    return placed


def reduce_plain(grads):
    order = spread_order()
    place = [order.index(p) for p in range(32)]
    chunks = []
    for keep, send in grads:
        both = jnp.concatenate([keep, send])
        chunks.append(jnp.stack([both[q] for q in place]).astype(F32))
    half = FEED // 2
    whole = []
    for late, mid, early in (chunks[3:], chunks[:3]):
        glue = lambda part, begin, rows: (
            part[:, begin : begin + rows].reshape(2, 16, rows, 512).transpose(1, 0, 2, 3).reshape(16, 2 * rows, 512)
        )
        feeds = [glue(early, 0, half), glue(late, 0, half)]
        attn, conv = glue(mid, 0, ATTN // 2), glue(mid, ATTN // 2, CONV // 2)
        spread = lambda w, n: jax.vmap(lambda rows: unpack_in(rows, n))(w).reshape(512, 512 * n)
        whole.append(
            (
                jnp.stack([spread(f, 4) for f in feeds]),
                jnp.stack([f[:, 128:].reshape(FF, 512) for f in feeds]),
                spread(attn, 3),
                attn[:, 96:].reshape(512, 512),
                spread(conv, 2),
                conv[:, 64:].reshape(512, 512),
            )
        )
    head = chunks[3][:, half:].reshape(1024, 512).T
    g_stem_in, g_stem_out, g_depth, g_gains = jax.vmap(unpack_stem)(chunks[5][:, half:], jnp.arange(32) % 4)
    g_stem_in = jnp.moveaxis(g_stem_in, 0, 1).reshape(640, 256)
    g_stem_out = g_stem_out.reshape(256, 512)
    lanes = lambda w: jnp.moveaxis(w.reshape(2, 16, w.shape[1], 32), 1, 2).reshape(2, w.shape[1], 512)
    g_depth, g_gains = lanes(g_depth), lanes(g_gains)
    stacked = [jnp.stack([whole[0][i], whole[1][i]]) for i in range(6)]

    def shard(value, axis):
        value = lax.psum_scatter(value, "section", scatter_dimension=0, tiled=True)
        return lax.psum_scatter(value, "dp", scatter_dimension=axis, tiled=True)

    return (
        shard(stacked[0], 2),
        shard(stacked[1], 2),
        shard(stacked[2], 1),
        shard(stacked[3], 1),
        shard(stacked[4], 1),
        shard(g_depth, 2),
        shard(stacked[5], 1),
        shard(g_gains, 2),
        lax.psum_scatter(g_stem_in, BOTH, scatter_dimension=1, tiled=True),
        lax.psum_scatter(g_stem_out, BOTH, scatter_dimension=0, tiled=True),
        lax.psum_scatter(head, BOTH, scatter_dimension=1, tiled=True),
    )


def solution(mesh):
    fast = dict(mesh.shape) == {"section": 2, "dp": 16}

    def body(*args):
        return on_device(fast, *args)

    layer_specs = (
        P("section", None, "dp", None),
        P("section", None, "dp", None),
        P("section", "dp", None),
        P("section", "dp", None),
        P("section", "dp", None),
        P("section", None, "dp"),
        P("section", "dp", None),
        P("section", None, "dp"),
        P(None, BOTH),
        P(BOTH, None),
        P(None, BOTH),
    )
    rows = P("section", None, "dp", None, None)
    return jax.shard_map(
        body,
        mesh=mesh,
        in_specs=(P(None, "dp", None, None), P(None, "dp"), P(None, "dp"), P(), rows) + layer_specs,
        out_specs=(rows, rows, rows) + layer_specs,
        check_vma=False,
    )
```

```python
import types

import jax
import jax.numpy as jnp
from jax import lax
from jax.experimental import pallas as pl
from jax.experimental.pallas import tpu as pltpu
from jax.sharding import PartitionSpec as P

D = 512
HEADS = 8
HDIM = 64
FF = 2048
TAPS = 9
EPS = 1e-05
MASKED = -1e30
RB = 512
BOTH = ("section", "dp")
BF = jnp.bfloat16
F32 = jnp.float32

FEED, ATTN, CONV = 256, 128, 96
FLAT = 32
SMALL = 16


def dotn(a, b):
    return lax.dot_general(a, b, (((1,), (0,)), ((), ())), preferred_element_type=F32)


def dotr(a, b):
    return lax.dot_general(a, b, (((1,), (1,)), ((), ())), preferred_element_type=F32)


def dotl(a, b):
    return lax.dot_general(a, b, (((0,), (0,)), ((), ())), preferred_element_type=F32)


def sigmoid(v):
    return 0.5 * jnp.tanh(0.5 * v) + 0.5


def unit_rows(v):
    c = v - jnp.mean(v, axis=-1, keepdims=True)
    r = lax.rsqrt(jnp.mean(c * c, axis=-1, keepdims=True) + EPS)
    return c * r, r


def unit_back(dn, u, r, gain):
    du = dn * gain
    dv = r * (du - jnp.mean(du, axis=-1, keepdims=True) - u * jnp.mean(du * u, axis=-1, keepdims=True))
    return dv, jnp.sum(dn * u, axis=0, keepdims=True)


def row_mask(length, start, rows, columns):
    return (lax.broadcasted_iota(jnp.int32, (rows, columns), 0) + start < length).astype(F32)


def row_loop(body):
    for i in range(512 // RB):
        body(slice(i * RB, i * RB + RB), i * RB)


def piece_of(ids, cr, a, b, zk):
    pc = ids[3] ^ cr
    px = ids[0] ^ (a + pc * (b - a))
    py = ids[2] ^ (b + pc * (a - b))
    pz = ids[1] ^ zk
    return px, pz * 4 + py * 2 + pc


def pieces():
    return [(cr, a, b, zk) for cr in range(2) for a in range(2) for b in range(2) for zk in range(4)]


def start_load(ids, bufs, row, rows, scr, sem, flat=False):
    for cr, a, b, zk in pieces():
        px, d = piece_of(ids, cr, a, b, zk)
        if len(bufs) == 4:
            begin = row + a * (bufs[0].shape[1] // 2)
            src = bufs[cr * 2 + b].at[zk, begin : begin + rows]
        else:
            src = bufs[cr * 4 + a * 2 + b].at[zk, row : row + rows]
        if flat:
            dst = scr.at[px * 16 + d]
        else:
            dst = scr.at[d, pl.ds(pl.multiple_of(px * rows, 16), rows)]
        pltpu.make_async_copy(src, dst, sem).start()


def wait_load(scr, sem):
    pltpu.make_async_copy(scr, scr, sem).wait()


def start_store(ids, scr, keep, send, row, rows, sem, flat=False):
    for cr, a, b, zk in pieces():
        px, d = piece_of(ids, cr, a, b, zk)
        if flat:
            src = scr.at[px * 16 + d]
        else:
            src = scr.at[d, pl.ds(pl.multiple_of(px * rows, 16), rows)]
        dst = (send if cr else keep).at[a * 8 + b * 4 + zk, row : row + rows]
        pltpu.make_async_copy(src, dst, sem).start()


def start_piece(ids, scr, keep, send, row, rows, sem, px, d):
    pz, py, pc = d // 4, (d // 2) % 2, d % 2
    xr, yr, zk, cr = px ^ ids[0], py ^ ids[2], pz ^ ids[1], pc ^ ids[3]
    a, b = (yr, xr) if pc else (xr, yr)
    src = scr.at[d, px * rows : px * rows + rows]
    for side, target in enumerate((keep, send)):

        @pl.when(cr == side)
        def _():
            pltpu.make_async_copy(src, target.at[a * 8 + b * 4 + zk, row : row + rows], sem).start()


def wait_store(scr, sem):
    pltpu.make_async_copy(scr, scr, sem).wait()


def in_block(w, j):
    return w[:, 32 * j : 32 * j + 32, :].reshape(512, 512)


def out_block(w, j):
    return w[4 * j : 4 * j + 4, 128:256, :].reshape(512, 512)


def feed_fwd(x, w, gain, hid, out):
    def body(rs, start):
        v = x[rs, :].astype(F32)
        u, _ = unit_rows(v)
        n = (u * gain).astype(BF)
        total = jnp.zeros((RB, 512), F32)
        for j in range(4):
            h = dotn(n, in_block(w, j))
            hid[rs, 512 * j : 512 * j + 512] = h.astype(BF)
            total = total + dotn((h * sigmoid(h)).astype(BF), out_block(w, j))
        out[rs, :] = v + 0.5 * total

    row_loop(body)


def feed_bwd(dx, x, hid, w, gain, result, gw, small, row, s):
    def body(rs, start):
        g = dx[rs, :]
        v = x[rs, :].astype(F32)
        u, r = unit_rows(v)
        s.n[rs, :] = (u * gain).astype(BF)
        d = (0.5 * g).astype(BF)
        s.d[rs, :] = d
        dn = jnp.zeros((RB, 512), F32)
        for j in range(4):
            h = hid[rs, 512 * j : 512 * j + 512].astype(F32)
            sg = sigmoid(h)
            s.act[rs, 512 * j : 512 * j + 512] = (h * sg).astype(BF)
            dh = (dotr(d, out_block(w, j)) * (sg * (1.0 + h * (1.0 - sg)))).astype(BF)
            s.dh[rs, 512 * j : 512 * j + 512] = dh
            dn = dn + dotr(dh, in_block(w, j))
        dv, gg = unit_back(dn, u, r, gain)
        result.held[rs, :] = g + dv
        small[row : row + 1, :] += gg

    row_loop(body)
    result.go()
    for j in range(4):
        cols = slice(512 * j, 512 * j + 512)
        gw[4 * j : 4 * j + 4, 128:256, :] = dotl(s.act[:, cols], s.d[...]).astype(BF).reshape(4, 128, 512)
        for d in range(4 * j, 4 * j + 4):
            start_piece(s.ids, gw, s.keep, s.send, 0, FEED // 2, s.sems.at[3], 1, d)
    for j in range(4):
        cols = slice(512 * j, 512 * j + 512)
        gw[:, 32 * j : 32 * j + 32, :] = dotl(s.n[...], s.dh[:, cols]).astype(BF).reshape(16, 32, 512)
    for d in range(16):
        start_piece(s.ids, gw, s.keep, s.send, 0, FEED // 2, s.sems.at[3], 0, d)


def lanes_of(half, axis=1, count=1):
    shape = (count, 128) if axis else (128, count)
    return (lax.broadcasted_iota(jnp.int32, shape, axis) + 64 * half) % 128 - 64


def attn_fwd(x, w, gain, length, qkv, ls, mixt, out):
    def project(rs, start):
        u, _ = unit_rows(x[rs, :])
        n = (u * gain).astype(BF)
        for j in range(3):
            qkv[rs, 512 * j : 512 * j + 512] = dotn(n, in_block(w, j)).astype(BF)

    row_loop(project)

    for hp in range(4):
        at = hp * 128
        k = qkv[:, pl.ds(512 + at, 128)].astype(F32)
        vt = qkv[:, pl.ds(1024 + at, 128)].astype(F32).T
        outside = jnp.where(lax.broadcasted_iota(jnp.int32, (512, 128), 0) < length, 0.0, MASKED)
        kx, vx = [], []
        for hh in range(2):
            free = lanes_of(hh)
            kx.append(jnp.where(free < 0, k, jnp.where(free == 0, outside, 0.0)).astype(BF))
            free = lanes_of(hh, 0, 512)
            vx.append(jnp.where(free < 0, vt, jnp.where(free == 0, 1.0, 0.0)).astype(BF))

        def body(rs, start):
            q = qkv[rs, pl.ds(at, 128)].astype(F32) * HDIM**-0.5
            parts = []
            for hh in range(2):
                free = lanes_of(hh)
                qx = jnp.where(free < 0, q, jnp.where(free == 0, 1.0, 0.0)).astype(BF)
                sc = dotr(kx[hh], qx)
                top = jnp.max(sc, axis=0, keepdims=True)
                both = dotn(vx[hh], jnp.exp(sc - top).astype(BF))
                tot = both[64 * (1 - hh) : 64 * (1 - hh) + 1, :]
                parts.append(both * (1.0 / tot))
                ls[pl.ds(hp * 2 + hh, 1), rs] = top + jnp.log(tot)
            mixt[pl.ds(at, 128), rs] = jnp.where(lanes_of(0, 0, RB) < 0, parts[0], parts[1]).astype(BF)

        row_loop(body)

    def project_out(rs, start):
        out[rs, :] = x[rs, :] + dotl(mixt[:, rs], w[:, 96:128, :].reshape(512, 512))

    row_loop(project_out)


def attn_bwd(dx, x, qkv, ls, mixt, w, gain, length, out, gw, small, row, s):
    def first(rs, start):
        u, _ = unit_rows(x[rs, :])
        s.n[rs, :] = (u * gain).astype(BF)
        d = dx[rs, :].astype(BF)
        s.d[rs, :] = d
        s.dm[:, rs] = dotr(w[:, 96:128, :].reshape(512, 512), d).astype(BF)

    row_loop(first)
    gw[:, 96:128, :] = dotn(mixt[...], s.d[...]).astype(BF).reshape(16, 32, 512)

    for hp in range(4):
        at = hp * 128
        s.dq[...] = jnp.zeros((128, 512), F32)
        q = qkv[:, pl.ds(at, 128)].astype(F32) * HDIM**-0.5
        kt = qkv[:, pl.ds(512 + at, 128)].astype(F32).T * HDIM**-0.5
        dmt = s.dm[pl.ds(at, 128), :].astype(F32)
        prod = dmt * mixt[pl.ds(at, 128), :].astype(F32)
        qx, qs, dms, deltas, sums = [], [], [], [], []
        for hh in range(2):
            free = lanes_of(hh)
            qs.append(jnp.where(free < 0, q, 0.0).astype(BF))
            qx.append(jnp.where(free < 0, q, jnp.where(free == 0, 1.0, 0.0)).astype(BF))
            free = lanes_of(hh, 0, 512)
            dms.append(jnp.where(free < 0, dmt, 0.0).astype(BF))
            deltas.append(jnp.sum(prod[64 * hh : 64 * hh + 64, :], axis=0, keepdims=True))
            s.kt[128 * hh : 128 * hh + 128, :] = jnp.where(free < 0, kt, 0.0).astype(BF)
            sums.append(ls[pl.ds(hp * 2 + hh, 1), :])

        def body(rs, start):
            k = qkv[rs, pl.ds(512 + at, 128)].astype(F32)
            v = qkv[rs, pl.ds(1024 + at, 128)]
            outside = jnp.where(lax.broadcasted_iota(jnp.int32, (RB, 128), 0) + start < length, 0.0, MASKED)
            dk = jnp.zeros((RB, 128), F32)
            dv = jnp.zeros((RB, 128), F32)
            for hh in range(2):
                free = lanes_of(hh)
                kx = jnp.where(free < 0, k, jnp.where(free == 0, outside, 0.0)).astype(BF)
                p = jnp.exp(dotr(kx, qx[hh]) - sums[hh])
                ds = (p * (dotn(v, dms[hh]) - deltas[hh])).astype(BF)
                dv = dv + dotr(p.astype(BF), dms[hh])
                dk = dk + dotn(ds, qs[hh])
                s.dq[...] += dotn(s.kt[128 * hh : 128 * hh + 128, rs], ds)
            s.dpk[rs, pl.ds(512 + at, 128)] = dk.astype(BF)
            s.dpk[rs, pl.ds(1024 + at, 128)] = dv.astype(BF)

        row_loop(body)
        s.dpk[:, pl.ds(at, 128)] = s.dq[...].T.astype(BF)

    def last(rs, start):
        u, r = unit_rows(x[rs, :])
        dn = jnp.zeros((RB, 512), F32)
        for j in range(3):
            dn = dn + dotr(s.dpk[rs, 512 * j : 512 * j + 512], in_block(w, j))
        dv, gg = unit_back(dn, u, r, gain)
        out[rs, :] = dx[rs, :] + dv
        small[row : row + 1, :] += gg

    row_loop(last)
    for j in range(3):
        gw[:, 32 * j : 32 * j + 32, :] = (
            dotl(s.n[...], s.dpk[:, 512 * j : 512 * j + 512]).astype(BF).reshape(16, 32, 512)
        )


PAD = 8


def conv_fwd(x, w, prm, length, gated, deep, out, pad):
    pad[0:PAD, :] = jnp.zeros((PAD, 512), F32)
    pad[PAD + 512 : 2 * PAD + 512, :] = jnp.zeros((PAD, 512), F32)

    def first(rs, start):
        u, _ = unit_rows(x[rs, :])
        n = (u * prm[TAPS + 2 : TAPS + 3, :]).astype(BF)
        a = dotn(n, in_block(w, 0))
        b = dotn(n, in_block(w, 1))
        gated[rs, 0:512] = a
        gated[rs, 512:1024] = b
        pad[pl.ds(start + PAD, RB), :] = a * sigmoid(b) * row_mask(length, start, RB, 512)

    row_loop(first)
    for i in range(512 // RB):
        total = jnp.zeros((RB, 512), F32)
        for t in range(TAPS):
            begin = i * RB + PAD - TAPS // 2 + t
            total = total + prm[t : t + 1, :] * pad[begin : begin + RB, :]
        deep[i * RB : i * RB + RB, :] = total

    def last(rs, start):
        u, _ = unit_rows(deep[rs, :])
        m = u * prm[TAPS + 3 : TAPS + 4, :]
        act = (m * sigmoid(m)).astype(BF)
        out[rs, :] = x[rs, :] + dotn(act, w[:, 64:96, :].reshape(512, 512))

    row_loop(last)


def conv_bwd(dx, x, gated, deep, w, prm, length, out, gw, small, s):
    s.back[0:PAD, :] = jnp.zeros((PAD, 512), F32)
    s.back[PAD + 512 : 2 * PAD + 512, :] = jnp.zeros((PAD, 512), F32)
    gain_in = prm[TAPS + 2 : TAPS + 3, :]
    gain_mid = prm[TAPS + 3 : TAPS + 4, :]

    def first(rs, start):
        padded = pl.ds(start + PAD, RB)
        d = dx[rs, :].astype(BF)
        s.d[rs, :] = d
        u3, r3 = unit_rows(deep[rs, :])
        m = u3 * gain_mid
        sg = sigmoid(m)
        s.act[rs, :] = (m * sg).astype(BF)
        dmid = dotr(d, w[:, 64:96, :].reshape(512, 512)) * (sg * (1.0 + m * (1.0 - sg)))
        ddeep, gg = unit_back(dmid, u3, r3, gain_mid)
        s.back[padded, :] = ddeep
        small[TAPS + 3 : TAPS + 4, :] += gg
        s.glu[rs, :] = (
            gated[rs, 0:512] * sigmoid(gated[rs, 512:1024]) * row_mask(length, start, RB, 512)
        )

    row_loop(first)
    gw[:, 64:96, :] = dotl(s.act[...], s.d[...]).astype(BF).reshape(16, 32, 512)
    for i in range(512 // RB):
        rows = slice(i * RB, i * RB + RB)
        glu = s.glu[rows, :]
        dglu = jnp.zeros((RB, 512), F32)
        for t in range(TAPS):
            begin = i * RB + PAD + TAPS // 2 - t
            later = s.back[begin : begin + RB, :]
            small[t : t + 1, :] += jnp.sum(glu * later, axis=0, keepdims=True)
            dglu = dglu + prm[t : t + 1, :] * later
        dglu = dglu * row_mask(length, i * RB, RB, 512)
        sg = sigmoid(gated[rows, 512:1024])
        ga = dglu * sg
        s.dga[rows, :] = ga.astype(BF)
        s.dgb[rows, :] = (ga * gated[rows, 0:512] * (1.0 - sg)).astype(BF)

    def last(rs, start):
        u, r = unit_rows(x[rs, :])
        s.n[rs, :] = (u * gain_in).astype(BF)
        dn = dotr(s.dga[rs, :], in_block(w, 0)) + dotr(s.dgb[rs, :], in_block(w, 1))
        dv, gg = unit_back(dn, u, r, gain_in)
        out[rs, :] = dx[rs, :] + dv
        small[TAPS + 2 : TAPS + 3, :] += gg

    row_loop(last)
    gw[:, 0:32, :] = dotl(s.n[...], s.dga[...]).astype(BF).reshape(16, 32, 512)
    gw[:, 32:64, :] = dotl(s.n[...], s.dgb[...]).astype(BF).reshape(16, 32, 512)


def finish_fwd(x4, prm, length, sent):
    def body(rs, start):
        u, _ = unit_rows(x4[rs, :])
        sent[rs, :] = (u * prm[TAPS + 5 : TAPS + 6, :] * row_mask(length, start, RB, 512)).astype(BF)

    row_loop(body)


def head_rows(sent, w, permit):
    logits = dotr(sent, w)
    top = jnp.max(jnp.where(permit, logits, MASKED), axis=-1, keepdims=True)
    e = jnp.exp(jnp.where(permit, logits - top, MASKED))
    return logits, top + jnp.log(jnp.sum(e, axis=-1, keepdims=True))


def head_bwd(x4, sent, w, allowed, cot, prm, length, extra, out, gl, small):
    permit = allowed[...] > 0
    gain = prm[TAPS + 5 : TAPS + 6, :]

    def body(rs, start):
        hw = w[...].reshape(1024, 512)
        logits, logsum = head_rows(sent[rs, :], hw, permit)
        weighted = jnp.where(permit, cot[rs, :].astype(F32), 0.0) * row_mask(length, start, RB, 1024)
        probs = jnp.exp(jnp.where(permit, logits - logsum, MASKED))
        g = (weighted - probs * jnp.sum(weighted, axis=-1, keepdims=True)).astype(BF)
        gl[rs, :] = g
        gs = dotn(g, hw)
        if extra is not None:
            gs = gs + extra[rs, :].astype(BF).astype(F32)
        u, r = unit_rows(x4[rs, :])
        dv, gg = unit_back(gs * row_mask(length, start, RB, 512), u, r, gain)
        out[rs, :] = dv
        small[TAPS + 5 : TAPS + 6, :] += gg

    row_loop(body)


ANY, VMEM, SMEM = pl.ANY, pltpu.VMEM, pltpu.SMEM
LATE = object()


class Late:
    def __init__(self, source, held, sem):
        self.copy, self.held, self.going, self.here = pltpu.make_async_copy(source, held, sem), held, False, False

    def go(self):
        self.going = True
        self.copy.start()

    def get(self):
        if not self.going:
            self.go()
        if not self.here:
            self.copy.wait()
        self.here = True
        return self.held


class Soon:
    def __init__(self, held, target, sem):
        self.copy, self.held, self.going = pltpu.make_async_copy(held, target, sem), held, False

    def go(self):
        self.going = True
        self.copy.start()

    def end(self):
        if not self.going:
            self.go()
        self.copy.wait()


def run(body, micros, ins, outs, scratch):
    flat, held = [], []
    for value, space in ins.values():
        flat += [(array, ANY if space is LATE else space) for array in (value if isinstance(value, list) else [value])]
        if space is LATE:
            held.append((value.shape, value.dtype))
    held += [(shape, dtype) for shape, dtype, space in outs.values() if space is LATE]

    def kernel(*refs):
        left = list(refs)
        ns = types.SimpleNamespace()
        waiting, soon = [], []
        for key, (value, space) in ins.items():
            if isinstance(value, list):
                setattr(ns, key, [left.pop(0) for _ in value])
            else:
                setattr(ns, key, left.pop(0))
        for key in [*outs, *scratch]:
            setattr(ns, key, left.pop(0))
        ns.sems = left.pop()
        number = 8
        for key, (_, space) in ins.items():
            if space is LATE:
                setattr(ns, key, Late(getattr(ns, key), left.pop(0), ns.sems.at[number]))
                number += 1
        for key, (_, _, space) in outs.items():
            if space is LATE:
                soon.append(Soon(left.pop(0), getattr(ns, key), ns.sems.at[number]))
                setattr(ns, key, soon[-1])
                number += 1
        body(ns)
        for result in soon:
            result.end()

    result = pl.pallas_call(
        kernel,
        out_shape=[jax.ShapeDtypeStruct(shape, dtype) for shape, dtype, _ in outs.values()],
        in_specs=[pl.BlockSpec(memory_space=space) for _, space in flat],
        out_specs=[pl.BlockSpec(memory_space=ANY if space is LATE else space) for _, _, space in outs.values()],
        scratch_shapes=[pltpu.VMEM(shape, dtype) for shape, dtype in [*scratch.values(), *held]]
        + [pltpu.SemaphoreType.DMA((8 + len(held),))],
        compiler_params=pltpu.CompilerParams(vmem_limit_bytes=55 * 2**20),
        cost_estimate=pl.CostEstimate(flops=int(micros * 1.1e9), bytes_accessed=2**20, transcendentals=0),
        name=body.__name__,
    )(*[array for array, _ in flat])
    return types.SimpleNamespace(**dict(zip(outs, result)))


ROWS = (512, 512)
WF, WA, WC, WH = ((16, FEED, 512), BF), ((16, ATTN, 512), BF), ((16, CONV, 512), BF), ((32, FLAT, 512), BF)
PADDED = ((512 + 2 * PAD, 512), F32)
LATE_ROWS = ATTN // 2 + CONV // 2


def gain_of(prm, number):
    return prm[TAPS + number : TAPS + number + 1, :]


def kernel_stem_feed(ids, bufs, frames):
    def stem_feed(k):
        start_load(k.ids, k.bufs, 0, FLAT, k.stem, k.sems.at[0], flat=True)
        k.frames.go()
        start_load(k.ids, k.bufs, FLAT, FEED // 2, k.w, k.sems.at[1])
        wait_load(k.stem, k.sems.at[0])
        stem = k.stem[...].astype(F32)
        for layer in range(2):
            for z in range(4):
                part = jnp.zeros((8, 512), F32)
                for q in range(4):
                    part = part + stem[layer * 16 + z * 4 + q, 24:32, :]
                k.prm[layer, 0:8, 128 * z : 128 * z + 128] = part[:, 0:128]
                k.prm[layer, 8:16, 128 * z : 128 * z + 128] = part[:, 128:256]
        win_a = stem[:, 0:8, :].reshape(256, 512).astype(BF)
        win_b = stem[:, 8:16, 0:128].reshape(256, 128).astype(BF)
        k.wout[...] = stem[:, 16:24, :].reshape(256, 512).astype(BF)
        frames, x0, x1, hid, pre = k.frames.get(), k.x0.held, k.x1.held, k.hid.held, k.pre.held

        def rows(rs, start):
            p = dotr(frames[rs, 0:512], win_a) + dotr(frames[rs, 512:640], win_b)
            pre[rs, :] = p
            x = dotn((p * sigmoid(p)).astype(BF), k.wout[...])
            x0[rs, :] = (x * row_mask(k.ids[4], start, RB, 512)).astype(BF)

        row_loop(rows)
        k.pre.go()
        k.x0.go()
        wait_load(k.w, k.sems.at[1])
        feed_fwd(x0, k.w, gain_of(k.prm.at[0], 0), hid, x1)

    return run(
        stem_feed,
        9,
        dict(ids=(ids, SMEM), bufs=(bufs, ANY), frames=(frames, LATE)),
        dict(
            prm=((2, SMALL, 512), F32, VMEM),
            pre=((512, 256), F32, LATE),
            wout=((256, 512), BF, VMEM),
            x0=(ROWS, BF, LATE),
            hid=((512, FF), BF, LATE),
            x1=(ROWS, F32, LATE),
        ),
        dict(stem=WH, w=WF),
    )


ATTN_OUTS = dict(qkv=((512, 1536), BF, LATE), ls=((8, 512), F32, VMEM), mixed=(ROWS, BF, LATE), x2=(ROWS, F32, LATE))
CONV_OUTS = dict(gated=((512, 1024), F32, LATE), deep=(ROWS, F32, LATE), x3=(ROWS, F32, LATE))


def attn_conv(k, x1, prm):
    wait_load(k.wa, k.sems.at[0])
    attn_fwd(x1, k.wa, gain_of(prm, 1), k.ids[4], k.qkv.held, k.ls, k.mixed.held, k.x2.held)
    for result in (k.qkv, k.mixed, k.x2):
        result.go()
    wait_load(k.wc, k.sems.at[1])
    conv_fwd(k.x2.held, k.wc, prm, k.ids[4], k.gated.held, k.deep.held, k.x3.held, k.pad)
    for result in (k.gated, k.deep, k.x3):
        result.go()


def kernel_rest_first(ids, bufs, prm, x1):
    def rest_first(k):
        k.x1.go()
        start_load(k.ids, k.bufs, 0, ATTN // 2, k.wa, k.sems.at[0])
        start_load(k.ids, k.bufs, ATTN // 2, CONV // 2, k.wc, k.sems.at[1])
        start_load(k.ids, k.bufs, LATE_ROWS, FEED // 2, k.wf, k.sems.at[2])
        prm = k.prm.at[0]
        attn_conv(k, k.x1.get(), prm)
        wait_load(k.wf, k.sems.at[2])
        feed_fwd(k.x3.held, k.wf, gain_of(prm, 4), k.hid.held, k.x4.held)
        k.hid.go()
        k.x4.go()
        finish_fwd(k.x4.held, prm, k.ids[4], k.sent)

    return run(
        rest_first,
        20,
        dict(ids=(ids, SMEM), bufs=(bufs, ANY), prm=(prm, VMEM), x1=(x1, LATE)),
        ATTN_OUTS | CONV_OUTS | dict(hid=((512, FF), BF, LATE), x4=(ROWS, F32, LATE), sent=(ROWS, BF, VMEM)),
        dict(wa=WA, wc=WC, wf=WF, pad=PADDED),
    )


def kernel_first_second(ids, bufs, prm, x0):
    def first_second(k):
        start_load(k.ids, k.bufs, 0, FEED // 2, k.wf, k.sems.at[2])
        start_load(k.ids, k.bufs, FEED // 2, ATTN // 2, k.wa, k.sems.at[0])
        start_load(k.ids, k.bufs, FEED // 2 + ATTN // 2, CONV // 2, k.wc, k.sems.at[1])
        prm = k.prm.at[1]
        wait_load(k.wf, k.sems.at[2])
        feed_fwd(k.x0, k.wf, gain_of(prm, 0), k.hid.held, k.x1.held)
        k.hid.go()
        k.x1.go()
        attn_conv(k, k.x1.held, prm)

    return run(
        first_second,
        20,
        dict(ids=(ids, SMEM), bufs=(bufs, ANY), prm=(prm, VMEM), x0=(x0, VMEM)),
        dict(hid=((512, FF), BF, LATE), x1=(ROWS, F32, LATE)) | ATTN_OUTS | CONV_OUTS,
        dict(wa=WA, wc=WC, wf=WF, pad=PADDED),
    )


def start_cot(k, layer):
    @pl.when(k.ids[5] == layer)
    def _():
        pltpu.make_async_copy(k.cots.at[k.ids[5]], k.cot, k.sems.at[2]).start()

    @pl.when(k.ids[5] != layer)
    def _():
        at = 0
        for part in k.cot_other:
            pltpu.make_async_copy(part, k.cot.at[at : at + part.shape[0]], k.sems.at[2]).start()
            at += part.shape[0]


FEED_SCRATCH = dict(n=(ROWS, BF), d=(ROWS, BF), act=((512, FF), BF), dh=((512, FF), BF), wf=WF, gf=WF)
HEAD_SCRATCH = dict(wh=WH, cot=((512, 1024), BF), gl=((512, 1024), BF), dx4=(ROWS, F32))


def kernel_turn(ids, bufs, prm, x3, cots, cot_other, allowed):
    def turn(k):
        k.prm.go()
        k.x3.go()
        start_load(k.ids, k.bufs, 0, FEED // 2, k.wf, k.sems.at[0])
        start_load(k.ids, k.bufs, FEED // 2, FLAT, k.wh, k.sems.at[1], flat=True)
        start_cot(k, 1)
        prm = k.prm.get().at[1]
        small = k.small.held
        small[...] = jnp.zeros((SMALL, 512), F32)
        x3 = k.x3.get()
        wait_load(k.wf, k.sems.at[0])
        feed_fwd(x3, k.wf, gain_of(prm, 4), k.hid, k.x4)
        finish_fwd(k.x4, prm, k.ids[4], k.sent)
        wait_load(k.wh, k.sems.at[1])
        wait_load(k.cot, k.sems.at[2])
        head_bwd(k.x4, k.sent, k.wh, k.allowed, k.cot, prm, k.ids[4], None, k.dx4, k.gl, small)
        k.ghead.held[...] = dotl(k.gl[...], k.sent[...])
        k.ghead.go()
        feed_bwd(k.dx4, x3, k.hid, k.wf, gain_of(prm, 4), k.dx3, k.gf, small, TAPS + 4, k)
        wait_store(k.gf, k.sems.at[3])

    rows = FEED // 2
    return run(
        turn,
        22,
        dict(
            ids=(ids, SMEM),
            bufs=(bufs, ANY),
            prm=(prm, LATE),
            x3=(x3, LATE),
            cots=(cots, ANY),
            cot_other=(cot_other, ANY),
            allowed=(allowed, VMEM),
        ),
        dict(
            sent=(ROWS, BF, VMEM),
            ghead=((1024, 512), F32, LATE),
            dx3=(ROWS, F32, LATE),
            small=((SMALL, 512), F32, LATE),
            keep=((16, rows, 512), BF, ANY),
            send=((16, rows, 512), BF, ANY),
        ),
        FEED_SCRATCH | HEAD_SCRATCH | dict(hid=((512, FF), BF), x4=(ROWS, F32)),
    )


def kernel_late(ids, bufs, head_bufs, prm, x4, sent, cots, cot_other, allowed, ig, x3, hid, ghead):
    def late(k):
        start_load(k.ids, k.hbufs, FEED // 2, FLAT, k.wh, k.sems.at[1], flat=True)
        start_cot(k, 0)
        for operand in (k.prm, k.x4, k.sent, k.ig):
            operand.go()
        start_load(k.ids, k.bufs, LATE_ROWS, FEED // 2, k.wf, k.sems.at[0])
        for operand in (k.ghead, k.x3, k.hid):
            operand.go()
        prm = k.prm.get().at[0]
        small = k.small.held
        small[...] = jnp.zeros((SMALL, 512), F32)
        wait_load(k.wh, k.sems.at[1])
        wait_load(k.cot, k.sems.at[2])
        sent = k.sent.get()
        head_bwd(k.x4.get(), sent, k.wh, k.allowed, k.cot, prm, k.ids[4], k.ig.get(), k.dx4, k.gl, small)
        k.gh[...] = (k.ghead.get()[...] + dotl(k.gl[...], sent[...])).astype(BF).reshape(32, FLAT, 512)
        start_store(k.ids, k.gh, k.keep, k.send, FEED // 2, FLAT, k.sems.at[4], flat=True)
        wait_load(k.wf, k.sems.at[0])
        feed_bwd(k.dx4, k.x3.get(), k.hid.get(), k.wf, gain_of(prm, 4), k.dx3, k.gf, small, TAPS + 4, k)
        wait_store(k.gh, k.sems.at[4])
        wait_store(k.gf, k.sems.at[3])

    rows = FEED // 2 + FLAT
    return run(
        late,
        17,
        dict(
            ids=(ids, SMEM),
            bufs=(bufs, ANY),
            hbufs=(head_bufs, ANY),
            prm=(prm, LATE),
            x4=(x4, LATE),
            sent=(sent, LATE),
            cots=(cots, ANY),
            cot_other=(cot_other, ANY),
            allowed=(allowed, VMEM),
            ig=(ig, LATE),
            x3=(x3, LATE),
            hid=(hid, LATE),
            ghead=(ghead, LATE),
        ),
        dict(
            dx3=(ROWS, F32, LATE),
            small=((SMALL, 512), F32, LATE),
            keep=((16, rows, 512), BF, ANY),
            send=((16, rows, 512), BF, ANY),
        ),
        FEED_SCRATCH | HEAD_SCRATCH | dict(gh=WH),
    )


def kernel_mid(layer, ids, bufs, row, prm, dx3, x2, gated, deep, x1, qkv, ls, mixed):
    def mid(k):
        for operand in (k.prm, k.dx3, k.deep):
            operand.go()
        start_load(k.ids, k.bufs, row + ATTN // 2, CONV // 2, k.wc, k.sems.at[1])
        for operand in (k.gated, k.x2):
            operand.go()
        start_load(k.ids, k.bufs, row, ATTN // 2, k.wa, k.sems.at[0])
        for operand in (k.x1, k.mixed, k.qkv, k.ls):
            operand.go()
        prm = k.prm.get().at[layer]
        small = k.small.held
        small[...] = jnp.zeros((SMALL, 512), F32)
        wait_load(k.wc, k.sems.at[1])
        s = types.SimpleNamespace(
            n=k.n, d=k.d, act=k.act.at[:, 0:512], dga=k.dh.at[:, 0:512], dgb=k.dh.at[:, 512:1024], glu=k.glu, back=k.back
        )
        conv_bwd(k.dx3.get(), k.x2.get(), k.gated.get(), k.deep.get(), k.wc, prm, k.ids[4], k.dx2, k.gc, small, s)
        start_store(k.ids, k.gc, k.keep, k.send, ATTN // 2, CONV // 2, k.sems.at[3])
        wait_load(k.wa, k.sems.at[0])
        s = types.SimpleNamespace(n=k.n, d=k.d, dm=k.dm, dpk=k.act, dq=k.dq, kt=k.kt)
        attn_bwd(
            k.dx2, k.x1.get(), k.qkv.get(), k.ls.get(), k.mixed.get(), k.wa, gain_of(prm, 1), k.ids[4], k.dx1.held, k.ga,
            small, TAPS + 1, s,
        )
        start_store(k.ids, k.ga, k.keep, k.send, 0, ATTN // 2, k.sems.at[2])
        wait_store(k.gc, k.sems.at[3])
        wait_store(k.ga, k.sems.at[2])

    return run(
        mid,
        21,
        dict(
            ids=(ids, SMEM),
            bufs=(bufs, ANY),
            prm=(prm, LATE),
            dx3=(dx3, LATE),
            x2=(x2, LATE),
            gated=(gated, LATE),
            deep=(deep, LATE),
            x1=(x1, LATE),
            qkv=(qkv, LATE),
            ls=(ls, LATE),
            mixed=(mixed, LATE),
        ),
        dict(
            dx1=(ROWS, F32, LATE),
            small=((SMALL, 512), F32, LATE),
            keep=((16, LATE_ROWS, 512), BF, ANY),
            send=((16, LATE_ROWS, 512), BF, ANY),
        ),
        dict(
            wa=WA,
            wc=WC,
            ga=WA,
            gc=WC,
            dx2=(ROWS, F32),
            n=(ROWS, BF),
            d=(ROWS, BF),
            dm=(ROWS, BF),
            act=((512, 1536), BF),
            dh=((512, 1024), BF),
            glu=(ROWS, F32),
            back=PADDED,
            dq=((128, 512), F32),
            kt=((256, 512), BF),
        ),
    )


def kernel_early(layer, ids, bufs, row, prm, dx1, x0, hid, stem):
    def early(k):
        for operand in (k.prm, k.dx1, k.x0):
            operand.go()
        start_load(k.ids, k.bufs, row, FEED // 2, k.wf, k.sems.at[1])
        k.hid.go()
        if stem is not None:
            k.pre.go()
            k.frames.go()
        prm = k.prm.get().at[layer]
        small = k.small.held
        small[...] = jnp.zeros((SMALL, 512), F32)
        wait_load(k.wf, k.sems.at[1])
        ig = k.ig.held
        feed_bwd(k.dx1.get(), k.x0.get(), k.hid.get(), k.wf, gain_of(prm, 0), k.ig, k.gf, small, TAPS, k)
        k.small.go()
        if stem is not None:
            pre, frames = k.pre.get(), k.frames.get()

            def rows(rs, start):
                d = (ig[rs, :] * row_mask(k.ids[4], start, RB, 512)).astype(BF)
                k.d[rs, :] = d
                p = pre[rs, :]
                sg = sigmoid(p)
                k.n[rs, 0:256] = (p * sg).astype(BF)
                k.n[rs, 256:512] = (dotr(d, k.wout[...]) * (sg * (1.0 + p * (1.0 - sg)))).astype(BF)

            row_loop(rows)
            k.gs[:, 0:8, :] = dotl(k.n[:, 256:512], frames[:, 0:512]).reshape(32, 8, 512)
            k.gs[:, 8:16, 0:128] = dotl(k.n[:, 256:512], frames[:, 512:640]).reshape(32, 8, 128)
            k.gs[:, 8:16, 128:512] = jnp.zeros((32, 8, 384), F32)
            k.gs[:, 16:24, :] = dotl(k.n[:, 0:256], k.d[...]).reshape(32, 8, 512)
            first, second = small[...], jnp.zeros((SMALL, 512), F32)
            for part in k.smalls[:2]:
                first = first + part[...]
            for part in k.smalls[2:]:
                second = second + part[...]
            for number, total in enumerate((first, second)):
                for z in range(4):
                    lanes = slice(128 * z, 128 * z + 128)
                    block = jnp.concatenate([total[0:8, lanes], total[8:16, lanes], jnp.zeros((8, 256), F32)], axis=1)
                    for q in range(4):
                        k.gs[number * 16 + z * 4 + q, 24:32, :] = block
            k.gsb[...] = k.gs[...].astype(BF)
            start_store(k.ids, k.gsb, k.keep, k.send, FEED // 2, FLAT, k.sems.at[4], flat=True)
            wait_store(k.gsb, k.sems.at[4])
        wait_store(k.gf, k.sems.at[3])

    rows = FEED // 2 + (0 if stem is None else FLAT)
    ins = dict(
        ids=(ids, SMEM),
        bufs=(bufs, ANY),
        prm=(prm, LATE),
        dx1=(dx1, LATE),
        x0=(x0, LATE),
        hid=(hid, LATE),
    )
    scratch = dict(FEED_SCRATCH)
    if stem is not None:
        pre, wout, frames, smalls = stem
        ins |= dict(pre=(pre, LATE), wout=(wout, VMEM), frames=(frames, LATE), smalls=(smalls, VMEM))
        scratch |= dict(gs=((32, FLAT, 512), F32), gsb=WH)
    return run(
        early,
        13 if stem is not None else 10,
        ins,
        dict(
            ig=(ROWS, F32, LATE),
            small=((SMALL, 512), F32, LATE),
            keep=((16, rows, 512), BF, ANY),
            send=((16, rows, 512), BF, ANY),
        ),
        scratch,
    )


def kernel_outputs(ids, head_bufs, sent_first, sent_second, other, allowed, lengths):
    def outputs(k):
        start_load(k.ids, k.hbufs, FEED // 2, FLAT, k.wh, k.sems.at[0], flat=True)
        for sec in range(2):

            @pl.when(k.ids[5] == sec)
            def _():
                pltpu.make_async_copy(k.second if sec else k.first, k.sent.at[sec], k.sems.at[1]).start()
                pltpu.make_async_copy(k.other, k.sent.at[1 - sec], k.sems.at[1]).start()

        wait_load(k.sent, k.sems.at[1])
        wait_load(k.wh, k.sems.at[0])
        for batch in range(2):
            permit = k.allowed[batch : batch + 1, :] > 0
            sent = k.sent[batch]
            logits, logsum = head_rows(sent, k.wh[...].reshape(1024, 512), permit)
            ok = row_mask(k.lengths[batch], 0, 512, 1024)
            k.logp.held[batch] = jnp.where(permit, logits - logsum, 0.0) * ok
            k.acts.held[batch] = sent.astype(F32)

    return run(
        outputs,
        9,
        dict(
            ids=(ids, SMEM),
            lengths=(lengths, SMEM),
            hbufs=(head_bufs, ANY),
            first=(sent_first, ANY),
            second=(sent_second, ANY),
            other=(other, ANY),
            allowed=(allowed, VMEM),
        ),
        dict(logp=((2, 512, 1024), F32, LATE), acts=((2, 512, 512), F32, LATE)),
        dict(wh=WH, sent=((2, 512, 512), BF)),
    )


def kernel_grads(ids, first, second, other):
    def grads(k):
        sec = k.ids[5]
        k.out.held[1 - sec] = k.other[...].astype(F32)

        @pl.when(sec == 0)
        def _():
            k.out.held[0] = k.first[...]

        @pl.when(sec != 0)
        def _():
            k.out.held[1] = k.second[...]

    return run(
        grads,
        3,
        dict(ids=(ids, SMEM), first=(first, VMEM), second=(second, VMEM), other=(other, VMEM)),
        dict(out=((2, 512, 512), F32, LATE)),
        dict(),
    ).out


def pack_feed(w_in, w_out):
    return jnp.concatenate([w_in.reshape(32, 4, 512).transpose(1, 0, 2).reshape(128, 512), w_out])


def pack_attn(w_in, w_out):
    return jnp.concatenate([w_in.reshape(32, 3, 512).transpose(1, 0, 2).reshape(96, 512), w_out])


def pack_conv(w_in, w_out):
    return jnp.concatenate([w_in.reshape(32, 2, 512).transpose(1, 0, 2).reshape(64, 512), w_out])


def unpack_in(rows, blocks):
    return rows[: 32 * blocks].reshape(blocks, 32, 512).transpose(1, 0, 2).reshape(32, 512 * blocks)


def pack_stem(stem_in, stem_out, depth, gains, quarter):
    turned = stem_in.T
    small = jnp.concatenate([depth, gains, jnp.zeros((1, 32), depth.dtype)])
    spread = lax.dynamic_update_slice(jnp.zeros((16, 128), depth.dtype), small, (0, 32 * quarter))
    return jnp.concatenate(
        [
            turned[:, :512],
            jnp.pad(turned[:, 512:], ((0, 0), (0, 384))),
            stem_out,
            jnp.concatenate([spread[:8], spread[8:], jnp.zeros((8, 256), depth.dtype)], axis=1),
        ]
    )


def unpack_stem(rows, quarter):
    turned = jnp.concatenate([rows[0:8], rows[8:16, :128]], axis=1)
    spread = jnp.concatenate([rows[24:32, 0:128], rows[24:32, 128:256]])
    small = lax.dynamic_slice(spread, (0, 32 * quarter), (16, 32))
    return turned.T, rows[16:24], small[:TAPS], small[TAPS : TAPS + 6]


def permutation(target):
    pairs = []
    for x in range(2):
        for d in range(16):
            tx, tz, ty, tc = target(x, d // 4, (d // 2) % 2, d % 2)
            pairs.append((x * 16 + d, tx * 16 + tz * 4 + ty * 2 + tc))
    return pairs


def across(value, target):
    return lax.ppermute(value, BOTH, permutation(target))


def over_x(value):
    return across(value, lambda x, z, y, c: (1 - x, z, y, c))


def over_core(value):
    return across(value, lambda x, z, y, c: (x, z, y, 1 - c))


def over_z(value, k):
    return across(value, lambda x, z, y, c: (x, z ^ k, y, c))


def over_a(value):
    return across(value, lambda x, z, y, c: (1 - x, z, y, c) if c == 0 else (x, z, 1 - y, c))


def over_b(value):
    return across(value, lambda x, z, y, c: (1 - x, z, y, c) if c == 1 else (x, z, 1 - y, c))


def fence(*values):
    return lax.optimization_barrier(values)


def z_parts(own):
    return [own] + [over_z(own, k) for k in (1, 2, 3)]


def ab_parts(quad):
    return over_a(quad), over_b(quad)


def core_parts(quad, ra, rb, rab):
    return [quad, rb, ra, rab] + [over_core(v) for v in (quad, rb, ra, rab)]


def add(*values):
    total = values[0].astype(F32)
    for value in values[1:]:
        total = total + value.astype(F32)
    return total


def halves(kept, came):
    cut = kept.shape[0] // 2
    return add(kept[:cut], came[:cut]).astype(BF), add(kept[cut:], came[cut:]).astype(BF)


def quarters(kept, came):
    return [add(kept[k], came[k]).astype(BF) for k in range(4)]


def z_sum(parts):
    return add(parts[0], *[over_z(parts[k], k) for k in (1, 2, 3)])


def pick(first, own, other):
    return jnp.where(first, own, other), jnp.where(first, other, own)


def on_device(fast, *args):
    (spectra, lengths, languages, token_masks, cotangent) = args[:5]
    masters = args[5:]
    sec = lax.axis_index("section")
    dp = lax.axis_index("dp")
    first = sec == 0
    low = [m.astype(BF) for m in masters]
    swap = lambda v: lax.ppermute(v, "section", [(0, 1), (1, 0)])
    cots = cotangent[0, :, 0]
    cot_send = lax.dynamic_index_in_dim(cots, 1 - sec, 0, keepdims=False)
    place = [sec, dp // 4, (dp // 2) % 2, dp % 2] if fast else [sec * 0] * 4
    ids = jnp.stack(place + [lengths[sec, 0], sec]).astype(jnp.int32)
    frames = lax.dynamic_index_in_dim(spectra, sec, 0, keepdims=False).reshape(512, -1)
    allowed_both = jnp.concatenate(
        [lax.dynamic_slice_in_dim(token_masks, languages[m, 0], 1, 0) for m in range(2)]
    ).astype(F32)
    allowed = lax.dynamic_slice_in_dim(allowed_both, sec, 1, 0)
    if fast:
        chunks = [None] * 4
        own_first, rest = own_pieces(low, sec, dp, first)
        early_cot, late_cot = cot_send[:320], cot_send[320:]
        own_first, rest, early_cot = fence(own_first, rest, early_cot)
        z0 = z_parts(own_first)
        own = own_rest(rest, low, sec, first)
        early_cot = swap(early_cot)
        *z0, own[0], early_cot = fence(*z0, own[0], early_cot)
        quad0 = jnp.stack(z0)
        a0, b0 = ab_parts(quad0)
        z1 = z_parts(own[0])
        quad0, a0, b0, own[2], *z1 = fence(quad0, a0, b0, own[2], *z1)
        pair3 = jnp.concatenate([own[2], over_a(own[2])])
        ab0 = over_b(a0)
        core0 = [over_core(v) for v in (quad0, b0, a0)]
        quad1 = jnp.stack(z1)
        quad1, ab0, frames, pair3, *core0 = fence(quad1, ab0, frames, pair3, *core0)
        a1, b1 = ab_parts(quad1)
        chunks[0] = [quad0, b0, a0, ab0] + core0 + [over_core(ab0)]
        *chunks[0], own[1] = fence(*chunks[0], own[1])
        z2 = z_parts(own[1])
    else:
        chunks = gather_plain(low)
        early_cot, late_cot = swap(cot_send[:320]), swap(cot_send[320:])
    ka = kernel_stem_feed(ids, chunks[0], frames)
    prm = ka.prm
    if fast:
        ka.x1, quad1, a1, b1, pair3, *z2 = fence(ka.x1, quad1, a1, b1, pair3, *z2)
        mid3 = over_z(pair3, 2)
        ab1 = over_b(a1)
        core1 = [over_core(v) for v in (quad1, b1, a1)]
        quad2 = jnp.stack(z2)
        ab1, quad2, pair3, mid3, *core1 = fence(ab1, quad2, pair3, mid3, *core1)
        a2, b2 = ab_parts(quad2)
        chunks[1] = [quad1, b1, a1, ab1] + core1 + [over_core(ab1)]
        *chunks[1], pair3 = fence(*chunks[1], pair3)
        far3, near3 = over_z(pair3, 3), over_z(pair3, 1)
    kb = kernel_rest_first(ids, chunks[1], prm, ka.x1)
    if fast:
        kb.sent, quad2, a2, b2, near3, far3, pair3 = fence(kb.sent, quad2, a2, b2, near3, far3, pair3)
        ab2 = over_b(a2)
        oct3 = jnp.stack([pair3, near3, mid3, far3])
        core2 = [over_core(v) for v in (quad2, b2, a2)]
        ab2, oct3, late_cot, *core2 = fence(ab2, oct3, late_cot, *core2)
        b3 = over_b(oct3)
        late_cot = swap(late_cot)
        chunks[2] = [quad2, b2, a2, ab2] + core2 + [over_core(ab2)]
        chunks[2] = list(fence(*chunks[2]))
        core3 = over_core(oct3)
    kc = kernel_first_second(ids, chunks[2], prm, kb.sent)
    if fast:
        kc.x3, oct3, b3, core3, late_cot = fence(kc.x3, oct3, b3, core3, late_cot)
        chunks[3] = [oct3, b3, core3, over_core(b3)]
    cot_other = [early_cot, late_cot]
    kd = kernel_turn(ids, chunks[3], prm, kc.x3, cots, cot_other, allowed)
    other_sent = swap(jnp.where(first, kd.sent, kb.sent))
    came = [None] * 6
    near, far, parts = [None] * 6, [None] * 6, [None] * 6

    def begin(n, kernel):
        near[n], far[n] = halves(kernel.keep, over_core(kernel.send))
        came[n] = over_a(far[n])

    def go_on(n):
        near[n], far[n] = halves(near[n], came[n])
        came[n] = over_b(far[n])

    def gather_parts(n):
        parts[n] = quarters(near[n], came[n])

    if fast:
        begin(0, kd)
    ke = kernel_mid(1, ids, chunks[2], FEED // 2, prm, kd.dx3, kc.x2, kc.gated, kc.deep, kc.x1, kc.qkv, kc.ls, kc.mixed)
    if fast:
        came[0], other_sent, ke.send, ke.dx1 = fence(came[0], other_sent, ke.send, ke.dx1)
        go_on(0)
        begin(1, ke)
    kf = kernel_early(1, ids, chunks[2], 0, prm, ke.dx1, kb.sent, kc.hid, None)
    if fast:
        came[0], came[1], kf.send, kf.ig = fence(came[0], came[1], kf.send, kf.ig)
        gather_parts(0)
        go_on(1)
        begin(2, kf)
    kg = kernel_late(
        ids, chunks[1], chunks[3], prm, kb.x4, kb.sent, cots, cot_other, allowed, kf.ig, kb.x3, kb.hid, kd.ghead
    )
    if fast:
        came[1], came[2], kg.send, kg.dx3 = fence(came[1], came[2], kg.send, kg.dx3)
        gather_parts(1)
        go_on(2)
        begin(3, kg)
        sums_a = z_sum([jnp.concatenate([p, q]) for p, q in zip(parts[0], parts[1])])
    kh = kernel_mid(0, ids, chunks[1], 0, prm, kg.dx3, kb.x2, kb.gated, kb.deep, ka.x1, kb.qkv, kb.ls, kb.mixed)
    if fast:
        came[2], came[3], sums_a, kh.send, kh.dx1 = fence(came[2], came[3], sums_a, kh.send, kh.dx1)
        gather_parts(2)
        go_on(3)
        begin(4, kh)
        sum_2 = z_sum(parts[2])
    stem = (ka.pre, ka.wout, frames, [kg.small, kh.small, kd.small, ke.small, kf.small])
    ki = kernel_early(0, ids, chunks[0], FLAT, prm, kh.dx1, ka.x0, ka.hid, stem)
    if fast:
        came[3], came[4], sum_2, ki.send, ki.ig, other_sent = fence(came[3], came[4], sum_2, ki.send, ki.ig, other_sent)
        gather_parts(3)
        go_on(4)
        begin(5, ki)
        sum_3 = z_sum(parts[3])
    ko = kernel_outputs(ids, chunks[3], kb.sent, kd.sent, other_sent, allowed_both, lengths[:, 0])
    if fast:
        came[4], came[5], sum_3, ki.ig, ko.acts, ko.logp = fence(came[4], came[5], sum_3, ki.ig, ko.acts, ko.logp)
        gather_parts(4)
        go_on(5)
        sum_4 = z_sum(parts[4])
        late = join(sum_3[: FEED // 2], sums_a[: FEED // 2], first).reshape(FEED, 512)
        head = sum_3[FEED // 2 :].T
        came[5], sum_4, ki.ig, late, head = fence(came[5], sum_4, ki.ig, late, head)
        gather_parts(5)
        sum_5 = z_sum(parts[5])
        late_in, late_out = unpack_in(late, 4), late[128:]
    other_grad = swap(jnp.where(first, kf.ig, ki.ig).astype(BF))
    if fast:
        sum_5, other_grad, late_in, late_out = fence(sum_5, other_grad, late_in, late_out)
        shards = all_shards(late_in, late_out, head, sums_a, sum_2, sum_4, sum_5, dp, first)
    else:
        shards = reduce_plain([(k.keep, k.send) for k in (kd, ke, kf, kg, kh, ki)])
    input_grads = kernel_grads(ids, ki.ig, kf.ig, other_grad)[None, :, None]
    activations = ko.acts[None, :, None]
    log_probs = ko.logp[None, :, None]
    return (activations, log_probs, input_grads, *shards)


def own_half(both, sec, first):
    mine = lax.dynamic_index_in_dim(both, sec, 0, keepdims=False)
    theirs = over_x(lax.dynamic_index_in_dim(both, 1 - sec, 0, keepdims=False))
    return pick(first, mine, theirs)


def own_pieces(low, sec, dp, first):
    feed_in, feed_out = low[:2]
    stem = pack_stem(low[8], low[9], low[5][0], low[7][0], dp % 4)
    feed_first, feed_second = own_half(pack_feed(feed_in[0, 0], feed_out[0, 0]).reshape(2, FEED // 2, 512), sec, first)
    return jnp.concatenate([stem, feed_first]), feed_second


def own_rest(feed_second, low, sec, first):
    feed_in, feed_out, attend_in, attend_out, conv_in, _, conv_out = low[:7]
    feed = pack_feed(feed_in[0, 1], feed_out[0, 1]).reshape(2, FEED // 2, 512)
    attn = pack_attn(attend_in[0], attend_out[0]).reshape(2, ATTN // 2, 512)
    conv = pack_conv(conv_in[0], conv_out[0]).reshape(2, CONV // 2, 512)
    rest_first, rest_second = own_half(jnp.concatenate([attn, conv, feed], axis=1), sec, first)
    return [
        rest_first,
        jnp.concatenate([feed_second, rest_second[:LATE_ROWS]]),
        jnp.concatenate([rest_second[LATE_ROWS:], low[10].T]),
    ]


def join(of_first, of_second, first):
    own = jnp.where(first, of_first, of_second)
    other = over_x(jnp.where(first, of_second, of_first).astype(BF)).astype(F32)
    return jnp.stack(pick(first, own, other))


def all_shards(late_in, late_out, head, sums_a, sum_2, sum_4, sum_5, dp, first):
    half = FEED // 2
    both = join(jnp.concatenate([sum_4, sum_5[:half]]), jnp.concatenate([sums_a[half:], sum_2]), first)
    attn = both[:, : ATTN // 2].reshape(ATTN, 512)
    conv = both[:, ATTN // 2 : LATE_ROWS].reshape(CONV, 512)
    early = both[:, LATE_ROWS:].reshape(FEED, 512)
    g_stem_in, g_stem_out, g_depth, g_gains = unpack_stem(sum_5[half:], dp % 4)
    return (
        jnp.stack([unpack_in(early, 4), late_in])[None],
        jnp.stack([early[128:], late_out])[None],
        unpack_in(attn, 3)[None],
        attn[96:][None],
        unpack_in(conv, 2)[None],
        g_depth[None],
        conv[64:][None],
        g_gains[None],
        g_stem_in,
        g_stem_out,
        head,
    )


def spread_order():
    order = []
    for cr, a, b, zk in pieces():
        px, py = (b, a) if cr else (a, b)
        order.append(px * 16 + zk * 4 + py * 2 + cr)
    return order


def gather_plain(low):
    axes = (2, 2, 1, 1, 1, 2, 1, 2)
    whole = []
    for weight, axis in zip(low[:8], axes):
        axis = 2 if weight.ndim == 4 else axis
        part = lax.all_gather(weight[0], "dp", axis=axis - 1, tiled=True)
        whole.append(lax.all_gather(part, "section", axis=0))
    feed_in, feed_out, attend_in, attend_out, conv_in, depth, conv_out, gains = whole
    stem_in = lax.all_gather(low[8], BOTH, axis=1, tiled=True)
    stem_out = lax.all_gather(low[9], BOTH, axis=0, tiled=True)
    head = lax.all_gather(low[10], BOTH, axis=1, tiled=True)
    order = spread_order()

    def layer(l):
        rows = lambda w, n: w.reshape(16, n, w.shape[-1])
        feeds = [jax.vmap(pack_feed)(rows(feed_in[l, j], 32), rows(feed_out[l, j], 128)) for j in range(2)]
        attn = jax.vmap(pack_attn)(rows(attend_in[l], 32), rows(attend_out[l], 32))
        conv = jax.vmap(pack_conv)(rows(conv_in[l], 32), rows(conv_out[l], 32))
        cut = lambda w: w.reshape(16, 2, w.shape[1] // 2, 512).transpose(1, 0, 2, 3).reshape(32, w.shape[1] // 2, 512)
        return [cut(w) for w in (feeds[0], attn, conv, feeds[1])]

    one, two = layer(0), layer(1)
    columns = lambda w, n: w.reshape(*w.shape[:-1], n, w.shape[-1] // n)
    small = lambda w: jnp.moveaxis(columns(w, 16), 2, 1).reshape(32, w.shape[1], 32)
    stem = jax.vmap(pack_stem)(
        jnp.moveaxis(columns(stem_in, 32), 1, 0),
        stem_out.reshape(32, 8, 512),
        small(depth),
        small(gains),
        jnp.arange(32) % 4,
    )
    head = head.T.reshape(32, 32, 512)
    chunks = ([stem, one[0]], one[1:], [two[0], two[1], two[2]], [two[3], head])
    placed = []
    for parts in chunks:
        joined = jnp.concatenate(parts, axis=1)
        placed.append([jnp.stack([joined[p] for p in order[4 * i : 4 * i + 4]]) for i in range(8)])
    return placed


def reduce_plain(grads):
    order = spread_order()
    place = [order.index(p) for p in range(32)]
    chunks = []
    for keep, send in grads:
        both = jnp.concatenate([keep, send])
        chunks.append(jnp.stack([both[q] for q in place]).astype(F32))
    half = FEED // 2
    whole = []
    for late, mid, early in (chunks[3:], chunks[:3]):
        glue = lambda part, begin, rows: (
            part[:, begin : begin + rows].reshape(2, 16, rows, 512).transpose(1, 0, 2, 3).reshape(16, 2 * rows, 512)
        )
        feeds = [glue(early, 0, half), glue(late, 0, half)]
        attn, conv = glue(mid, 0, ATTN // 2), glue(mid, ATTN // 2, CONV // 2)
        spread = lambda w, n: jax.vmap(lambda rows: unpack_in(rows, n))(w).reshape(512, 512 * n)
        whole.append(
            (
                jnp.stack([spread(f, 4) for f in feeds]),
                jnp.stack([f[:, 128:].reshape(FF, 512) for f in feeds]),
                spread(attn, 3),
                attn[:, 96:].reshape(512, 512),
                spread(conv, 2),
                conv[:, 64:].reshape(512, 512),
            )
        )
    head = chunks[3][:, half:].reshape(1024, 512).T
    g_stem_in, g_stem_out, g_depth, g_gains = jax.vmap(unpack_stem)(chunks[5][:, half:], jnp.arange(32) % 4)
    g_stem_in = jnp.moveaxis(g_stem_in, 0, 1).reshape(640, 256)
    g_stem_out = g_stem_out.reshape(256, 512)
    lanes = lambda w: jnp.moveaxis(w.reshape(2, 16, w.shape[1], 32), 1, 2).reshape(2, w.shape[1], 512)
    g_depth, g_gains = lanes(g_depth), lanes(g_gains)
    stacked = [jnp.stack([whole[0][i], whole[1][i]]) for i in range(6)]

    def shard(value, axis):
        value = lax.psum_scatter(value, "section", scatter_dimension=0, tiled=True)
        return lax.psum_scatter(value, "dp", scatter_dimension=axis, tiled=True)

    return (
        shard(stacked[0], 2),
        shard(stacked[1], 2),
        shard(stacked[2], 1),
        shard(stacked[3], 1),
        shard(stacked[4], 1),
        shard(g_depth, 2),
        shard(stacked[5], 1),
        shard(g_gains, 2),
        lax.psum_scatter(g_stem_in, BOTH, scatter_dimension=1, tiled=True),
        lax.psum_scatter(g_stem_out, BOTH, scatter_dimension=0, tiled=True),
        lax.psum_scatter(head, BOTH, scatter_dimension=1, tiled=True),
    )


def solution(mesh):
    fast = dict(mesh.shape) == {"section": 2, "dp": 16}

    def body(*args):
        return on_device(fast, *args)

    layer_specs = (
        P("section", None, "dp", None),
        P("section", None, "dp", None),
        P("section", "dp", None),
        P("section", "dp", None),
        P("section", "dp", None),
        P("section", None, "dp"),
        P("section", "dp", None),
        P("section", None, "dp"),
        P(None, BOTH),
        P(BOTH, None),
        P(None, BOTH),
    )
    rows = P("section", None, "dp", None, None)
    return jax.shard_map(
        body,
        mesh=mesh,
        in_specs=(P(None, "dp", None, None), P(None, "dp"), P(None, "dp"), P(), rows) + layer_specs,
        out_specs=(rows, rows, rows) + layer_specs,
        check_vma=False,
    )
```

```python
import types

import jax
import jax.numpy as jnp
from jax import lax
from jax.experimental import pallas as pl
from jax.experimental.pallas import tpu as pltpu
from jax.sharding import PartitionSpec as P

D = 512
HEADS = 8
HDIM = 64
FF = 2048
TAPS = 9
EPS = 1e-05
MASKED = -1e30
RB = 512
BOTH = ("section", "dp")
BF = jnp.bfloat16
F32 = jnp.float32

FEED, ATTN, CONV = 256, 128, 96
FLAT = 32
SMALL = 16


def dotn(a, b):
    return lax.dot_general(a, b, (((1,), (0,)), ((), ())), preferred_element_type=F32)


def dotr(a, b):
    return lax.dot_general(a, b, (((1,), (1,)), ((), ())), preferred_element_type=F32)


def dotl(a, b):
    return lax.dot_general(a, b, (((0,), (0,)), ((), ())), preferred_element_type=F32)


def sigmoid(v):
    return 0.5 * jnp.tanh(0.5 * v) + 0.5


def unit_rows(v):
    c = v - jnp.mean(v, axis=-1, keepdims=True)
    r = lax.rsqrt(jnp.mean(c * c, axis=-1, keepdims=True) + EPS)
    return c * r, r


def unit_back(dn, u, r, gain):
    du = dn * gain
    dv = r * (du - jnp.mean(du, axis=-1, keepdims=True) - u * jnp.mean(du * u, axis=-1, keepdims=True))
    return dv, jnp.sum(dn * u, axis=0, keepdims=True)


def row_mask(length, start, rows, columns):
    return (lax.broadcasted_iota(jnp.int32, (rows, columns), 0) + start < length).astype(F32)


def row_loop(body):
    for i in range(512 // RB):
        body(slice(i * RB, i * RB + RB), i * RB)


def piece_of(ids, cr, a, b, zk):
    pc = ids[3] ^ cr
    px = ids[0] ^ (a + pc * (b - a))
    py = ids[2] ^ (b + pc * (a - b))
    pz = ids[1] ^ zk
    return px, pz * 4 + py * 2 + pc


def pieces():
    return [(cr, a, b, zk) for cr in range(2) for a in range(2) for b in range(2) for zk in range(4)]


def start_load(ids, bufs, row, rows, scr, sem, flat=False):
    for cr, a, b, zk in pieces():
        px, d = piece_of(ids, cr, a, b, zk)
        if len(bufs) == 4:
            begin = row + a * (bufs[0].shape[1] // 2)
            src = bufs[cr * 2 + b].at[zk, begin : begin + rows]
        else:
            src = bufs[cr * 4 + a * 2 + b].at[zk, row : row + rows]
        if flat:
            dst = scr.at[px * 16 + d]
        else:
            dst = scr.at[d, pl.ds(pl.multiple_of(px * rows, 16), rows)]
        pltpu.make_async_copy(src, dst, sem).start()


def wait_load(scr, sem):
    pltpu.make_async_copy(scr, scr, sem).wait()


def start_store(ids, scr, keep, send, row, rows, sem, flat=False):
    for cr, a, b, zk in pieces():
        px, d = piece_of(ids, cr, a, b, zk)
        if flat:
            src = scr.at[px * 16 + d]
        else:
            src = scr.at[d, pl.ds(pl.multiple_of(px * rows, 16), rows)]
        dst = (send if cr else keep).at[a * 8 + b * 4 + zk, row : row + rows]
        pltpu.make_async_copy(src, dst, sem).start()


def start_piece(ids, scr, keep, send, row, rows, sem, px, d):
    pz, py, pc = d // 4, (d // 2) % 2, d % 2
    xr, yr, zk, cr = px ^ ids[0], py ^ ids[2], pz ^ ids[1], pc ^ ids[3]
    a, b = (yr, xr) if pc else (xr, yr)
    src = scr.at[d, px * rows : px * rows + rows]
    for side, target in enumerate((keep, send)):

        @pl.when(cr == side)
        def _():
            pltpu.make_async_copy(src, target.at[a * 8 + b * 4 + zk, row : row + rows], sem).start()


def wait_store(scr, sem):
    pltpu.make_async_copy(scr, scr, sem).wait()


def in_block(w, j):
    return w[:, 32 * j : 32 * j + 32, :].reshape(512, 512)


def out_block(w, j):
    return w[4 * j : 4 * j + 4, 128:256, :].reshape(512, 512)


def feed_fwd(x, w, gain, hid, out):
    def body(rs, start):
        v = x[rs, :].astype(F32)
        u, _ = unit_rows(v)
        n = (u * gain).astype(BF)
        total = jnp.zeros((RB, 512), F32)
        for j in range(4):
            h = dotn(n, in_block(w, j))
            hid[rs, 512 * j : 512 * j + 512] = h.astype(BF)
            total = total + dotn((h * sigmoid(h)).astype(BF), out_block(w, j))
        out[rs, :] = v + 0.5 * total

    row_loop(body)


def feed_bwd(dx, x, hid, w, gain, result, gw, small, row, s):
    def body(rs, start):
        g = dx[rs, :]
        v = x[rs, :].astype(F32)
        u, r = unit_rows(v)
        s.n[rs, :] = (u * gain).astype(BF)
        d = (0.5 * g).astype(BF)
        s.d[rs, :] = d
        dn = jnp.zeros((RB, 512), F32)
        for j in range(4):
            h = hid[rs, 512 * j : 512 * j + 512].astype(F32)
            sg = sigmoid(h)
            s.act[rs, 512 * j : 512 * j + 512] = (h * sg).astype(BF)
            dh = (dotr(d, out_block(w, j)) * (sg * (1.0 + h * (1.0 - sg)))).astype(BF)
            s.dh[rs, 512 * j : 512 * j + 512] = dh
            dn = dn + dotr(dh, in_block(w, j))
        dv, gg = unit_back(dn, u, r, gain)
        result.held[rs, :] = g + dv
        small[row : row + 1, :] += gg

    row_loop(body)
    result.go()
    for j in range(4):
        cols = slice(512 * j, 512 * j + 512)
        gw[4 * j : 4 * j + 4, 128:256, :] = dotl(s.act[:, cols], s.d[...]).astype(BF).reshape(4, 128, 512)
        for d in range(4 * j, 4 * j + 4):
            start_piece(s.ids, gw, s.keep, s.send, 0, FEED // 2, s.sems.at[3], 1, d)
    for j in range(4):
        cols = slice(512 * j, 512 * j + 512)
        gw[:, 32 * j : 32 * j + 32, :] = dotl(s.n[...], s.dh[:, cols]).astype(BF).reshape(16, 32, 512)
    for d in range(16):
        start_piece(s.ids, gw, s.keep, s.send, 0, FEED // 2, s.sems.at[3], 0, d)


def lanes_of(half, axis=1, count=1):
    shape = (count, 128) if axis else (128, count)
    return (lax.broadcasted_iota(jnp.int32, shape, axis) + 64 * half) % 128 - 64


def attn_fwd(x, w, gain, length, qkv, ls, mixt, out):
    def project(rs, start):
        u, _ = unit_rows(x[rs, :])
        n = (u * gain).astype(BF)
        for j in range(3):
            qkv[rs, 512 * j : 512 * j + 512] = dotn(n, in_block(w, j)).astype(BF)

    row_loop(project)

    for hp in range(4):
        at = hp * 128
        k = qkv[:, pl.ds(512 + at, 128)].astype(F32)
        vt = qkv[:, pl.ds(1024 + at, 128)].astype(F32).T
        outside = jnp.where(lax.broadcasted_iota(jnp.int32, (512, 128), 0) < length, 0.0, MASKED)
        kx, vx = [], []
        for hh in range(2):
            free = lanes_of(hh)
            kx.append(jnp.where(free < 0, k, jnp.where(free == 0, outside, 0.0)).astype(BF))
            free = lanes_of(hh, 0, 512)
            vx.append(jnp.where(free < 0, vt, jnp.where(free == 0, 1.0, 0.0)).astype(BF))

        def body(rs, start):
            q = qkv[rs, pl.ds(at, 128)].astype(F32) * HDIM**-0.5
            parts = []
            for hh in range(2):
                free = lanes_of(hh)
                qx = jnp.where(free < 0, q, jnp.where(free == 0, 1.0, 0.0)).astype(BF)
                sc = dotr(kx[hh], qx)
                top = jnp.max(sc, axis=0, keepdims=True)
                both = dotn(vx[hh], jnp.exp(sc - top).astype(BF))
                tot = both[64 * (1 - hh) : 64 * (1 - hh) + 1, :]
                parts.append(both * (1.0 / tot))
                ls[pl.ds(hp * 2 + hh, 1), rs] = top + jnp.log(tot)
            mixt[pl.ds(at, 128), rs] = jnp.where(lanes_of(0, 0, RB) < 0, parts[0], parts[1]).astype(BF)

        row_loop(body)

    def project_out(rs, start):
        out[rs, :] = x[rs, :] + dotl(mixt[:, rs], w[:, 96:128, :].reshape(512, 512))

    row_loop(project_out)


def attn_bwd(dx, x, qkv, ls, mixt, w, gain, length, out, gw, small, row, s):
    def first(rs, start):
        u, _ = unit_rows(x[rs, :])
        s.n[rs, :] = (u * gain).astype(BF)
        d = dx[rs, :].astype(BF)
        s.d[rs, :] = d
        s.dm[:, rs] = dotr(w[:, 96:128, :].reshape(512, 512), d).astype(BF)

    row_loop(first)
    gw[:, 96:128, :] = dotn(mixt[...], s.d[...]).astype(BF).reshape(16, 32, 512)

    for hp in range(4):
        at = hp * 128
        s.dq[...] = jnp.zeros((128, 512), F32)
        q = qkv[:, pl.ds(at, 128)].astype(F32) * HDIM**-0.5
        kt = qkv[:, pl.ds(512 + at, 128)].astype(F32).T * HDIM**-0.5
        dmt = s.dm[pl.ds(at, 128), :].astype(F32)
        prod = dmt * mixt[pl.ds(at, 128), :].astype(F32)
        qx, qs, dms, deltas, sums = [], [], [], [], []
        for hh in range(2):
            free = lanes_of(hh)
            qs.append(jnp.where(free < 0, q, 0.0).astype(BF))
            qx.append(jnp.where(free < 0, q, jnp.where(free == 0, 1.0, 0.0)).astype(BF))
            free = lanes_of(hh, 0, 512)
            dms.append(jnp.where(free < 0, dmt, 0.0).astype(BF))
            deltas.append(jnp.sum(prod[64 * hh : 64 * hh + 64, :], axis=0, keepdims=True))
            s.kt[128 * hh : 128 * hh + 128, :] = jnp.where(free < 0, kt, 0.0).astype(BF)
            sums.append(ls[pl.ds(hp * 2 + hh, 1), :])

        def body(rs, start):
            k = qkv[rs, pl.ds(512 + at, 128)].astype(F32)
            v = qkv[rs, pl.ds(1024 + at, 128)]
            outside = jnp.where(lax.broadcasted_iota(jnp.int32, (RB, 128), 0) + start < length, 0.0, MASKED)
            dk = jnp.zeros((RB, 128), F32)
            dv = jnp.zeros((RB, 128), F32)
            for hh in range(2):
                free = lanes_of(hh)
                kx = jnp.where(free < 0, k, jnp.where(free == 0, outside, 0.0)).astype(BF)
                p = jnp.exp(dotr(kx, qx[hh]) - sums[hh])
                ds = (p * (dotn(v, dms[hh]) - deltas[hh])).astype(BF)
                dv = dv + dotr(p.astype(BF), dms[hh])
                dk = dk + dotn(ds, qs[hh])
                s.dq[...] += dotn(s.kt[128 * hh : 128 * hh + 128, rs], ds)
            s.dpk[rs, pl.ds(512 + at, 128)] = dk.astype(BF)
            s.dpk[rs, pl.ds(1024 + at, 128)] = dv.astype(BF)

        row_loop(body)
        s.dpk[:, pl.ds(at, 128)] = s.dq[...].T.astype(BF)

    def last(rs, start):
        u, r = unit_rows(x[rs, :])
        dn = jnp.zeros((RB, 512), F32)
        for j in range(3):
            dn = dn + dotr(s.dpk[rs, 512 * j : 512 * j + 512], in_block(w, j))
        dv, gg = unit_back(dn, u, r, gain)
        out[rs, :] = dx[rs, :] + dv
        small[row : row + 1, :] += gg

    row_loop(last)
    for j in range(3):
        gw[:, 32 * j : 32 * j + 32, :] = (
            dotl(s.n[...], s.dpk[:, 512 * j : 512 * j + 512]).astype(BF).reshape(16, 32, 512)
        )


PAD = 8


def conv_fwd(x, w, prm, length, gated, deep, out, pad):
    pad[0:PAD, :] = jnp.zeros((PAD, 512), F32)
    pad[PAD + 512 : 2 * PAD + 512, :] = jnp.zeros((PAD, 512), F32)

    def first(rs, start):
        u, _ = unit_rows(x[rs, :])
        n = (u * prm[TAPS + 2 : TAPS + 3, :]).astype(BF)
        a = dotn(n, in_block(w, 0))
        b = dotn(n, in_block(w, 1))
        gated[rs, 0:512] = a
        gated[rs, 512:1024] = b
        pad[pl.ds(start + PAD, RB), :] = a * sigmoid(b) * row_mask(length, start, RB, 512)

    row_loop(first)
    for i in range(512 // RB):
        total = jnp.zeros((RB, 512), F32)
        for t in range(TAPS):
            begin = i * RB + PAD - TAPS // 2 + t
            total = total + prm[t : t + 1, :] * pad[begin : begin + RB, :]
        deep[i * RB : i * RB + RB, :] = total

    def last(rs, start):
        u, _ = unit_rows(deep[rs, :])
        m = u * prm[TAPS + 3 : TAPS + 4, :]
        act = (m * sigmoid(m)).astype(BF)
        out[rs, :] = x[rs, :] + dotn(act, w[:, 64:96, :].reshape(512, 512))

    row_loop(last)


def conv_bwd(dx, x, gated, deep, w, prm, length, out, gw, small, s):
    s.back[0:PAD, :] = jnp.zeros((PAD, 512), F32)
    s.back[PAD + 512 : 2 * PAD + 512, :] = jnp.zeros((PAD, 512), F32)
    gain_in = prm[TAPS + 2 : TAPS + 3, :]
    gain_mid = prm[TAPS + 3 : TAPS + 4, :]

    def first(rs, start):
        padded = pl.ds(start + PAD, RB)
        d = dx[rs, :].astype(BF)
        s.d[rs, :] = d
        u3, r3 = unit_rows(deep[rs, :])
        m = u3 * gain_mid
        sg = sigmoid(m)
        s.act[rs, :] = (m * sg).astype(BF)
        dmid = dotr(d, w[:, 64:96, :].reshape(512, 512)) * (sg * (1.0 + m * (1.0 - sg)))
        ddeep, gg = unit_back(dmid, u3, r3, gain_mid)
        s.back[padded, :] = ddeep
        small[TAPS + 3 : TAPS + 4, :] += gg
        s.glu[rs, :] = (
            gated[rs, 0:512] * sigmoid(gated[rs, 512:1024]) * row_mask(length, start, RB, 512)
        )

    row_loop(first)
    gw[:, 64:96, :] = dotl(s.act[...], s.d[...]).astype(BF).reshape(16, 32, 512)
    for i in range(512 // RB):
        rows = slice(i * RB, i * RB + RB)
        glu = s.glu[rows, :]
        dglu = jnp.zeros((RB, 512), F32)
        for t in range(TAPS):
            begin = i * RB + PAD + TAPS // 2 - t
            later = s.back[begin : begin + RB, :]
            small[t : t + 1, :] += jnp.sum(glu * later, axis=0, keepdims=True)
            dglu = dglu + prm[t : t + 1, :] * later
        dglu = dglu * row_mask(length, i * RB, RB, 512)
        sg = sigmoid(gated[rows, 512:1024])
        ga = dglu * sg
        s.dga[rows, :] = ga.astype(BF)
        s.dgb[rows, :] = (ga * gated[rows, 0:512] * (1.0 - sg)).astype(BF)

    def last(rs, start):
        u, r = unit_rows(x[rs, :])
        s.n[rs, :] = (u * gain_in).astype(BF)
        dn = dotr(s.dga[rs, :], in_block(w, 0)) + dotr(s.dgb[rs, :], in_block(w, 1))
        dv, gg = unit_back(dn, u, r, gain_in)
        out[rs, :] = dx[rs, :] + dv
        small[TAPS + 2 : TAPS + 3, :] += gg

    row_loop(last)
    gw[:, 0:32, :] = dotl(s.n[...], s.dga[...]).astype(BF).reshape(16, 32, 512)
    gw[:, 32:64, :] = dotl(s.n[...], s.dgb[...]).astype(BF).reshape(16, 32, 512)


def finish_fwd(x4, prm, length, sent):
    def body(rs, start):
        u, _ = unit_rows(x4[rs, :])
        sent[rs, :] = (u * prm[TAPS + 5 : TAPS + 6, :] * row_mask(length, start, RB, 512)).astype(BF)

    row_loop(body)


def head_rows(sent, w, permit):
    logits = dotr(sent, w)
    top = jnp.max(jnp.where(permit, logits, MASKED), axis=-1, keepdims=True)
    e = jnp.exp(jnp.where(permit, logits - top, MASKED))
    return logits, top + jnp.log(jnp.sum(e, axis=-1, keepdims=True))


def head_bwd(x4, sent, w, allowed, cot, prm, length, extra, out, gl, small):
    permit = allowed[...] > 0
    gain = prm[TAPS + 5 : TAPS + 6, :]

    def body(rs, start):
        hw = w[...].reshape(1024, 512)
        logits, logsum = head_rows(sent[rs, :], hw, permit)
        weighted = jnp.where(permit, cot[rs, :].astype(F32), 0.0) * row_mask(length, start, RB, 1024)
        probs = jnp.exp(jnp.where(permit, logits - logsum, MASKED))
        g = (weighted - probs * jnp.sum(weighted, axis=-1, keepdims=True)).astype(BF)
        gl[rs, :] = g
        gs = dotn(g, hw)
        if extra is not None:
            gs = gs + extra[rs, :].astype(BF).astype(F32)
        u, r = unit_rows(x4[rs, :])
        dv, gg = unit_back(gs * row_mask(length, start, RB, 512), u, r, gain)
        out[rs, :] = dv
        small[TAPS + 5 : TAPS + 6, :] += gg

    row_loop(body)


ANY, VMEM, SMEM = pl.ANY, pltpu.VMEM, pltpu.SMEM
LATE = object()


class Late:
    def __init__(self, source, held, sem):
        self.copy, self.held, self.going, self.here = pltpu.make_async_copy(source, held, sem), held, False, False

    def go(self):
        self.going = True
        self.copy.start()

    def get(self):
        if not self.going:
            self.go()
        if not self.here:
            self.copy.wait()
        self.here = True
        return self.held


class Soon:
    def __init__(self, held, target, sem):
        self.copy, self.held, self.going = pltpu.make_async_copy(held, target, sem), held, False

    def go(self):
        self.going = True
        self.copy.start()

    def end(self):
        if not self.going:
            self.go()
        self.copy.wait()


def run(body, micros, ins, outs, scratch, room=55):
    flat, held = [], []
    for value, space in ins.values():
        flat += [(array, ANY if space is LATE else space) for array in (value if isinstance(value, list) else [value])]
        if space is LATE:
            held.append((value.shape, value.dtype))
    held += [(shape, dtype) for shape, dtype, space in outs.values() if space is LATE]

    def kernel(*refs):
        left = list(refs)
        ns = types.SimpleNamespace()
        waiting, soon = [], []
        for key, (value, space) in ins.items():
            if isinstance(value, list):
                setattr(ns, key, [left.pop(0) for _ in value])
            else:
                setattr(ns, key, left.pop(0))
        for key in [*outs, *scratch]:
            setattr(ns, key, left.pop(0))
        ns.sems = left.pop()
        number = 8
        for key, (_, space) in ins.items():
            if space is LATE:
                setattr(ns, key, Late(getattr(ns, key), left.pop(0), ns.sems.at[number]))
                number += 1
        for key, (_, _, space) in outs.items():
            if space is LATE:
                soon.append(Soon(left.pop(0), getattr(ns, key), ns.sems.at[number]))
                setattr(ns, key, soon[-1])
                number += 1
        body(ns)
        for result in soon:
            result.end()

    result = pl.pallas_call(
        kernel,
        out_shape=[jax.ShapeDtypeStruct(shape, dtype) for shape, dtype, _ in outs.values()],
        in_specs=[pl.BlockSpec(memory_space=space) for _, space in flat],
        out_specs=[pl.BlockSpec(memory_space=ANY if space is LATE else space) for _, _, space in outs.values()],
        scratch_shapes=[pltpu.VMEM(shape, dtype) for shape, dtype in [*scratch.values(), *held]]
        + [pltpu.SemaphoreType.DMA((8 + len(held),))],
        compiler_params=pltpu.CompilerParams(vmem_limit_bytes=room * 2**20),
        cost_estimate=pl.CostEstimate(flops=int(micros * 1.1e9), bytes_accessed=2**20, transcendentals=0),
        name=body.__name__,
    )(*[array for array, _ in flat])
    return types.SimpleNamespace(**dict(zip(outs, result)))


ROWS = (512, 512)
WF, WA, WC, WH = ((16, FEED, 512), BF), ((16, ATTN, 512), BF), ((16, CONV, 512), BF), ((32, FLAT, 512), BF)
PADDED = ((512 + 2 * PAD, 512), F32)
LATE_ROWS = ATTN // 2 + CONV // 2


def gain_of(prm, number):
    return prm[TAPS + number : TAPS + number + 1, :]


def kernel_stem_feed(ids, bufs, frames):
    def stem_feed(k):
        start_load(k.ids, k.bufs, 0, FLAT, k.stem, k.sems.at[0], flat=True)
        k.frames.go()
        start_load(k.ids, k.bufs, FLAT, FEED // 2, k.w, k.sems.at[1])
        wait_load(k.stem, k.sems.at[0])
        stem = k.stem[...].astype(F32)
        for layer in range(2):
            for z in range(4):
                part = jnp.zeros((8, 512), F32)
                for q in range(4):
                    part = part + stem[layer * 16 + z * 4 + q, 24:32, :]
                k.prm[layer, 0:8, 128 * z : 128 * z + 128] = part[:, 0:128]
                k.prm[layer, 8:16, 128 * z : 128 * z + 128] = part[:, 128:256]
        win_a = stem[:, 0:8, :].reshape(256, 512).astype(BF)
        win_b = stem[:, 8:16, 0:128].reshape(256, 128).astype(BF)
        k.wout[...] = stem[:, 16:24, :].reshape(256, 512).astype(BF)
        frames, x0, x1, hid, pre = k.frames.get(), k.x0.held, k.x1.held, k.hid.held, k.pre.held

        def rows(rs, start):
            p = dotr(frames[rs, 0:512], win_a) + dotr(frames[rs, 512:640], win_b)
            pre[rs, :] = p
            x = dotn((p * sigmoid(p)).astype(BF), k.wout[...])
            x0[rs, :] = (x * row_mask(k.ids[4], start, RB, 512)).astype(BF)

        row_loop(rows)
        k.pre.go()
        k.x0.go()
        wait_load(k.w, k.sems.at[1])
        feed_fwd(x0, k.w, gain_of(k.prm.at[0], 0), hid, x1)

    return run(
        stem_feed,
        9,
        dict(ids=(ids, SMEM), bufs=(bufs, ANY), frames=(frames, LATE)),
        dict(
            prm=((2, SMALL, 512), F32, VMEM),
            pre=((512, 256), F32, LATE),
            wout=((256, 512), BF, VMEM),
            x0=(ROWS, BF, LATE),
            hid=((512, FF), BF, LATE),
            x1=(ROWS, F32, LATE),
        ),
        dict(stem=WH, w=WF),
    )


ATTN_OUTS = dict(qkv=((512, 1536), BF, LATE), ls=((8, 512), F32, VMEM), mixed=(ROWS, BF, LATE), x2=(ROWS, F32, LATE))
CONV_OUTS = dict(gated=((512, 1024), F32, LATE), deep=(ROWS, F32, LATE), x3=(ROWS, F32, LATE))


def attn_conv(k, x1, prm):
    wait_load(k.wa, k.sems.at[0])
    attn_fwd(x1, k.wa, gain_of(prm, 1), k.ids[4], k.qkv.held, k.ls, k.mixed.held, k.x2.held)
    for result in (k.qkv, k.mixed, k.x2):
        result.go()
    wait_load(k.wc, k.sems.at[1])
    conv_fwd(k.x2.held, k.wc, prm, k.ids[4], k.gated.held, k.deep.held, k.x3.held, k.pad)
    for result in (k.gated, k.deep, k.x3):
        result.go()


def kernel_rest_first(ids, bufs, prm, x1):
    def rest_first(k):
        k.x1.go()
        start_load(k.ids, k.bufs, 0, ATTN // 2, k.wa, k.sems.at[0])
        start_load(k.ids, k.bufs, ATTN // 2, CONV // 2, k.wc, k.sems.at[1])
        start_load(k.ids, k.bufs, LATE_ROWS, FEED // 2, k.wf, k.sems.at[2])
        prm = k.prm.at[0]
        attn_conv(k, k.x1.get(), prm)
        wait_load(k.wf, k.sems.at[2])
        feed_fwd(k.x3.held, k.wf, gain_of(prm, 4), k.hid.held, k.x4.held)
        k.hid.go()
        k.x4.go()
        finish_fwd(k.x4.held, prm, k.ids[4], k.sent)

    return run(
        rest_first,
        20,
        dict(ids=(ids, SMEM), bufs=(bufs, ANY), prm=(prm, VMEM), x1=(x1, LATE)),
        ATTN_OUTS | CONV_OUTS | dict(hid=((512, FF), BF, LATE), x4=(ROWS, F32, LATE), sent=(ROWS, BF, VMEM)),
        dict(wa=WA, wc=WC, wf=WF, pad=PADDED),
    )


def kernel_first_second(ids, bufs, prm, x0):
    def first_second(k):
        start_load(k.ids, k.bufs, 0, FEED // 2, k.wf, k.sems.at[2])
        start_load(k.ids, k.bufs, FEED // 2, ATTN // 2, k.wa, k.sems.at[0])
        start_load(k.ids, k.bufs, FEED // 2 + ATTN // 2, CONV // 2, k.wc, k.sems.at[1])
        prm = k.prm.at[1]
        wait_load(k.wf, k.sems.at[2])
        feed_fwd(k.x0, k.wf, gain_of(prm, 0), k.hid.held, k.x1.held)
        k.hid.go()
        k.x1.go()
        attn_conv(k, k.x1.held, prm)

    return run(
        first_second,
        20,
        dict(ids=(ids, SMEM), bufs=(bufs, ANY), prm=(prm, VMEM), x0=(x0, VMEM)),
        dict(hid=((512, FF), BF, LATE), x1=(ROWS, F32, LATE)) | ATTN_OUTS | CONV_OUTS,
        dict(wa=WA, wc=WC, wf=WF, pad=PADDED),
    )


def start_cot(k, layer):
    @pl.when(k.ids[5] == layer)
    def _():
        pltpu.make_async_copy(k.cots.at[k.ids[5]], k.cot, k.sems.at[2]).start()

    @pl.when(k.ids[5] != layer)
    def _():
        at = 0
        for part in k.cot_other:
            pltpu.make_async_copy(part, k.cot.at[at : at + part.shape[0]], k.sems.at[2]).start()
            at += part.shape[0]


FEED_SCRATCH = dict(n=(ROWS, BF), d=(ROWS, BF), act=((512, FF), BF), dh=((512, FF), BF), wf=WF, gf=WF)
HEAD_SCRATCH = dict(wh=WH, cot=((512, 1024), BF), gl=((512, 1024), BF), dx4=(ROWS, F32))


def kernel_turn(ids, bufs, prm, x3, cots, cot_other, allowed):
    def turn(k):
        k.prm.go()
        k.x3.go()
        start_load(k.ids, k.bufs, 0, FEED // 2, k.wf, k.sems.at[0])
        start_load(k.ids, k.bufs, FEED // 2, FLAT, k.wh, k.sems.at[1], flat=True)
        start_cot(k, 1)
        prm = k.prm.get().at[1]
        small = k.small.held
        small[...] = jnp.zeros((SMALL, 512), F32)
        x3 = k.x3.get()
        wait_load(k.wf, k.sems.at[0])
        feed_fwd(x3, k.wf, gain_of(prm, 4), k.hid, k.x4)
        finish_fwd(k.x4, prm, k.ids[4], k.sent)
        wait_load(k.wh, k.sems.at[1])
        wait_load(k.cot, k.sems.at[2])
        head_bwd(k.x4, k.sent, k.wh, k.allowed, k.cot, prm, k.ids[4], None, k.dx4, k.gl, small)
        k.ghead.held[...] = dotl(k.gl[...], k.sent[...])
        k.ghead.go()
        feed_bwd(k.dx4, x3, k.hid, k.wf, gain_of(prm, 4), k.dx3, k.gf, small, TAPS + 4, k)
        wait_store(k.gf, k.sems.at[3])

    rows = FEED // 2
    return run(
        turn,
        22,
        dict(
            ids=(ids, SMEM),
            bufs=(bufs, ANY),
            prm=(prm, LATE),
            x3=(x3, LATE),
            cots=(cots, ANY),
            cot_other=(cot_other, ANY),
            allowed=(allowed, VMEM),
        ),
        dict(
            sent=(ROWS, BF, VMEM),
            ghead=((1024, 512), F32, LATE),
            dx3=(ROWS, F32, LATE),
            small=((SMALL, 512), F32, LATE),
            keep=((16, rows, 512), BF, ANY),
            send=((16, rows, 512), BF, ANY),
        ),
        FEED_SCRATCH | HEAD_SCRATCH | dict(hid=((512, FF), BF), x4=(ROWS, F32)),
        room=52,
    )


def kernel_late(ids, bufs, head_bufs, prm, x4, sent, cots, cot_other, allowed, ig, x3, hid, ghead):
    def late(k):
        start_load(k.ids, k.hbufs, FEED // 2, FLAT, k.wh, k.sems.at[1], flat=True)
        start_cot(k, 0)
        for operand in (k.prm, k.x4, k.sent, k.ig):
            operand.go()
        start_load(k.ids, k.bufs, LATE_ROWS, FEED // 2, k.wf, k.sems.at[0])
        for operand in (k.ghead, k.x3, k.hid):
            operand.go()
        prm = k.prm.get().at[0]
        small = k.small.held
        small[...] = jnp.zeros((SMALL, 512), F32)
        wait_load(k.wh, k.sems.at[1])
        wait_load(k.cot, k.sems.at[2])
        sent = k.sent.get()
        head_bwd(k.x4.get(), sent, k.wh, k.allowed, k.cot, prm, k.ids[4], k.ig.get(), k.dx4, k.gl, small)
        k.gh[...] = (k.ghead.get()[...] + dotl(k.gl[...], sent[...])).astype(BF).reshape(32, FLAT, 512)
        start_store(k.ids, k.gh, k.keep, k.send, FEED // 2, FLAT, k.sems.at[4], flat=True)
        wait_load(k.wf, k.sems.at[0])
        feed_bwd(k.dx4, k.x3.get(), k.hid.get(), k.wf, gain_of(prm, 4), k.dx3, k.gf, small, TAPS + 4, k)
        wait_store(k.gh, k.sems.at[4])
        wait_store(k.gf, k.sems.at[3])

    rows = FEED // 2 + FLAT
    return run(
        late,
        17,
        dict(
            ids=(ids, SMEM),
            bufs=(bufs, ANY),
            hbufs=(head_bufs, ANY),
            prm=(prm, LATE),
            x4=(x4, LATE),
            sent=(sent, LATE),
            cots=(cots, ANY),
            cot_other=(cot_other, ANY),
            allowed=(allowed, VMEM),
            ig=(ig, LATE),
            x3=(x3, LATE),
            hid=(hid, LATE),
            ghead=(ghead, LATE),
        ),
        dict(
            dx3=(ROWS, F32, LATE),
            small=((SMALL, 512), F32, LATE),
            keep=((16, rows, 512), BF, ANY),
            send=((16, rows, 512), BF, ANY),
        ),
        FEED_SCRATCH | HEAD_SCRATCH | dict(gh=WH),
        room=52,
    )


def kernel_mid(layer, ids, bufs, row, prm, dx3, x2, gated, deep, x1, qkv, ls, mixed):
    def mid(k):
        for operand in (k.prm, k.dx3, k.deep):
            operand.go()
        start_load(k.ids, k.bufs, row + ATTN // 2, CONV // 2, k.wc, k.sems.at[1])
        for operand in (k.gated, k.x2):
            operand.go()
        start_load(k.ids, k.bufs, row, ATTN // 2, k.wa, k.sems.at[0])
        for operand in (k.x1, k.mixed, k.qkv, k.ls):
            operand.go()
        prm = k.prm.get().at[layer]
        small = k.small.held
        small[...] = jnp.zeros((SMALL, 512), F32)
        wait_load(k.wc, k.sems.at[1])
        s = types.SimpleNamespace(
            n=k.n, d=k.d, act=k.act.at[:, 0:512], dga=k.dh.at[:, 0:512], dgb=k.dh.at[:, 512:1024], glu=k.glu, back=k.back
        )
        conv_bwd(k.dx3.get(), k.x2.get(), k.gated.get(), k.deep.get(), k.wc, prm, k.ids[4], k.dx2, k.gc, small, s)
        start_store(k.ids, k.gc, k.keep, k.send, ATTN // 2, CONV // 2, k.sems.at[3])
        wait_load(k.wa, k.sems.at[0])
        s = types.SimpleNamespace(n=k.n, d=k.d, dm=k.dm, dpk=k.act, dq=k.dq, kt=k.kt)
        attn_bwd(
            k.dx2, k.x1.get(), k.qkv.get(), k.ls.get(), k.mixed.get(), k.wa, gain_of(prm, 1), k.ids[4], k.dx1.held, k.ga,
            small, TAPS + 1, s,
        )
        start_store(k.ids, k.ga, k.keep, k.send, 0, ATTN // 2, k.sems.at[2])
        wait_store(k.gc, k.sems.at[3])
        wait_store(k.ga, k.sems.at[2])

    return run(
        mid,
        21,
        dict(
            ids=(ids, SMEM),
            bufs=(bufs, ANY),
            prm=(prm, LATE),
            dx3=(dx3, LATE),
            x2=(x2, LATE),
            gated=(gated, LATE),
            deep=(deep, LATE),
            x1=(x1, LATE),
            qkv=(qkv, LATE),
            ls=(ls, LATE),
            mixed=(mixed, LATE),
        ),
        dict(
            dx1=(ROWS, F32, LATE),
            small=((SMALL, 512), F32, LATE),
            keep=((16, LATE_ROWS, 512), BF, ANY),
            send=((16, LATE_ROWS, 512), BF, ANY),
        ),
        dict(
            wa=WA,
            wc=WC,
            ga=WA,
            gc=WC,
            dx2=(ROWS, F32),
            n=(ROWS, BF),
            d=(ROWS, BF),
            dm=(ROWS, BF),
            act=((512, 1536), BF),
            dh=((512, 1024), BF),
            glu=(ROWS, F32),
            back=PADDED,
            dq=((128, 512), F32),
            kt=((256, 512), BF),
        ),
        room=52,
    )


def kernel_early(layer, ids, bufs, row, prm, dx1, x0, hid, stem):
    def early(k):
        for operand in (k.prm, k.dx1, k.x0):
            operand.go()
        start_load(k.ids, k.bufs, row, FEED // 2, k.wf, k.sems.at[1])
        k.hid.go()
        if stem is not None:
            k.pre.go()
            k.frames.go()
        prm = k.prm.get().at[layer]
        small = k.small.held
        small[...] = jnp.zeros((SMALL, 512), F32)
        wait_load(k.wf, k.sems.at[1])
        ig = k.ig.held
        feed_bwd(k.dx1.get(), k.x0.get(), k.hid.get(), k.wf, gain_of(prm, 0), k.ig, k.gf, small, TAPS, k)
        k.small.go()
        if stem is not None:
            pre, frames = k.pre.get(), k.frames.get()

            def rows(rs, start):
                d = (ig[rs, :] * row_mask(k.ids[4], start, RB, 512)).astype(BF)
                k.d[rs, :] = d
                p = pre[rs, :]
                sg = sigmoid(p)
                k.n[rs, 0:256] = (p * sg).astype(BF)
                k.n[rs, 256:512] = (dotr(d, k.wout[...]) * (sg * (1.0 + p * (1.0 - sg)))).astype(BF)

            row_loop(rows)
            k.gs[:, 0:8, :] = dotl(k.n[:, 256:512], frames[:, 0:512]).reshape(32, 8, 512)
            k.gs[:, 8:16, 0:128] = dotl(k.n[:, 256:512], frames[:, 512:640]).reshape(32, 8, 128)
            k.gs[:, 8:16, 128:512] = jnp.zeros((32, 8, 384), F32)
            k.gs[:, 16:24, :] = dotl(k.n[:, 0:256], k.d[...]).reshape(32, 8, 512)
            first, second = small[...], jnp.zeros((SMALL, 512), F32)
            for part in k.smalls[:2]:
                first = first + part[...]
            for part in k.smalls[2:]:
                second = second + part[...]
            for number, total in enumerate((first, second)):
                for z in range(4):
                    lanes = slice(128 * z, 128 * z + 128)
                    block = jnp.concatenate([total[0:8, lanes], total[8:16, lanes], jnp.zeros((8, 256), F32)], axis=1)
                    for q in range(4):
                        k.gs[number * 16 + z * 4 + q, 24:32, :] = block
            k.gsb[...] = k.gs[...].astype(BF)
            start_store(k.ids, k.gsb, k.keep, k.send, FEED // 2, FLAT, k.sems.at[4], flat=True)
            wait_store(k.gsb, k.sems.at[4])
        wait_store(k.gf, k.sems.at[3])

    rows = FEED // 2 + (0 if stem is None else FLAT)
    ins = dict(
        ids=(ids, SMEM),
        bufs=(bufs, ANY),
        prm=(prm, LATE),
        dx1=(dx1, LATE),
        x0=(x0, LATE),
        hid=(hid, LATE),
    )
    scratch = dict(FEED_SCRATCH)
    if stem is not None:
        pre, wout, frames, smalls = stem
        ins |= dict(pre=(pre, LATE), wout=(wout, VMEM), frames=(frames, LATE), smalls=(smalls, VMEM))
        scratch |= dict(gs=((32, FLAT, 512), F32), gsb=WH)
    return run(
        early,
        13 if stem is not None else 10,
        ins,
        dict(
            ig=(ROWS, F32, LATE),
            small=((SMALL, 512), F32, LATE),
            keep=((16, rows, 512), BF, ANY),
            send=((16, rows, 512), BF, ANY),
        ),
        scratch,
        room=55 if stem is not None else 52,
    )


def kernel_outputs(ids, head_bufs, sent_first, sent_second, other, allowed, lengths):
    def outputs(k):
        start_load(k.ids, k.hbufs, FEED // 2, FLAT, k.wh, k.sems.at[0], flat=True)
        for sec in range(2):

            @pl.when(k.ids[5] == sec)
            def _():
                pltpu.make_async_copy(k.second if sec else k.first, k.sent.at[sec], k.sems.at[1]).start()
                pltpu.make_async_copy(k.other, k.sent.at[1 - sec], k.sems.at[1]).start()

        wait_load(k.sent, k.sems.at[1])
        wait_load(k.wh, k.sems.at[0])
        for batch in range(2):
            permit = k.allowed[batch : batch + 1, :] > 0
            sent = k.sent[batch]
            logits, logsum = head_rows(sent, k.wh[...].reshape(1024, 512), permit)
            ok = row_mask(k.lengths[batch], 0, 512, 1024)
            k.logp.held[batch] = jnp.where(permit, logits - logsum, 0.0) * ok
            k.acts.held[batch] = sent.astype(F32)

    return run(
        outputs,
        9,
        dict(
            ids=(ids, SMEM),
            lengths=(lengths, SMEM),
            hbufs=(head_bufs, ANY),
            first=(sent_first, ANY),
            second=(sent_second, ANY),
            other=(other, ANY),
            allowed=(allowed, VMEM),
        ),
        dict(logp=((2, 512, 1024), F32, LATE), acts=((2, 512, 512), F32, LATE)),
        dict(wh=WH, sent=((2, 512, 512), BF)),
    )


def kernel_grads(ids, first, second, other):
    def grads(k):
        sec = k.ids[5]
        k.out.held[1 - sec] = k.other[...].astype(F32)

        @pl.when(sec == 0)
        def _():
            k.out.held[0] = k.first[...]

        @pl.when(sec != 0)
        def _():
            k.out.held[1] = k.second[...]

    return run(
        grads,
        3,
        dict(ids=(ids, SMEM), first=(first, VMEM), second=(second, VMEM), other=(other, VMEM)),
        dict(out=((2, 512, 512), F32, LATE)),
        dict(),
    ).out


def pack_feed(w_in, w_out):
    return jnp.concatenate([w_in.reshape(32, 4, 512).transpose(1, 0, 2).reshape(128, 512), w_out])


def pack_attn(w_in, w_out):
    return jnp.concatenate([w_in.reshape(32, 3, 512).transpose(1, 0, 2).reshape(96, 512), w_out])


def pack_conv(w_in, w_out):
    return jnp.concatenate([w_in.reshape(32, 2, 512).transpose(1, 0, 2).reshape(64, 512), w_out])


def unpack_in(rows, blocks):
    return rows[: 32 * blocks].reshape(blocks, 32, 512).transpose(1, 0, 2).reshape(32, 512 * blocks)


def pack_stem(stem_in, stem_out, depth, gains, quarter):
    turned = stem_in.T
    small = jnp.concatenate([depth, gains, jnp.zeros((1, 32), depth.dtype)])
    spread = lax.dynamic_update_slice(jnp.zeros((16, 128), depth.dtype), small, (0, 32 * quarter))
    return jnp.concatenate(
        [
            turned[:, :512],
            jnp.pad(turned[:, 512:], ((0, 0), (0, 384))),
            stem_out,
            jnp.concatenate([spread[:8], spread[8:], jnp.zeros((8, 256), depth.dtype)], axis=1),
        ]
    )


def unpack_stem(rows, quarter):
    turned = jnp.concatenate([rows[0:8], rows[8:16, :128]], axis=1)
    spread = jnp.concatenate([rows[24:32, 0:128], rows[24:32, 128:256]])
    small = lax.dynamic_slice(spread, (0, 32 * quarter), (16, 32))
    return turned.T, rows[16:24], small[:TAPS], small[TAPS : TAPS + 6]


def permutation(target):
    pairs = []
    for x in range(2):
        for d in range(16):
            tx, tz, ty, tc = target(x, d // 4, (d // 2) % 2, d % 2)
            pairs.append((x * 16 + d, tx * 16 + tz * 4 + ty * 2 + tc))
    return pairs


def across(value, target):
    return lax.ppermute(value, BOTH, permutation(target))


def over_x(value):
    return across(value, lambda x, z, y, c: (1 - x, z, y, c))


def over_core(value):
    return across(value, lambda x, z, y, c: (x, z, y, 1 - c))


def over_z(value, k):
    return across(value, lambda x, z, y, c: (x, z ^ k, y, c))


def over_a(value):
    return across(value, lambda x, z, y, c: (1 - x, z, y, c) if c == 0 else (x, z, 1 - y, c))


def over_b(value):
    return across(value, lambda x, z, y, c: (1 - x, z, y, c) if c == 1 else (x, z, 1 - y, c))


def fence(*values):
    return lax.optimization_barrier(values)


def z_parts(own):
    return [own] + [over_z(own, k) for k in (1, 2, 3)]


def ab_parts(quad):
    return over_a(quad), over_b(quad)


def core_parts(quad, ra, rb, rab):
    return [quad, rb, ra, rab] + [over_core(v) for v in (quad, rb, ra, rab)]


def add(*values):
    total = values[0].astype(F32)
    for value in values[1:]:
        total = total + value.astype(F32)
    return total


def halves(kept, came):
    cut = kept.shape[0] // 2
    return add(kept[:cut], came[:cut]).astype(BF), add(kept[cut:], came[cut:]).astype(BF)


def quarters(kept, came):
    return [add(kept[k], came[k]).astype(BF) for k in range(4)]


def z_sum(parts):
    return add(parts[0], *[over_z(parts[k], k) for k in (1, 2, 3)])


def pick(first, own, other):
    return jnp.where(first, own, other), jnp.where(first, other, own)


def on_device(fast, *args):
    (spectra, lengths, languages, token_masks, cotangent) = args[:5]
    masters = args[5:]
    sec = lax.axis_index("section")
    dp = lax.axis_index("dp")
    first = sec == 0
    low = [m.astype(BF) for m in masters]
    swap = lambda v: lax.ppermute(v, "section", [(0, 1), (1, 0)])
    cots = cotangent[0, :, 0]
    cot_send = lax.dynamic_index_in_dim(cots, 1 - sec, 0, keepdims=False)
    place = [sec, dp // 4, (dp // 2) % 2, dp % 2] if fast else [sec * 0] * 4
    ids = jnp.stack(place + [lengths[sec, 0], sec]).astype(jnp.int32)
    frames = lax.dynamic_index_in_dim(spectra, sec, 0, keepdims=False).reshape(512, -1)
    allowed_both = jnp.concatenate(
        [lax.dynamic_slice_in_dim(token_masks, languages[m, 0], 1, 0) for m in range(2)]
    ).astype(F32)
    allowed = lax.dynamic_slice_in_dim(allowed_both, sec, 1, 0)
    if fast:
        chunks = [None] * 4
        own_first, rest = own_pieces(low, sec, dp, first)
        early_cot, late_cot = cot_send[:320], cot_send[320:]
        own_first, rest, early_cot = fence(own_first, rest, early_cot)
        z0 = z_parts(own_first)
        own = own_rest(rest, low, sec, first)
        early_cot = swap(early_cot)
        *z0, own[0], early_cot = fence(*z0, own[0], early_cot)
        quad0 = jnp.stack(z0)
        a0, b0 = ab_parts(quad0)
        z1 = z_parts(own[0])
        quad0, a0, b0, own[2], *z1 = fence(quad0, a0, b0, own[2], *z1)
        pair3 = jnp.concatenate([own[2], over_a(own[2])])
        ab0 = over_b(a0)
        core0 = [over_core(v) for v in (quad0, b0, a0)]
        quad1 = jnp.stack(z1)
        quad1, ab0, frames, pair3, *core0 = fence(quad1, ab0, frames, pair3, *core0)
        a1, b1 = ab_parts(quad1)
        chunks[0] = [quad0, b0, a0, ab0] + core0 + [over_core(ab0)]
        *chunks[0], own[1] = fence(*chunks[0], own[1])
        z2 = z_parts(own[1])
    else:
        chunks = gather_plain(low)
        early_cot, late_cot = swap(cot_send[:320]), swap(cot_send[320:])
    ka = kernel_stem_feed(ids, chunks[0], frames)
    prm = ka.prm
    if fast:
        ka.x1, quad1, a1, b1, pair3, *z2 = fence(ka.x1, quad1, a1, b1, pair3, *z2)
        mid3 = over_z(pair3, 2)
        ab1 = over_b(a1)
        core1 = [over_core(v) for v in (quad1, b1, a1)]
        quad2 = jnp.stack(z2)
        ab1, quad2, pair3, mid3, *core1 = fence(ab1, quad2, pair3, mid3, *core1)
        a2, b2 = ab_parts(quad2)
        chunks[1] = [quad1, b1, a1, ab1] + core1 + [over_core(ab1)]
        *chunks[1], pair3 = fence(*chunks[1], pair3)
        far3, near3 = over_z(pair3, 3), over_z(pair3, 1)
    kb = kernel_rest_first(ids, chunks[1], prm, ka.x1)
    if fast:
        kb.sent, quad2, a2, b2, near3, far3, pair3 = fence(kb.sent, quad2, a2, b2, near3, far3, pair3)
        ab2 = over_b(a2)
        oct3 = jnp.stack([pair3, near3, mid3, far3])
        core2 = [over_core(v) for v in (quad2, b2, a2)]
        ab2, oct3, late_cot, *core2 = fence(ab2, oct3, late_cot, *core2)
        b3 = over_b(oct3)
        late_cot = swap(late_cot)
        chunks[2] = [quad2, b2, a2, ab2] + core2 + [over_core(ab2)]
        chunks[2] = list(fence(*chunks[2]))
        core3 = over_core(oct3)
    kc = kernel_first_second(ids, chunks[2], prm, kb.sent)
    if fast:
        kc.x3, oct3, b3, core3, late_cot = fence(kc.x3, oct3, b3, core3, late_cot)
        chunks[3] = [oct3, b3, core3, over_core(b3)]
    cot_other = [early_cot, late_cot]
    kd = kernel_turn(ids, chunks[3], prm, kc.x3, cots, cot_other, allowed)
    other_sent = swap(jnp.where(first, kd.sent, kb.sent))
    came = [None] * 6
    near, far, parts = [None] * 6, [None] * 6, [None] * 6

    def begin(n, kernel):
        near[n], far[n] = halves(kernel.keep, over_core(kernel.send))
        came[n] = over_a(far[n])

    def go_on(n):
        near[n], far[n] = halves(near[n], came[n])
        came[n] = over_b(far[n])

    def gather_parts(n):
        parts[n] = quarters(near[n], came[n])

    if fast:
        begin(0, kd)
    ke = kernel_mid(1, ids, chunks[2], FEED // 2, prm, kd.dx3, kc.x2, kc.gated, kc.deep, kc.x1, kc.qkv, kc.ls, kc.mixed)
    if fast:
        came[0], other_sent, ke.send, ke.dx1 = fence(came[0], other_sent, ke.send, ke.dx1)
        go_on(0)
        begin(1, ke)
    kf = kernel_early(1, ids, chunks[2], 0, prm, ke.dx1, kb.sent, kc.hid, None)
    if fast:
        came[0], came[1], kf.send, kf.ig = fence(came[0], came[1], kf.send, kf.ig)
        gather_parts(0)
        go_on(1)
        begin(2, kf)
    kg = kernel_late(
        ids, chunks[1], chunks[3], prm, kb.x4, kb.sent, cots, cot_other, allowed, kf.ig, kb.x3, kb.hid, kd.ghead
    )
    if fast:
        came[1], came[2], kg.send, kg.dx3 = fence(came[1], came[2], kg.send, kg.dx3)
        gather_parts(1)
        go_on(2)
        begin(3, kg)
        sums_a = z_sum([jnp.concatenate([p, q]) for p, q in zip(parts[0], parts[1])])
    kh = kernel_mid(0, ids, chunks[1], 0, prm, kg.dx3, kb.x2, kb.gated, kb.deep, ka.x1, kb.qkv, kb.ls, kb.mixed)
    if fast:
        came[2], came[3], sums_a, kh.send, kh.dx1 = fence(came[2], came[3], sums_a, kh.send, kh.dx1)
        gather_parts(2)
        go_on(3)
        begin(4, kh)
        sum_2 = z_sum(parts[2])
    stem = (ka.pre, ka.wout, frames, [kg.small, kh.small, kd.small, ke.small, kf.small])
    ki = kernel_early(0, ids, chunks[0], FLAT, prm, kh.dx1, ka.x0, ka.hid, stem)
    if fast:
        came[3], came[4], sum_2, ki.send, ki.ig, other_sent = fence(came[3], came[4], sum_2, ki.send, ki.ig, other_sent)
        gather_parts(3)
        go_on(4)
        begin(5, ki)
        sum_3 = z_sum(parts[3])
    ko = kernel_outputs(ids, chunks[3], kb.sent, kd.sent, other_sent, allowed_both, lengths[:, 0])
    if fast:
        came[4], came[5], sum_3, ki.ig, ko.acts, ko.logp = fence(came[4], came[5], sum_3, ki.ig, ko.acts, ko.logp)
        gather_parts(4)
        go_on(5)
        sum_4 = z_sum(parts[4])
        late = join(sum_3[: FEED // 2], sums_a[: FEED // 2], first).reshape(FEED, 512)
        head = sum_3[FEED // 2 :].T
        came[5], sum_4, ki.ig, late, head = fence(came[5], sum_4, ki.ig, late, head)
        gather_parts(5)
        sum_5 = z_sum(parts[5])
        late_in, late_out = unpack_in(late, 4), late[128:]
    other_grad = swap(jnp.where(first, kf.ig, ki.ig).astype(BF))
    if fast:
        sum_5, other_grad, late_in, late_out = fence(sum_5, other_grad, late_in, late_out)
        shards = all_shards(late_in, late_out, head, sums_a, sum_2, sum_4, sum_5, dp, first)
    else:
        shards = reduce_plain([(k.keep, k.send) for k in (kd, ke, kf, kg, kh, ki)])
    input_grads = kernel_grads(ids, ki.ig, kf.ig, other_grad)[None, :, None]
    activations = ko.acts[None, :, None]
    log_probs = ko.logp[None, :, None]
    return (activations, log_probs, input_grads, *shards)


def own_half(both, sec, first):
    mine = lax.dynamic_index_in_dim(both, sec, 0, keepdims=False)
    theirs = over_x(lax.dynamic_index_in_dim(both, 1 - sec, 0, keepdims=False))
    return pick(first, mine, theirs)


def own_pieces(low, sec, dp, first):
    feed_in, feed_out = low[:2]
    stem = pack_stem(low[8], low[9], low[5][0], low[7][0], dp % 4)
    feed_first, feed_second = own_half(pack_feed(feed_in[0, 0], feed_out[0, 0]).reshape(2, FEED // 2, 512), sec, first)
    return jnp.concatenate([stem, feed_first]), feed_second


def own_rest(feed_second, low, sec, first):
    feed_in, feed_out, attend_in, attend_out, conv_in, _, conv_out = low[:7]
    feed = pack_feed(feed_in[0, 1], feed_out[0, 1]).reshape(2, FEED // 2, 512)
    attn = pack_attn(attend_in[0], attend_out[0]).reshape(2, ATTN // 2, 512)
    conv = pack_conv(conv_in[0], conv_out[0]).reshape(2, CONV // 2, 512)
    rest_first, rest_second = own_half(jnp.concatenate([attn, conv, feed], axis=1), sec, first)
    return [
        rest_first,
        jnp.concatenate([feed_second, rest_second[:LATE_ROWS]]),
        jnp.concatenate([rest_second[LATE_ROWS:], low[10].T]),
    ]


def join(of_first, of_second, first):
    own = jnp.where(first, of_first, of_second)
    other = over_x(jnp.where(first, of_second, of_first).astype(BF)).astype(F32)
    return jnp.stack(pick(first, own, other))


def all_shards(late_in, late_out, head, sums_a, sum_2, sum_4, sum_5, dp, first):
    half = FEED // 2
    both = join(jnp.concatenate([sum_4, sum_5[:half]]), jnp.concatenate([sums_a[half:], sum_2]), first)
    attn = both[:, : ATTN // 2].reshape(ATTN, 512)
    conv = both[:, ATTN // 2 : LATE_ROWS].reshape(CONV, 512)
    early = both[:, LATE_ROWS:].reshape(FEED, 512)
    g_stem_in, g_stem_out, g_depth, g_gains = unpack_stem(sum_5[half:], dp % 4)
    return (
        jnp.stack([unpack_in(early, 4), late_in])[None],
        jnp.stack([early[128:], late_out])[None],
        unpack_in(attn, 3)[None],
        attn[96:][None],
        unpack_in(conv, 2)[None],
        g_depth[None],
        conv[64:][None],
        g_gains[None],
        g_stem_in,
        g_stem_out,
        head,
    )


def spread_order():
    order = []
    for cr, a, b, zk in pieces():
        px, py = (b, a) if cr else (a, b)
        order.append(px * 16 + zk * 4 + py * 2 + cr)
    return order


def gather_plain(low):
    axes = (2, 2, 1, 1, 1, 2, 1, 2)
    whole = []
    for weight, axis in zip(low[:8], axes):
        axis = 2 if weight.ndim == 4 else axis
        part = lax.all_gather(weight[0], "dp", axis=axis - 1, tiled=True)
        whole.append(lax.all_gather(part, "section", axis=0))
    feed_in, feed_out, attend_in, attend_out, conv_in, depth, conv_out, gains = whole
    stem_in = lax.all_gather(low[8], BOTH, axis=1, tiled=True)
    stem_out = lax.all_gather(low[9], BOTH, axis=0, tiled=True)
    head = lax.all_gather(low[10], BOTH, axis=1, tiled=True)
    order = spread_order()

    def layer(l):
        rows = lambda w, n: w.reshape(16, n, w.shape[-1])
        feeds = [jax.vmap(pack_feed)(rows(feed_in[l, j], 32), rows(feed_out[l, j], 128)) for j in range(2)]
        attn = jax.vmap(pack_attn)(rows(attend_in[l], 32), rows(attend_out[l], 32))
        conv = jax.vmap(pack_conv)(rows(conv_in[l], 32), rows(conv_out[l], 32))
        cut = lambda w: w.reshape(16, 2, w.shape[1] // 2, 512).transpose(1, 0, 2, 3).reshape(32, w.shape[1] // 2, 512)
        return [cut(w) for w in (feeds[0], attn, conv, feeds[1])]

    one, two = layer(0), layer(1)
    columns = lambda w, n: w.reshape(*w.shape[:-1], n, w.shape[-1] // n)
    small = lambda w: jnp.moveaxis(columns(w, 16), 2, 1).reshape(32, w.shape[1], 32)
    stem = jax.vmap(pack_stem)(
        jnp.moveaxis(columns(stem_in, 32), 1, 0),
        stem_out.reshape(32, 8, 512),
        small(depth),
        small(gains),
        jnp.arange(32) % 4,
    )
    head = head.T.reshape(32, 32, 512)
    chunks = ([stem, one[0]], one[1:], [two[0], two[1], two[2]], [two[3], head])
    placed = []
    for parts in chunks:
        joined = jnp.concatenate(parts, axis=1)
        placed.append([jnp.stack([joined[p] for p in order[4 * i : 4 * i + 4]]) for i in range(8)])
    return placed


def reduce_plain(grads):
    order = spread_order()
    place = [order.index(p) for p in range(32)]
    chunks = []
    for keep, send in grads:
        both = jnp.concatenate([keep, send])
        chunks.append(jnp.stack([both[q] for q in place]).astype(F32))
    half = FEED // 2
    whole = []
    for late, mid, early in (chunks[3:], chunks[:3]):
        glue = lambda part, begin, rows: (
            part[:, begin : begin + rows].reshape(2, 16, rows, 512).transpose(1, 0, 2, 3).reshape(16, 2 * rows, 512)
        )
        feeds = [glue(early, 0, half), glue(late, 0, half)]
        attn, conv = glue(mid, 0, ATTN // 2), glue(mid, ATTN // 2, CONV // 2)
        spread = lambda w, n: jax.vmap(lambda rows: unpack_in(rows, n))(w).reshape(512, 512 * n)
        whole.append(
            (
                jnp.stack([spread(f, 4) for f in feeds]),
                jnp.stack([f[:, 128:].reshape(FF, 512) for f in feeds]),
                spread(attn, 3),
                attn[:, 96:].reshape(512, 512),
                spread(conv, 2),
                conv[:, 64:].reshape(512, 512),
            )
        )
    head = chunks[3][:, half:].reshape(1024, 512).T
    g_stem_in, g_stem_out, g_depth, g_gains = jax.vmap(unpack_stem)(chunks[5][:, half:], jnp.arange(32) % 4)
    g_stem_in = jnp.moveaxis(g_stem_in, 0, 1).reshape(640, 256)
    g_stem_out = g_stem_out.reshape(256, 512)
    lanes = lambda w: jnp.moveaxis(w.reshape(2, 16, w.shape[1], 32), 1, 2).reshape(2, w.shape[1], 512)
    g_depth, g_gains = lanes(g_depth), lanes(g_gains)
    stacked = [jnp.stack([whole[0][i], whole[1][i]]) for i in range(6)]

    def shard(value, axis):
        value = lax.psum_scatter(value, "section", scatter_dimension=0, tiled=True)
        return lax.psum_scatter(value, "dp", scatter_dimension=axis, tiled=True)

    return (
        shard(stacked[0], 2),
        shard(stacked[1], 2),
        shard(stacked[2], 1),
        shard(stacked[3], 1),
        shard(stacked[4], 1),
        shard(g_depth, 2),
        shard(stacked[5], 1),
        shard(g_gains, 2),
        lax.psum_scatter(g_stem_in, BOTH, scatter_dimension=1, tiled=True),
        lax.psum_scatter(g_stem_out, BOTH, scatter_dimension=0, tiled=True),
        lax.psum_scatter(head, BOTH, scatter_dimension=1, tiled=True),
    )


def solution(mesh):
    fast = dict(mesh.shape) == {"section": 2, "dp": 16}

    def body(*args):
        return on_device(fast, *args)

    layer_specs = (
        P("section", None, "dp", None),
        P("section", None, "dp", None),
        P("section", "dp", None),
        P("section", "dp", None),
        P("section", "dp", None),
        P("section", None, "dp"),
        P("section", "dp", None),
        P("section", None, "dp"),
        P(None, BOTH),
        P(BOTH, None),
        P(None, BOTH),
    )
    rows = P("section", None, "dp", None, None)
    return jax.shard_map(
        body,
        mesh=mesh,
        in_specs=(P(None, "dp", None, None), P(None, "dp"), P(None, "dp"), P(), rows) + layer_specs,
        out_specs=(rows, rows, rows) + layer_specs,
        check_vma=False,
    )
```
